32 devices in a mesh: dp: 8 (over z, y), mp: 4 (over x, core).
Axes of the slice: x: 2, y: 2, z: 4, core: 2. Of those that a mesh axis runs over, the one named last changes fastest.
Arguments:
- block_input: bfloat16 [96, 256, 768], P('dp'), may hold values from -6 to 6
- cotangent: bfloat16 [96, 256, 768], P('dp')
- crop_boxes: int32 [96, 4], P('dp'), may hold values from 0 to 16, as said below
- front_weights: float32 [7, 768, 768], P(None, 'dp', 'mp'), may hold values from -0.21875 to 0.21875
- back_weights: float32 [5, 768, 768], P(None, 'mp', 'dp')
- split_biases: float32 [6, 768], P(None, ('mp', 'dp')), may hold values from -4 to 4
- norm_params: float32 [6, 768], P(None, 'dp')
- pos_table: float32 [256, 768], P('dp'), may hold values from -6 to 6
- front_first: float32 [7, 768, 768], P(None, 'dp', 'mp'), may hold values from -5.722046e-06 to 5.722046e-06
- back_weight_first_moment: float32 [5, 768, 768], P(None, 'mp', 'dp'), may hold values from -5.722046e-06 to 5.722046e-06
- split_first: float32 [6, 768], P(None, ('mp', 'dp')), may hold values from -5.722046e-06 to 5.722046e-06
- norm_first: float32 [6, 768], P(None, 'dp'), may hold values from -5.722046e-06 to 5.722046e-06
- table_first: float32 [256, 768], P('dp'), may hold values from -7.1525574e-07 to 7.1525574e-07
- front_second: float32 [7, 768, 768], P(None, 'dp', 'mp'), may hold values from 7.436057e-13 to 2.9744228e-12
- back_second: float32 [5, 768, 768], P(None, 'mp', 'dp'), may hold values from 7.436057e-13 to 2.9744228e-12
- split_second: float32 [6, 768], P(None, ('mp', 'dp')), may hold values from 7.436057e-13 to 2.9744228e-12
- norm_second: float32 [6, 768], P(None, 'dp'), may hold values from 7.436057e-13 to 2.9744228e-12
- table_second: float32 [256, 768], P('dp'), may hold values from 1.1612473e-14 to 4.644989e-14
Outputs:
- block_output: bfloat16 [96, 256, 768], P('dp')
- input_grad: bfloat16 [96, 256, 768], P('dp')
- clip_norm: float32 [], replicated
- new_front: float32 [7, 768, 768], P(None, 'dp', 'mp')
- new_back: float32 [5, 768, 768], P(None, 'mp', 'dp')
- new_split: float32 [6, 768], P(None, ('mp', 'dp'))
- new_norm: float32 [6, 768], P(None, 'dp')
- new_table: float32 [256, 768], P('dp')
- front_first_new: float32 [7, 768, 768], P(None, 'dp', 'mp')
- back_first_new: float32 [5, 768, 768], P(None, 'mp', 'dp')
- split_first_new: float32 [6, 768], P(None, ('mp', 'dp'))
- norm_first_new: float32 [6, 768], P(None, 'dp')
- table_first_new: float32 [256, 768], P('dp')
- front_second_new: float32 [7, 768, 768], P(None, 'dp', 'mp')
- back_second_new: float32 [5, 768, 768], P(None, 'mp', 'dp')
- split_second_new: float32 [6, 768], P(None, ('mp', 'dp'))
- norm_second_new: float32 [6, 768], P(None, 'dp')
- table_second_new: float32 [256, 768], P('dp')
- norm_grad: float32 [6, 768], P(None, 'dp')
The draws below stay inside these ranges and needn't reach their ends.
Inputs may be any that keep to these rules, and one draw needn't show every extreme that they name: `crop_boxes`: each row holds one grid's crop height and breadth, each 12 to 16, then its top row and left column, each at most 16 minus the height or breadth; the first grid is the whole 16 x 16 table.
All inputs are finite; a program needn't handle non-finite values.
Results may differ from the reference program's by a relative error of at most 0.019.
Values may be sent and summed in bfloat16 or wider, within the bound.
No kernel may reach another device: no remote copies, remote signals or barrier semaphores. Data moves between devices by JAX's collectives and lax.ppermute only.
A program may use at most 256 MiB of HBM per device.

```python
import math
import jax
import jax.numpy as jnp
from jax import lax

D = 768
HEADS = 16
FF = 3072
SIDE = 16
CROP_MIN = 12
CELLS = 256
GRIDS = 96
STEP = 5
N_MP = 4


def draw_cotangent(key, part):
    key = jax.random.fold_in(key, 23)
    base = jax.random.normal(key, (GRIDS, CELLS, D), jnp.float32)
    top_end = 3.0
    rising = 1.0 + (top_end - 1.0) * jnp.arange(D, dtype=jnp.float32) / (D - 1)
    return (base * rising[None, None, :]).astype(jnp.bfloat16)


def draw_crop_boxes(key, part):
    key = jax.random.fold_in(key, 11)
    streams = jax.random.split(key, 4)
    height = jax.random.randint(streams[0], (GRIDS,), CROP_MIN, SIDE + 1)
    breadth = jax.random.randint(streams[1], (GRIDS,), CROP_MIN, SIDE + 1)
    is_first = jnp.arange(GRIDS) == 0
    height = jnp.where(is_first, SIDE, height)
    breadth = jnp.where(is_first, SIDE, breadth)
    top_row = jax.random.randint(streams[2], (GRIDS,), 0, 1 << 20) % (SIDE - height + 1)
    left_col = jax.random.randint(streams[3], (GRIDS,), 0, 1 << 20) % (SIDE - breadth + 1)
    return jnp.stack([height, breadth, top_row, left_col], axis=1).astype(jnp.int32)


def draw_back_weights(key, part):
    key = jax.random.fold_in(key, 5)
    blocks = 1 + FF // D
    base = jax.random.normal(key, (blocks, D, D), jnp.float32)
    top_end = 3.0
    rising = 1.0 + (top_end - 1.0) * jnp.arange(D, dtype=jnp.float32) / (D - 1)
    block_scale = jnp.where(jnp.arange(blocks) == 0, 5.0 * D ** (-0.5), 0.7 * FF ** (-0.5))
    return base * rising[None, :, None] * block_scale[:, None, None]


def draw_norm_params(key, part):
    key = jax.random.fold_in(key, 7)
    noise = jax.random.normal(key, (6, D), jnp.float32)
    low_end = 0.5
    rising = low_end + jnp.arange(D, dtype=jnp.float32) / (D - 1)
    gains = rising[None, :] * (1.0 + 0.1 * noise)
    shifts = 0.3 * noise
    is_gain = (jnp.arange(6) % 3 == 0)[:, None]
    return jnp.where(is_gain, gains, shifts)


def shard_levels(rng, extent, shards, smallest, largest):
    factor_of, own = 1.0, jax.random.fold_in(rng, 6)
    for axis_at, parts in shards:
        draws = jnp.exp(jax.random.uniform(jax.random.fold_in(own, axis_at), (parts,), jnp.float32, smallest / len(shards), largest / len(shards)))
        factor_of = factor_of * jnp.repeat(draws, extent[axis_at] // parts).reshape([-1 if axis == axis_at else 1 for axis in range(len(extent))])
    return factor_of


def gaussian(key, shape, deviation, most, shards=(), held_as=jnp.bfloat16):
    gain = shard_levels(key, shape, shards, -0.22, 0.18) if shards else 1.0
    entries = jax.random.normal(key, shape, jnp.float32) * deviation * gain
    return jnp.minimum(jnp.maximum(entries, -most), most).astype(held_as)


def setup_inputs(seed: int = 0) -> dict:
    seeds = jax.random.split(jax.random.key(seed), 19)
    return {
        "block_input": gaussian(seeds[0], (GRIDS, CELLS, D), 1.0, 6.0, ((0, 8),)),
        "cotangent": draw_cotangent(jax.random.fold_in(seeds[18], 71), 0),
        "crop_boxes": draw_crop_boxes(jax.random.fold_in(seeds[18], 71), 0),
        "front_weights": gaussian(seeds[3], (3 + FF // D, D, D), D ** -0.5, 0.21875, ((1, 8), (2, 4)), jnp.float32),
        "back_weights": draw_back_weights(jax.random.fold_in(seeds[18], 71), 0),
        "split_biases": gaussian(seeds[5], (2 + FF // D, D), 0.3, 4.0, ((1, 32),), jnp.float32),
        "norm_params": draw_norm_params(jax.random.fold_in(seeds[18], 71), 0),
        "pos_table": gaussian(seeds[7], (CELLS, D), 0.5, 6.0, ((0, 8),), jnp.float32),
        "front_first": gaussian(seeds[8], (3 + FF // D, D, D), (0.00032 * D ** -1), 5.7220458984375e-06, ((1, 8), (2, 4)), jnp.float32),
        "back_weight_first_moment": gaussian(seeds[9], (1 + FF // D, D, D), (0.00032 * D ** -1), 5.7220458984375e-06, ((1, 4), (2, 8)), jnp.float32),
        "split_first": gaussian(seeds[10], (2 + FF // D, D), (0.00032 * D ** -1), 5.7220458984375e-06, ((1, 32),), jnp.float32),
        "norm_first": gaussian(seeds[11], (6, D), (0.00032 * D ** -1), 5.7220458984375e-06, ((1, 8),), jnp.float32),
        "table_first": gaussian(seeds[12], (CELLS, D), (0.00004 * D ** -1), 7.152557373046875e-07, ((0, 8),), jnp.float32),
        "front_second": jnp.clip(jnp.exp(math.log(2.9744227914019206e-12) - 1.3862944 * jax.random.uniform(seeds[13], (3 + FF // D, D, D), jnp.float32) ** shard_levels(seeds[13], (3 + FF // D, D, D), ((1, 8), (2, 4)), -0.2, 0.2)), 7.436056978504801e-13, 2.9744227914019206e-12),
        "back_second": jnp.clip(jnp.exp(math.log(2.9744227914019206e-12) - 1.3862944 * jax.random.uniform(seeds[14], (1 + FF // D, D, D), jnp.float32) ** shard_levels(seeds[14], (1 + FF // D, D, D), ((1, 4), (2, 8)), -0.2, 0.2)), 7.436056978504801e-13, 2.9744227914019206e-12),
        "split_second": jnp.clip(jnp.exp(math.log(2.9744227914019206e-12) - 1.3862944 * jax.random.uniform(seeds[15], (2 + FF // D, D), jnp.float32) ** shard_levels(seeds[15], (2 + FF // D, D), ((1, 32),), -0.2, 0.2)), 7.436056978504801e-13, 2.9744227914019206e-12),
        "norm_second": jnp.clip(jnp.exp(math.log(2.9744227914019206e-12) - 1.3862944 * jax.random.uniform(seeds[16], (6, D), jnp.float32) ** shard_levels(seeds[16], (6, D), ((1, 8),), -0.2, 0.2)), 7.436056978504801e-13, 2.9744227914019206e-12),
        "table_second": jnp.clip(jnp.exp(math.log(4.6449890917128756e-14) - 1.3862944 * jax.random.uniform(seeds[17], (CELLS, D), jnp.float32) ** shard_levels(seeds[17], (CELLS, D), ((0, 8),), -0.2, 0.2)), 1.1612472729282189e-14, 4.6449890917128756e-14),
    }


@jax.custom_vjp
def low(v):
    return lax.optimization_barrier(v.astype(jnp.bfloat16)).astype(jnp.float32)

@jax.custom_vjp
def low_back(v):
    return v

def low_keep(v):
    return (low(v), None)

def low_pass(kept, grad):
    return (grad,)

def back_keep(v):
    return (v, None)

def back_low(kept, grad):
    return (low(grad),)
low.defvjp(low_keep, low_pass)
low_back.defvjp(back_keep, back_low)
NORM_EPS = 1e-05
BETA_FIRST = 0.9
BETA_SECOND = 0.95
ADAM_EPS = 1e-08
RATE_MATRIX = 0.05
RATE_TABLE = 0.2
RATE_VECTOR = 0.5
DECAY_RATE = 0.1
CLIP_LIMIT = 0.01
MASK_FILL = -1e+30
TOP_PRECISION = lax.Precision.HIGHEST

def layer_norm(inputs, norm_gain, norm_shift):
    average = lax.optimization_barrier(jnp.mean(inputs, axis=-1, keepdims=True))
    centred = inputs - average
    spread = lax.optimization_barrier(jnp.mean(centred * centred, axis=-1, keepdims=True))
    return centred * lax.rsqrt(spread + NORM_EPS) * norm_gain + norm_shift

def position_codes(crop_boxes, cell_count, grid_side):
    height = crop_boxes[:, 0:1]
    breadth = crop_boxes[:, 1:2]
    top_row = crop_boxes[:, 2:3]
    left_col = crop_boxes[:, 3:4]
    position = jnp.arange(cell_count, dtype=jnp.int32)[None, :]
    is_valid = position < height * breadth
    target = (top_row + position // breadth) * grid_side + left_col + position % breadth
    target = jnp.where(is_valid, target, -1)
    onehot_tokens = target[:, :, None] == jnp.arange(cell_count, dtype=jnp.int32)[None, None, :]
    return (onehot_tokens, is_valid)

def exact_gelu(inputs):
    return jax.nn.gelu(inputs, approximate=False)

def layer_body(params, layer_step_input, onehot_tokens, is_valid):
    front, back, split_vectors, norm_vectors, embedding_table = params
    grid_count, cell_count, model_width = layer_step_input.shape
    local_width = model_width // N_MP
    head_size = model_width // HEADS
    heads_here = HEADS // N_MP
    token_embeddings = layer_step_input + jnp.einsum('vfu,uk->vfk', onehot_tokens, embedding_table, precision=TOP_PRECISION)
    normed_first = low(layer_norm(token_embeddings, norm_vectors[0], norm_vectors[1]))
    first_copies = low_back(jnp.broadcast_to(normed_first[None], (N_MP,) + normed_first.shape))
    front_groups = front.reshape(front.shape[0], model_width, N_MP, local_width)
    split_groups = split_vectors.reshape(split_vectors.shape[0], N_MP, local_width)
    back_groups = back.reshape(back.shape[0], N_MP, local_width, model_width)

    def project(copies, matrix):
        return jnp.einsum('ngcd,dne->ngce', copies, matrix, precision=TOP_PRECISION)
    queries = low(low_back(project(first_copies, front_groups[0]) + split_groups[0][:, None, None, :]))
    key_rows = low(low_back(project(first_copies, front_groups[1])))
    value_rows = low(low_back(project(first_copies, front_groups[2]) + split_groups[1][:, None, None, :]))
    head_shape = (N_MP, grid_count, cell_count, heads_here, head_size)
    queries = queries.reshape(head_shape)
    key_rows = key_rows.reshape(head_shape)
    value_rows = value_rows.reshape(head_shape)
    scores = low_back(jnp.einsum('ngqhs,ngkhs->nghqk', queries, key_rows, precision=TOP_PRECISION) * head_size ** (-0.5))
    scores = jnp.where(is_valid[None, :, None, None, :], scores, MASK_FILL)
    soft_low = low(jax.nn.softmax(scores, axis=-1))
    mixed = jnp.einsum('nghqk,ngkhs->ngqhs', soft_low, value_rows, precision=TOP_PRECISION)
    mixed = low(low_back(mixed.reshape(N_MP, grid_count, cell_count, local_width)))
    attention_parts = low(low_back(jnp.einsum('ngce,ned->ngcd', mixed, back_groups[0], precision=TOP_PRECISION)))
    after_attention = token_embeddings + lax.optimization_barrier(jnp.sum(attention_parts, axis=0)) + norm_vectors[2]
    normed_second = low(layer_norm(after_attention, norm_vectors[3], norm_vectors[4]))
    second_copies = low_back(jnp.broadcast_to(normed_second[None], (N_MP,) + normed_second.shape))
    up_bias = jnp.transpose(split_groups[2:], (1, 0, 2))[:, None, None, :, :]
    hidden_pre = jnp.einsum('ngcd,jdne->ngcje', second_copies, front_groups[3:], precision=TOP_PRECISION) + up_bias
    hidden_low = low(exact_gelu(low_back(hidden_pre)))
    mlp_parts = low(low_back(jnp.einsum('ngcje,jned->ngcd', hidden_low, back_groups[1:], precision=TOP_PRECISION)))
    return after_attention + lax.optimization_barrier(jnp.sum(mlp_parts, axis=0)) + norm_vectors[5]

def adam_step(weight, gradient, first, second, rate, decay):
    first_new = BETA_FIRST * first + (1.0 - BETA_FIRST) * gradient
    second_new = BETA_SECOND * second + (1.0 - BETA_SECOND) * gradient * gradient
    first_hat = first_new / (1.0 - BETA_FIRST ** STEP)
    second_hat = second_new / (1.0 - BETA_SECOND ** STEP)
    weight_new = weight - rate * (first_hat / (jnp.sqrt(second_hat) + ADAM_EPS) + decay * weight)
    return (weight_new, first_new, second_new)

def reference(block_input, cotangent, crop_boxes, front_weights, back_weights, split_biases, norm_params, pos_table, front_first, back_weight_first_moment, split_first, norm_first, table_first, front_second, back_second, split_second, norm_second, table_second):
    cell_count = SIDE * SIDE
    onehot_tokens, is_valid = position_codes(crop_boxes, cell_count, SIDE)
    onehot_tokens = onehot_tokens.astype(jnp.float32)
    grid_total = block_input.shape[0]
    per_step = math.gcd(grid_total, max(1, 4096 // cell_count))
    step_count = grid_total // per_step
    inputs = block_input.astype(jnp.float32).reshape(step_count, per_step, cell_count, D)
    onehot_steps = onehot_tokens.reshape(step_count, per_step, cell_count, cell_count)
    valid_steps = is_valid.reshape(step_count, per_step, cell_count)

    def forward(params, layer_inputs):
        rounded = tuple((low(item) for item in params))

        def one_step(pieces):
            return layer_body(rounded, pieces[0], pieces[1], pieces[2])
        return lax.map(jax.checkpoint(one_step), (layer_inputs, onehot_steps, valid_steps))
    params = (front_weights, back_weights, split_biases, norm_params, pos_table)
    outputs, back_fn = jax.vjp(forward, params, inputs)
    grads, grad_inputs = back_fn(cotangent.astype(jnp.float32).reshape(outputs.shape))
    squares = jnp.float32(0.0)
    for gradient in grads:
        squares = squares + jnp.sum(gradient * gradient)
    clip_norm = jnp.sqrt(squares)
    factor = jnp.minimum(1.0, CLIP_LIMIT / (clip_norm + 1e-06))
    settings = ((RATE_MATRIX, DECAY_RATE), (RATE_MATRIX, DECAY_RATE), (RATE_VECTOR, 0.0), (RATE_VECTOR, 0.0), (RATE_TABLE, DECAY_RATE))
    firsts = (front_first, back_weight_first_moment, split_first, norm_first, table_first)
    second_moments = (front_second, back_second, split_second, norm_second, table_second)
    results = []
    for index in range(5):
        results.append(adam_step(params[index], grads[index] * factor, firsts[index], second_moments[index], settings[index][0], settings[index][1]))
    norm_grad = grads[3] * factor
    block_output = outputs.reshape(block_input.shape).astype(jnp.bfloat16)
    input_grad = grad_inputs.reshape(block_input.shape).astype(jnp.bfloat16)
    return (block_output, input_grad, clip_norm, results[0][0], results[1][0], results[2][0], results[3][0], results[4][0], results[0][1], results[1][1], results[2][1], results[3][1], results[4][1], results[0][2], results[1][2], results[2][2], results[3][2], results[4][2], norm_grad)
```

```python
import functools

import jax
import jax.numpy as jnp
from jax import lax
from jax.experimental import pallas as pl
from jax.experimental.pallas import tpu as pltpu
from jax.sharding import PartitionSpec as P

D = 768
HEADS = 16
HEAD = D // HEADS
SIDE = 16
CELLS = 256
STEP = 5
CORES = 2

NORM_EPS = 1e-05
BETA_FIRST = 0.9
BETA_SECOND = 0.95
ADAM_EPS = 1e-08
RATE_MATRIX = 0.05
RATE_TABLE = 0.2
RATE_VECTOR = 0.5
DECAY_RATE = 0.1
CLIP_LIMIT = 0.01
MASK_FILL = -1e30
SCALE = HEAD ** (-0.5)
LOG2E = 1.4426950408889634
INV_SQRT_2PI = 0.3989422804014327

BF = jnp.bfloat16
F32 = jnp.float32
VMEM_LIMIT = 60 * 1024 * 1024
NN = (((1,), (0,)), ((), ()))
NT = (((1,), (1,)), ((), ()))
TN = (((0,), (0,)), ((), ()))


def dot(a, b, dims=NN):
    return lax.dot_general(a, b, dims, preferred_element_type=F32)


def params(limit=VMEM_LIMIT):
    return pltpu.CompilerParams(vmem_limit_bytes=limit)


def norm_stats(v):
    mean = jnp.mean(v, axis=-1, keepdims=True)
    centred = v - mean
    spread = jnp.mean(centred * centred, axis=-1, keepdims=True)
    rstd = lax.rsqrt(spread + NORM_EPS)
    return centred * rstd, rstd


def norm_back(c, gain, u, rstd):
    cg = c * gain
    mean_cg = jnp.mean(cg, axis=-1, keepdims=True)
    mean_cgu = jnp.mean(cg * u, axis=-1, keepdims=True)
    return rstd * (cg - mean_cg - u * mean_cgu)


def head_window(h):
    low = h * HEAD
    first = low // 128
    last = (low + HEAD - 1) // 128
    return first, last + 1 - first


def head_mask(h):
    first, tiles = head_window(h)
    lane = lax.broadcasted_iota(jnp.int32, (1, tiles * 128), 1) + first * 128
    return (lane >= h * HEAD) & (lane < (h + 1) * HEAD)


def crop_target(position, height, breadth, top, left):
    row = (position >> 4) - top
    col = (position & (SIDE - 1)) - left
    inside = (row >= 0) & (row < height) & (col >= 0) & (col < breadth)
    return jnp.where(inside, row * breadth + col, -1)


def attention_forward_kernel(
    scal, crop, x_ref, table_ref, w_ref, vec_ref,
    emb_ref, n1_ref, q_ref, k_ref, v_ref, p_ref, mixed_ref, after_ref, n2_ref,
):
    grid = scal[0] + pl.program_id(0)
    height, breadth, top, left = crop[grid, 0], crop[grid, 1], crop[grid, 2], crop[grid, 3]
    target = crop_target(
        lax.broadcasted_iota(jnp.int32, (1, CELLS), 1), height, breadth, top, left
    )
    cell = lax.broadcasted_iota(jnp.int32, (CELLS, CELLS), 0)
    onehot = jnp.where(cell == target, 1.0, 0.0).astype(BF)
    emb = x_ref[0].astype(F32) + dot(onehot, table_ref[...])
    emb_ref[...] = emb
    u, _ = norm_stats(emb)
    n1 = (u * vec_ref[0:1, :] + vec_ref[1:2, :]).astype(BF)
    n1_ref[...] = n1
    q_ref[...] = (dot(n1, w_ref[0]) + vec_ref[8:9, :]).astype(BF)
    k_ref[...] = dot(n1, w_ref[1]).astype(BF)
    v_ref[...] = (dot(n1, w_ref[2]) + vec_ref[9:10, :]).astype(BF)
    valid = lax.broadcasted_iota(jnp.int32, (1, CELLS), 1) < height * breadth
    tiles_out = [None] * (D // 128)
    for h in range(HEADS):
        first, tiles = head_window(h)
        lanes = slice(first * 128, (first + tiles) * 128)
        mask = head_mask(h)
        qh = jnp.where(mask, q_ref[:, lanes], 0).astype(BF)
        vh = jnp.where(mask, v_ref[:, lanes], 0).astype(BF)
        s = jnp.where(valid, dot(qh, k_ref[:, lanes], NT), MASK_FILL)
        top_score = jnp.max(s, axis=-1, keepdims=True)
        e = jnp.exp2((s - top_score) * (SCALE * LOG2E))
        p = (e * (1.0 / jnp.sum(e, axis=-1, keepdims=True))).astype(BF)
        p_ref[0, h] = p
        o = dot(p, vh)
        for t in range(tiles):
            part = o[:, t * 128 : (t + 1) * 128]
            at = first + t
            tiles_out[at] = part if tiles_out[at] is None else tiles_out[at] + part
    for t in range(D // 128):
        mixed_ref[:, t * 128 : (t + 1) * 128] = tiles_out[t].astype(BF)
    attention = dot(mixed_ref[...], w_ref[3], NT)
    after = emb_ref[...] + attention + vec_ref[2:3, :]
    after_ref[...] = after
    u2, _ = norm_stats(after)
    n2_ref[...] = (u2 * vec_ref[3:4, :] + vec_ref[4:5, :]).astype(BF)


def up_kernel(scal, n2_ref, w_ref, vec_ref, g_ref, hidden_ref, gp_ref, mine_ref, other_ref, gt_ref):
    j = pl.program_id(0)
    grids = g_ref.shape[0]

    @pl.when(j == 0)
    def _():
        for n in range(grids):
            gt_ref[:, n * CELLS : (n + 1) * CELLS] = g_ref[n].T

    bias = vec_ref[pl.ds(10 + j, 1), :]
    for n in range(grids):
        rows = slice(n * CELLS, (n + 1) * CELLS)
        pre = dot(n2_ref[rows, :], w_ref[0]) + bias
        phi = 0.5 + 0.5 * lax.erf(pre * (0.5**0.5))
        density = jnp.exp2(pre * pre * (-0.5 * LOG2E)) * INV_SQRT_2PI
        hidden_ref[0, rows, :] = (pre * phi).astype(BF)
        gp_ref[0, rows, :] = (phi + pre * density).astype(BF)
    grad = dot(gt_ref[...], hidden_ref[0]).astype(BF)
    keep(scal[1], j, grad, mine_ref, other_ref)


def keep(core, j, grad, mine_ref, other_ref):
    @pl.when(core == j // 2)
    def _():
        mine_ref[j % 2] = grad

    @pl.when(core != j // 2)
    def _():
        other_ref[j % 2] = grad


def mlp_kernel(
    scal, hidden_ref, gp_ref, down_ref, up_ref, n2_ref, g_ref, after_ref, vec_ref,
    out_ref, ga_ref, galow_ref, mine_ref, other_ref, gb_ref, gn_ref,
    mlp_acc, dn2_acc, n2t_ref,
):
    j = pl.program_id(0)
    grids = g_ref.shape[0]

    @pl.when(j == 0)
    def _():
        for n in range(grids):
            rows = slice(n * CELLS, (n + 1) * CELLS)
            n2t_ref[:, rows] = n2_ref[rows, :].T
        mlp_acc[...] = jnp.zeros_like(mlp_acc)
        dn2_acc[...] = jnp.zeros_like(dn2_acc)
        gb_ref[...] = jnp.zeros_like(gb_ref)
        gn_ref[...] = jnp.zeros_like(gn_ref)

    colsum = jnp.zeros((1, D), F32)
    for n in range(grids):
        rows = slice(n * CELLS, (n + 1) * CELLS)
        gh = dot(g_ref[n], down_ref[0])
        gpre = (gh * gp_ref[0, rows, :].astype(F32)).astype(BF)
        gp_ref[0, rows, :] = gpre
        colsum = colsum + jnp.sum(gpre.astype(F32), axis=0, keepdims=True)
        mlp_acc[rows, :] += dot(hidden_ref[0, rows, :], down_ref[0], NT)
        dn2_acc[rows, :] += dot(gpre, up_ref[0], NT)
    gb_ref[pl.ds(j, 1), :] = colsum
    keep(scal[1], j, dot(n2t_ref[...], gp_ref[0]).astype(BF), mine_ref, other_ref)

    @pl.when(j == pl.num_programs(0) - 1)
    def _():
        sums = [jnp.zeros((1, D), F32)] * 4
        for n in range(grids):
            rows = slice(n * CELLS, (n + 1) * CELLS)
            after = after_ref[rows, :]
            out_ref[n] = (after + mlp_acc[rows, :] + vec_ref[5:6, :]).astype(BF)
            u, rstd = norm_stats(after)
            c = dn2_acc[rows, :]
            g = g_ref[n].astype(F32)
            ga = g + norm_back(c, vec_ref[3:4, :], u, rstd)
            ga_ref[rows, :] = ga
            galow_ref[rows, :] = ga.astype(BF)
            parts = (ga, c * u, c, g)
            sums = [s + jnp.sum(v, axis=0, keepdims=True) for s, v in zip(sums, parts)]
        for i in range(4):
            gn_ref[2 + i : 3 + i, :] = sums[i]


def attention_backward_kernel(
    scal, crop, ga_ref, galow_ref, mixed_ref, p_ref, q_ref, k_ref, v_ref, emb_ref, w_ref, vec_ref,
    dq_ref, dk_ref, dv_ref, ig_ref, table_ref, gs_ref, dm_ref,
):
    i = pl.program_id(0)
    grid = scal[0] + i
    height, breadth, top, left = crop[grid, 0], crop[grid, 1], crop[grid, 2], crop[grid, 3]

    @pl.when(i == 0)
    def _():
        table_ref[...] = jnp.zeros_like(table_ref)
        gs_ref[...] = jnp.zeros_like(gs_ref)

    dm_ref[...] = dot(galow_ref[...], w_ref[3]).astype(BF)
    outs = [[None] * (D // 128) for _ in range(3)]
    for h in range(HEADS):
        first, tiles = head_window(h)
        lanes = slice(first * 128, (first + tiles) * 128)
        mask = head_mask(h)
        qh = jnp.where(mask, q_ref[:, lanes], 0).astype(BF)
        kh = jnp.where(mask, k_ref[:, lanes], 0).astype(BF)
        dmh = jnp.where(mask, dm_ref[:, lanes], 0).astype(BF)
        p = p_ref[0, h]
        dp = dot(dmh, v_ref[:, lanes], NT)
        delta = jnp.sum(
            dmh.astype(F32) * mixed_ref[:, lanes].astype(F32), axis=-1, keepdims=True
        )
        ds = (p.astype(F32) * (dp - delta)).astype(BF)
        got = (dot(ds, kh), dot(ds, qh, TN), dot(p, dmh, TN))
        for o in range(3):
            for t in range(tiles):
                part = got[o][:, t * 128 : (t + 1) * 128]
                at = first + t
                outs[o][at] = part if outs[o][at] is None else outs[o][at] + part
    for t in range(D // 128):
        lanes = slice(t * 128, (t + 1) * 128)
        dq_ref[:, lanes] = (outs[0][t] * SCALE).astype(BF)
        dk_ref[:, lanes] = (outs[1][t] * SCALE).astype(BF)
        dv_ref[:, lanes] = outs[2][t].astype(BF)
    dq, dk, dv = dq_ref[...], dk_ref[...], dv_ref[...]
    c = dot(dq, w_ref[0], NT) + dot(dk, w_ref[1], NT) + dot(dv, w_ref[2], NT)
    u, rstd = norm_stats(emb_ref[...])
    ge = ga_ref[...] + norm_back(c, vec_ref[0:1, :], u, rstd)
    high = ge.astype(BF)
    ig_ref[0] = high
    low = (ge - high.astype(F32)).astype(BF)
    target = crop_target(
        lax.broadcasted_iota(jnp.int32, (CELLS, 1), 0), height, breadth, top, left
    )
    cell = lax.broadcasted_iota(jnp.int32, (CELLS, CELLS), 1)
    onehot = jnp.where(cell == target, 1.0, 0.0).astype(BF)
    table_ref[...] += dot(onehot, high) + dot(onehot, low)
    for row, v in enumerate((dq.astype(F32), dv.astype(F32), c * u, c)):
        gs_ref[row : row + 1, :] += jnp.sum(v, axis=0, keepdims=True)


def projection_grad_kernel(
    scal, n1_ref, galow_ref, dq_ref, dk_ref, dv_ref, mixed_ref, mine_ref, other_ref, t_ref
):
    core = scal[1]
    tokens = n1_ref.shape[0]
    for n in range(tokens // CELLS):
        rows = slice(n * CELLS, (n + 1) * CELLS)
        t_ref[:, rows] = n1_ref[rows, :].T
    keep(core, 0, dot(t_ref[...], dq_ref[...]).astype(BF), mine_ref, other_ref)
    keep(core, 1, dot(t_ref[...], dk_ref[...]).astype(BF), mine_ref, other_ref)
    keep(core, 2, dot(t_ref[...], dv_ref[...]).astype(BF), mine_ref, other_ref)
    for n in range(tokens // CELLS):
        rows = slice(n * CELLS, (n + 1) * CELLS)
        t_ref[:, rows] = galow_ref[rows, :].T
    keep(core, 3, dot(t_ref[...], mixed_ref[...]).astype(BF), mine_ref, other_ref)


def sds(shape, dtype):
    return jax.ShapeDtypeStruct(shape, dtype)


def whole_block(shape):
    zeros = (0,) * len(shape)
    return pl.BlockSpec(shape, lambda i, *_: zeros)


def attention_forward(scal, crop, x, table, w, vec, grids):
    tokens = grids * CELLS
    rows = pl.BlockSpec((CELLS, D), lambda i, *_: (i, 0))
    spec = pltpu.PrefetchScalarGridSpec(
        num_scalar_prefetch=2,
        grid=(grids,),
        in_specs=[
            pl.BlockSpec((1, CELLS, D), lambda i, s, c: (s[0] + i, 0, 0)),
            whole_block((CELLS, D)),
            whole_block((4, D, D)),
            whole_block((16, D)),
        ],
        out_specs=[
            rows, rows, rows, rows, rows,
            pl.BlockSpec((1, HEADS, CELLS, CELLS), lambda i, *_: (i, 0, 0, 0)),
            rows, rows, rows,
        ],
    )
    low, full = sds((tokens, D), BF), sds((tokens, D), F32)
    return pl.pallas_call(
        attention_forward_kernel,
        grid_spec=spec,
        out_shape=[
            full, low, low, low, low, sds((grids, HEADS, CELLS, CELLS), BF), low, full, low,
        ],
        compiler_params=params(),
        cost_estimate=pl.CostEstimate(
            flops=8 * tokens * D * D + 64 * tokens * CELLS * 256,
            bytes_accessed=24 * tokens * D,
            transcendentals=tokens * CELLS * HEADS,
        ),
        name="attention_forward",
    )(scal, crop, x, table, w, vec)


def up_forward(scal, n2, w, vec, cotangent, grids):
    tokens = grids * CELLS
    block = pl.BlockSpec((1, tokens, D), lambda j, *_: (j, 0, 0))
    half = whole_block((2, D, D))
    spec = pltpu.PrefetchScalarGridSpec(
        num_scalar_prefetch=1,
        grid=(4,),
        in_specs=[
            whole_block((tokens, D)),
            pl.BlockSpec((1, D, D), lambda j, *_: (j, 0, 0)),
            whole_block((16, D)),
            pl.BlockSpec((grids, CELLS, D), lambda j, s: (s[2], 0, 0)),
        ],
        out_specs=[block, block, half, half],
        scratch_shapes=[pltpu.VMEM((D, tokens), BF)],
    )
    return pl.pallas_call(
        up_kernel,
        grid_spec=spec,
        out_shape=[
            sds((4, tokens, D), BF), sds((4, tokens, D), BF), sds((2, D, D), BF), sds((2, D, D), BF),
        ],
        compiler_params=params(),
        cost_estimate=pl.CostEstimate(
            flops=16 * tokens * D * D, bytes_accessed=40 * tokens * D, transcendentals=8 * tokens * D
        ),
        name="up_forward",
    )(scal, n2, w, vec, cotangent)


def mlp_backward(scal, hidden, gp, down, up, n2, cotangent, after, vec, grids):
    tokens = grids * CELLS
    block = pl.BlockSpec((1, tokens, D), lambda j, *_: (j, 0, 0))
    weight = pl.BlockSpec((1, D, D), lambda j, *_: (j, 0, 0))
    half = whole_block((2, D, D))
    rows = whole_block((tokens, D))
    spec = pltpu.PrefetchScalarGridSpec(
        num_scalar_prefetch=1,
        grid=(4,),
        in_specs=[
            block, block, weight, weight, rows,
            pl.BlockSpec((grids, CELLS, D), lambda j, s: (s[2], 0, 0)),
            rows, whole_block((16, D)),
        ],
        out_specs=[
            whole_block((grids, CELLS, D)), rows, rows, half, half,
            whole_block((8, D)), whole_block((8, D)),
        ],
        scratch_shapes=[
            pltpu.VMEM((tokens, D), F32), pltpu.VMEM((tokens, D), F32), pltpu.VMEM((D, tokens), BF),
        ],
    )
    return pl.pallas_call(
        mlp_kernel,
        grid_spec=spec,
        out_shape=[
            sds((grids, CELLS, D), BF), sds((tokens, D), F32), sds((tokens, D), BF),
            sds((2, D, D), BF), sds((2, D, D), BF), sds((8, D), F32), sds((8, D), F32),
        ],
        compiler_params=params(),
        cost_estimate=pl.CostEstimate(
            flops=32 * tokens * D * D, bytes_accessed=40 * tokens * D, transcendentals=0
        ),
        name="mlp_backward",
    )(scal, hidden, gp, down, up, n2, cotangent, after, vec)


def attention_backward(scal, crop, ga, galow, mixed, p, q, k, v, emb, w, vec, grids):
    tokens = grids * CELLS
    rows = pl.BlockSpec((CELLS, D), lambda i, *_: (i, 0))
    spec = pltpu.PrefetchScalarGridSpec(
        num_scalar_prefetch=2,
        grid=(grids,),
        in_specs=[
            rows, rows, rows,
            pl.BlockSpec((1, HEADS, CELLS, CELLS), lambda i, *_: (i, 0, 0, 0)),
            rows, rows, rows, rows,
            whole_block((4, D, D)),
            whole_block((16, D)),
        ],
        out_specs=[
            rows, rows, rows,
            pl.BlockSpec((1, CELLS, D), lambda i, *_: (i, 0, 0)),
            whole_block((CELLS, D)),
            whole_block((8, D)),
        ],
        scratch_shapes=[pltpu.VMEM((CELLS, D), BF)],
    )
    low = sds((tokens, D), BF)
    return pl.pallas_call(
        attention_backward_kernel,
        grid_spec=spec,
        out_shape=[low, low, low, sds((grids, CELLS, D), BF), sds((CELLS, D), F32), sds((8, D), F32)],
        compiler_params=params(),
        cost_estimate=pl.CostEstimate(
            flops=8 * tokens * D * D + 128 * tokens * CELLS * 256,
            bytes_accessed=32 * tokens * D,
            transcendentals=0,
        ),
        name="attention_backward",
    )(scal, crop, ga, galow, mixed, p, q, k, v, emb, w, vec)


def projection_grad(scal, n1, galow, dq, dk, dv, mixed):
    tokens = n1.shape[0]
    spec = pltpu.PrefetchScalarGridSpec(
        num_scalar_prefetch=1,
        grid=(1,),
        in_specs=[whole_block((tokens, D))] * 6,
        out_specs=[whole_block((2, D, D))] * 2,
        scratch_shapes=[pltpu.VMEM((D, tokens), BF)],
    )
    return pl.pallas_call(
        projection_grad_kernel,
        grid_spec=spec,
        out_shape=[sds((2, D, D), BF), sds((2, D, D), BF)],
        compiler_params=params(),
        cost_estimate=pl.CostEstimate(
            flops=8 * tokens * D * D, bytes_accessed=20 * tokens * D, transcendentals=0
        ),
        name="projection_grad",
    )(scal, n1, galow, dq, dk, dv, mixed)


class Place:
    def __init__(self, dp_size, mp_size):
        self.z_size = dp_size // 2
        dp, mp = lax.axis_index("dp"), lax.axis_index("mp")
        self.dp, self.mp = dp, mp
        self.z, self.y = dp // 2, dp % 2
        self.x, self.c = mp // 2, mp % 2
        self.core_pairs = [(i, i ^ 1) for i in range(mp_size)]
        self.x_pairs = [(i, i ^ 2) for i in range(mp_size)]
        self.y_pairs = [(i, i ^ 1) for i in range(dp_size)]
        self.z_shift = [
            [(i, ((i // 2 + s) % self.z_size) * 2 + i % 2) for i in range(dp_size)]
            for s in range(self.z_size)
        ]

    def core(self, v):
        return lax.ppermute(v, "mp", self.core_pairs)

    def over_x(self, v):
        return lax.ppermute(v, "mp", self.x_pairs)

    def over_y(self, v):
        return lax.ppermute(v, "dp", self.y_pairs)

    def over_z(self, v, shift):
        return lax.ppermute(v, "dp", self.z_shift[shift])


def after_op(value, *earlier):
    return lax.optimization_barrier((value,) + earlier)[0]


def assemble_kernel(rows, extra, where_ref, *refs):
    pieces, outs, sem = refs[:10], refs[10:-1], refs[-1]
    z, y, x, c = where_ref[0], where_ref[1], where_ref[2], where_ref[3]
    depth = pieces[0].shape[1]
    copies = []

    def add(src, dst):
        copies.append(pltpu.make_async_copy(src, dst, sem.at[len(copies)]))

    for core_rel in range(2):
        own, by_x, by_y, diag0, diag1 = pieces[core_rel * 5 : core_rel * 5 + 5]
        core = c if core_rel == 0 else 1 - c
        for s in range(depth):
            zs = lax.rem(z - s + depth, depth)
            for xr in range(2):
                for yr in range(2):
                    xs = x if xr == 0 else 1 - x
                    ys = y if yr == 0 else 1 - y
                    dp = zs * 2 + ys
                    row = pl.ds(pl.multiple_of(dp * rows, rows), rows)
                    lane = pl.ds(pl.multiple_of(xs * (D // 2), D // 2), D // 2)
                    if xr and yr:
                        for b, diag in enumerate((diag0, diag1)):
                            add(diag.at[s, 0:rows], outs[0].at[core * 2 + b, row, lane])
                        first, second = diag0.at[s], diag1.at[s]
                    else:
                        src = (own, by_x, by_y)[xr + 2 * yr]
                        add(
                            src.at[:, s, 0:rows],
                            outs[0].at[pl.ds(core * 2, 2), row, lane],
                        )
                        first, second = src.at[0, s], src.at[1, s]
                    if extra:
                        share = pl.ds(pl.multiple_of((dp * 2 + core) * extra, extra), extra)
                        tail = slice(rows, rows + extra)
                        add(first.at[tail], outs[1].at[share, lane])
                        add(second.at[tail], outs[2].at[dp, xs, core])
    for copy in copies:
        copy.start()
    for copy in copies:
        copy.wait()


def assemble(where, pieces, extra, dp_size):
    rows = D // dp_size
    outs = [sds((4, D, D), BF)]
    if extra:
        outs += [sds((dp_size * 2 * extra, D), BF), sds((dp_size, 2, 2, extra, D // 2), BF)]
    count = (dp_size // 2) * 2 * (3 + 2 + (8 if extra else 0))
    hbm = pl.BlockSpec(memory_space=pl.ANY)
    return pl.pallas_call(
        functools.partial(assemble_kernel, rows, extra),
        in_specs=[pl.BlockSpec(memory_space=pltpu.SMEM)] + [hbm] * 10,
        out_specs=[pl.BlockSpec(memory_space=pltpu.VMEM)] * len(outs),
        out_shape=outs,
        scratch_shapes=[pltpu.SemaphoreType.DMA((count,))],
        compiler_params=params(),
        cost_estimate=pl.CostEstimate(flops=0, bytes_accessed=16 * D * D, transcendentals=0),
        name="assemble",
    )(where, *pieces)


def gather_chunk(place, where, u, extra, dp_size):
    parts = [u] + [place.over_z(u, s) for s in range(1, place.z_size)]
    own = jnp.stack(parts, axis=1)
    by_x, by_y = place.over_x(own), place.over_y(own)
    diag0, diag1 = place.over_y(by_x[0]), place.over_x(by_y[1])
    mine = (own, by_x, by_y, diag0, diag1)
    pieces = mine + tuple(place.core(v) for v in mine)
    return assemble(where, pieces, extra, dp_size), own, (diag0, diag1)


def reduce_group(place, mine, other):
    zs = place.z_size
    rows, lanes = D // (2 * zs), D // 2
    x, y, z, c = place.x, place.y, place.z, place.c
    h = (mine.astype(F32) + place.core(other).astype(F32)).astype(BF)
    h = h.reshape(2, zs, 2, rows, D)

    def y_part(v, at):
        return lax.dynamic_index_in_dim(v, at, axis=1, keepdims=False)

    def x_part(v, at):
        return jnp.where(at == 0, v[..., :lanes], v[..., lanes:])

    def join(a, b):
        return (a.astype(F32) + b.astype(F32)).astype(BF)

    a0 = join(y_part(h[0], y), place.over_y(y_part(h[0], 1 - y)))
    a1 = join(x_part(h[1], x), place.over_x(x_part(h[1], 1 - x)))
    b0 = join(x_part(a0, x), place.over_x(x_part(a0, 1 - x)))
    b1 = join(y_part(a1, y), place.over_y(y_part(a1, 1 - y)))
    b = jnp.stack([b0, b1])

    def z_part(at):
        return lax.dynamic_index_in_dim(b, at, axis=1, keepdims=False)

    total = z_part(z).astype(F32)
    for s in range(1, zs):
        total = total + place.over_z(z_part((z + s) % zs), s).astype(F32)
    left, right = total[..., : lanes // 2], total[..., lanes // 2 :]
    kept = jnp.where(c == 0, left, right)
    got = place.core(jnp.where(c == 0, right, left))
    return jnp.where(c == 0, jnp.concatenate([kept, got]), jnp.concatenate([got, kept]))


def collect_kernel(where_ref, own, by_core, by_x, by_both, out, sem):
    x, c = where_ref[2], where_ref[3]
    grids = own.shape[0]
    copies = []
    for n, (piece, mp) in enumerate(
        ((own, 2 * x + c), (by_core, 2 * x + 1 - c), (by_x, 2 - 2 * x + c), (by_both, 3 - 2 * x - c))
    ):
        copies.append(pltpu.make_async_copy(piece, out.at[pl.ds(mp * grids, grids)], sem.at[n]))
    for copy in copies:
        copy.start()
    for copy in copies:
        copy.wait()


def gather_grids(place, where, own):
    by_core, by_x = place.core(own), place.over_x(own)
    by_both = place.core(by_x)
    hbm = pl.BlockSpec(memory_space=pl.ANY)
    return pl.pallas_call(
        collect_kernel,
        in_specs=[pl.BlockSpec(memory_space=pltpu.SMEM)] + [hbm] * 4,
        out_specs=pl.BlockSpec(memory_space=pltpu.VMEM),
        out_shape=sds((4 * own.shape[0],) + own.shape[1:], own.dtype),
        scratch_shapes=[pltpu.SemaphoreType.DMA((4,))],
        compiler_params=params(),
        cost_estimate=pl.CostEstimate(flops=0, bytes_accessed=8 * own.size, transcendentals=0),
        name="collect",
    )(where, own, by_core, by_x, by_both)


def sum_everywhere(place, value):
    value = value + place.core(value)
    value = value + place.over_x(value)
    value = value + place.over_y(value)
    total = value
    for s in range(1, place.z_size):
        total = total + place.over_z(value, s)
    return total


def adam_step(weight, gradient, first, second, rate, decay):
    first_new = BETA_FIRST * first + (1.0 - BETA_FIRST) * gradient
    second_new = BETA_SECOND * second + (1.0 - BETA_SECOND) * gradient * gradient
    first_hat = first_new / (1.0 - BETA_FIRST**STEP)
    second_hat = second_new / (1.0 - BETA_SECOND**STEP)
    weight_new = weight - rate * (first_hat / (jnp.sqrt(second_hat) + ADAM_EPS) + decay * weight)
    return (weight_new, first_new, second_new)


def body(
    dp_size, mp_size,
    block_input, cotangent, crop_boxes, front_weights, back_weights, split_biases, norm_params,
    pos_table, front_first, back_weight_first_moment, split_first, norm_first, table_first,
    front_second, back_second, split_second, norm_second, table_second,
):
    place = Place(dp_size, mp_size)
    direct = dp_size == 8 and mp_size == 4
    x, y, z, c = place.x, place.y, place.z, place.c
    grids = block_input.shape[0] // mp_size
    scal = jnp.stack([place.mp * grids, c, place.mp, place.dp]).astype(jnp.int32)
    where = jnp.stack([z, y, x, c]).astype(jnp.int32)
    turned = jnp.swapaxes(back_weights, 1, 2).astype(BF)
    low_front = front_weights.astype(BF)
    rows, lanes = low_front.shape[1], low_front.shape[2]

    if direct:
        shards = jnp.concatenate([low_front[:3], turned[:1], low_front[3:], turned[1:]])
        shards = shards.reshape(3, 2, 2, rows, lanes)
        mine = lax.dynamic_index_in_dim(shards, c, axis=1, keepdims=False)
        sent = lax.dynamic_index_in_dim(shards, 1 - c, axis=1, keepdims=False)
        got = place.core(sent)
        units = jnp.where(
            c == 0, jnp.concatenate([mine, got], -1), jnp.concatenate([got, mine], -1)
        )
        extra = pos_table.shape[0] // 2
        half = jnp.where(c == 0, pos_table[:extra], pos_table[extra:]).astype(BF)
        half = jnp.where(x == 0, half[:, : D // 2], half[:, D // 2 :])
        packed = jnp.zeros((extra, D // 2), BF)
        packed = lax.dynamic_update_slice(packed, norm_params.astype(BF), (0, 0))
        packed = lax.dynamic_update_slice(packed, split_biases.astype(BF), (0, 128))
        first_unit = jnp.concatenate([units[0], jnp.stack([half, packed])], axis=1)
        (w_attn, table, codes), gate1, _ = gather_chunk(place, where, first_unit, extra, dp_size)
        second_unit = after_op(units[1], gate1)
        (w_up,), gate2, last2 = gather_chunk(place, where, second_unit, 0, dp_size)
        third_unit = after_op(units[2], gate2)
        (w_down,), _, _ = gather_chunk(place, where, third_unit, 0, dp_size)
        norms = jnp.swapaxes(codes[:, 0, 0, 0:6, : norm_params.shape[1]], 0, 1).reshape(6, D)
        splits = codes[:, :, :, 0:6, 128 : 128 + split_biases.shape[1]]
        splits = jnp.transpose(splits, (3, 1, 2, 0, 4)).reshape(6, D)
    else:

        def whole(v):
            v = lax.all_gather(v, "dp", axis=1, tiled=True)
            return lax.all_gather(v, "mp", axis=2, tiled=True)

        w_attn = whole(jnp.concatenate([low_front[:3], turned[:1]]))
        w_up, w_down = whole(low_front[3:]), whole(turned[1:])
        table = lax.all_gather(pos_table.astype(BF), "dp", axis=0, tiled=True)
        norms = lax.all_gather(norm_params.astype(BF), "dp", axis=1, tiled=True)
        splits = lax.all_gather(split_biases.astype(BF), ("mp", "dp"), axis=1, tiled=True)
    gap = jnp.zeros((2, D), F32)
    vec = jnp.concatenate([norms.astype(F32), gap, splits.astype(F32), gap])

    emb, n1, q, k, v, p, mixed, after, n2 = attention_forward(
        scal, crop_boxes, block_input, table, w_attn, vec, grids
    )
    hidden, gp, down_mine, down_other = up_forward(scal, n2, w_up, vec, cotangent, grids)
    out, ga, galow, up_mine, up_other, gb, gn = mlp_backward(
        scal, hidden, gp, w_down, w_up, n2, cotangent, after, vec, grids
    )
    dq, dk, dv, ig, dtable, gs = attention_backward(
        scal, crop_boxes, ga, galow, mixed, p, q, k, v, emb, w_attn, vec, grids
    )
    attn_mine, attn_other = projection_grad(scal, n1, galow, dq, dk, dv, mixed)

    norm_grad = jnp.concatenate([gs[2:4], gn[2:6]])
    split_grad = jnp.concatenate([gs[0:2], gb[0:4]])
    if direct:
        down_share = reduce_group(place, down_mine, down_other)
        up_share = reduce_group(place, up_mine, up_other)
        attn_share = reduce_group(place, attn_mine, attn_other)
        block_output = gather_grids(place, where, out)
        input_grad = gather_grids(place, where, ig)
        small = lax.psum(jnp.concatenate([dtable, norm_grad, split_grad]), ("dp", "mp"))
        dtable, norm_grad, split_grad = small[:CELLS], small[CELLS : CELLS + 6], small[CELLS + 6 :]
    else:

        def share(mine, other):
            full = jnp.where(
                c == 0, jnp.concatenate([mine, other]), jnp.concatenate([other, mine])
            ).astype(F32)
            full = lax.psum_scatter(full, "dp", scatter_dimension=1, tiled=True)
            return lax.psum_scatter(full, "mp", scatter_dimension=2, tiled=True)

        down_share = share(down_mine, down_other)
        up_share = share(up_mine, up_other)
        attn_share = share(attn_mine, attn_other)
        block_output = lax.all_gather(out, "mp", axis=0, tiled=True)
        input_grad = lax.all_gather(ig, "mp", axis=0, tiled=True)
        dtable = lax.psum(dtable, ("dp", "mp"))
        norm_grad = lax.psum(norm_grad, ("dp", "mp"))
        split_grad = lax.psum(split_grad, ("dp", "mp"))
    cells_here, norm_here = pos_table.shape[0], norm_params.shape[1]
    split_here = split_biases.shape[1]
    table_share = lax.dynamic_slice(dtable, (place.dp * cells_here, 0), (cells_here, D))
    norm_share = lax.dynamic_slice(norm_grad, (0, place.dp * norm_here), (6, norm_here))
    split_share = lax.dynamic_slice(
        split_grad, (0, (place.mp * dp_size + place.dp) * split_here), (6, split_here)
    )
    front_share = jnp.concatenate([attn_share[:3], up_share])
    back_share = jnp.concatenate([attn_share[3:], down_share])
    owner = (place.mp == 0).astype(F32)
    square = (
        jnp.sum(attn_share * attn_share)
        + jnp.sum(up_share * up_share)
        + jnp.sum(down_share * down_share)
        + jnp.sum(split_share * split_share)
        + owner * (jnp.sum(norm_share * norm_share) + jnp.sum(table_share * table_share))
    )
    if direct:
        clip_norm = jnp.sqrt(sum_everywhere(place, square.reshape(1, 1)))[0, 0]
    else:
        clip_norm = jnp.sqrt(lax.psum(square, ("dp", "mp")))
    factor = jnp.minimum(1.0, CLIP_LIMIT / (clip_norm + 1e-06))
    norm_clipped = norm_share * factor
    new_front, front_first_new, front_second_new = adam_step(
        front_weights, front_share * factor, front_first, front_second, RATE_MATRIX, DECAY_RATE
    )
    new_back, back_first_new, back_second_new = adam_step(
        back_weights,
        jnp.swapaxes(back_share, 1, 2) * factor,
        back_weight_first_moment,
        back_second,
        RATE_MATRIX,
        DECAY_RATE,
    )
    new_split, split_first_new, split_second_new = adam_step(
        split_biases, split_share * factor, split_first, split_second, RATE_VECTOR, 0.0
    )
    new_norm, norm_first_new, norm_second_new = adam_step(
        norm_params, norm_clipped, norm_first, norm_second, RATE_VECTOR, 0.0
    )
    new_table, table_first_new, table_second_new = adam_step(
        pos_table, table_share * factor, table_first, table_second, RATE_TABLE, DECAY_RATE
    )
    return (
        block_output, input_grad, clip_norm,
        new_front, new_back, new_split, new_norm, new_table,
        front_first_new, back_first_new, split_first_new, norm_first_new, table_first_new,
        front_second_new, back_second_new, split_second_new, norm_second_new, table_second_new,
        norm_clipped,
    )


def solution(mesh):
    front, back = P(None, "dp", "mp"), P(None, "mp", "dp")
    split, norm, table = P(None, ("mp", "dp")), P(None, "dp"), P("dp", None)
    state = (front, back, split, norm, table)
    rows = P("dp", None, None)
    return jax.shard_map(
        functools.partial(body, mesh.shape["dp"], mesh.shape["mp"]),
        mesh=mesh,
        in_specs=(rows, rows, P("dp", None)) + state * 3,
        out_specs=(rows, rows, P()) + state * 3 + (norm,),
        check_vma=False,
    )
```

```python
import functools

import jax
import jax.numpy as jnp
from jax import lax
from jax.experimental import pallas as pl
from jax.experimental.pallas import tpu as pltpu
from jax.sharding import PartitionSpec as P

D = 768
HEADS = 16
HEAD = D // HEADS
SIDE = 16
CELLS = 256
STEP = 5
CORES = 2

NORM_EPS = 1e-05
BETA_FIRST = 0.9
BETA_SECOND = 0.95
ADAM_EPS = 1e-08
RATE_MATRIX = 0.05
RATE_TABLE = 0.2
RATE_VECTOR = 0.5
DECAY_RATE = 0.1
CLIP_LIMIT = 0.01
MASK_FILL = -1e30
SCALE = HEAD ** (-0.5)
LOG2E = 1.4426950408889634
INV_SQRT_2PI = 0.3989422804014327

OWNERS = 8
HALF = D // (2 * OWNERS)
SMALL = 32

BF = jnp.bfloat16
F32 = jnp.float32
MIB = 1024 * 1024
NN = (((1,), (0,)), ((), ()))
NT = (((1,), (1,)), ((), ()))
TN = (((0,), (0,)), ((), ()))


def dot(a, b, dims=NN):
    return lax.dot_general(a, b, dims, preferred_element_type=F32)


def params(limit):
    return pltpu.CompilerParams(vmem_limit_bytes=limit)


def norm_stats(v):
    mean = jnp.mean(v, axis=-1, keepdims=True)
    centred = v - mean
    spread = jnp.mean(centred * centred, axis=-1, keepdims=True)
    rstd = lax.rsqrt(spread + NORM_EPS)
    return centred * rstd, rstd


def norm_back(c, gain, u, rstd):
    cg = c * gain
    mean_cg = jnp.mean(cg, axis=-1, keepdims=True)
    mean_cgu = jnp.mean(cg * u, axis=-1, keepdims=True)
    return rstd * (cg - mean_cg - u * mean_cgu)


def head_window(h):
    low = h * HEAD
    first = low // 128
    last = (low + HEAD - 1) // 128
    return first, last + 1 - first


def head_mask(h):
    first, tiles = head_window(h)
    lane = lax.broadcasted_iota(jnp.int32, (1, tiles * 128), 1) + first * 128
    return (lane >= h * HEAD) & (lane < (h + 1) * HEAD)


def crop_target(position, height, breadth, top, left):
    row = (position >> 4) - top
    col = (position & (SIDE - 1)) - left
    inside = (row >= 0) & (row < height) & (col >= 0) & (col < breadth)
    return jnp.where(inside, row * breadth + col, -1)


def attention_forward_kernel(
    scal, crop, x_ref, table_ref, w_ref, vec_ref,
    emb_ref, n1_ref, q_ref, k_ref, v_ref, p_ref, mixed_ref, after_ref, n2_ref,
):
    grid = scal[0] + pl.program_id(0)
    height, breadth, top, left = crop[grid, 0], crop[grid, 1], crop[grid, 2], crop[grid, 3]
    target = crop_target(
        lax.broadcasted_iota(jnp.int32, (1, CELLS), 1), height, breadth, top, left
    )
    cell = lax.broadcasted_iota(jnp.int32, (CELLS, CELLS), 0)
    onehot = jnp.where(cell == target, 1.0, 0.0).astype(BF)
    emb = x_ref[0].astype(F32) + dot(onehot, table_ref[...])
    emb_ref[...] = emb
    u, _ = norm_stats(emb)
    n1 = (u * vec_ref[0:1, :] + vec_ref[1:2, :]).astype(BF)
    n1_ref[...] = n1
    q_ref[...] = (dot(n1, w_ref[0]) + vec_ref[8:9, :]).astype(BF)
    k_ref[...] = dot(n1, w_ref[1]).astype(BF)
    v_ref[...] = (dot(n1, w_ref[2]) + vec_ref[9:10, :]).astype(BF)
    valid = lax.broadcasted_iota(jnp.int32, (1, CELLS), 1) < height * breadth
    tiles_out = [None] * (D // 128)
    for h in range(HEADS):
        first, tiles = head_window(h)
        lanes = slice(first * 128, (first + tiles) * 128)
        mask = head_mask(h)
        qh = jnp.where(mask, q_ref[:, lanes], 0).astype(BF)
        vh = jnp.where(mask, v_ref[:, lanes], 0).astype(BF)
        s = jnp.where(valid, dot(qh, k_ref[:, lanes], NT), MASK_FILL)
        top_score = jnp.max(s, axis=-1, keepdims=True)
        e = jnp.exp2((s - top_score) * (SCALE * LOG2E))
        p = (e * (1.0 / jnp.sum(e, axis=-1, keepdims=True))).astype(BF)
        p_ref[0, h] = p
        o = dot(p, vh)
        for t in range(tiles):
            part = o[:, t * 128 : (t + 1) * 128]
            at = first + t
            tiles_out[at] = part if tiles_out[at] is None else tiles_out[at] + part
    for t in range(D // 128):
        mixed_ref[:, t * 128 : (t + 1) * 128] = tiles_out[t].astype(BF)
    attention = dot(mixed_ref[...], w_ref[3], NT)
    after = emb_ref[...] + attention + vec_ref[2:3, :]
    after_ref[...] = after
    u2, _ = norm_stats(after)
    n2_ref[...] = (u2 * vec_ref[3:4, :] + vec_ref[4:5, :]).astype(BF)


def up_kernel(scal, n2_ref, w_ref, vec_ref, g_ref, hidden_ref, gp_ref, mine_ref, other_ref, gt_ref):
    j = pl.program_id(0)
    grids = g_ref.shape[0]

    @pl.when(j == 0)
    def _():
        for n in range(grids):
            gt_ref[:, n * CELLS : (n + 1) * CELLS] = g_ref[n].T

    bias = vec_ref[pl.ds(10 + j, 1), :]
    for n in range(grids):
        rows = slice(n * CELLS, (n + 1) * CELLS)
        pre = dot(n2_ref[rows, :], w_ref[0]) + bias
        phi = 0.5 + 0.5 * lax.erf(pre * (0.5**0.5))
        density = jnp.exp2(pre * pre * (-0.5 * LOG2E)) * INV_SQRT_2PI
        hidden_ref[0, rows, :] = (pre * phi).astype(BF)
        gp_ref[0, rows, :] = (phi + pre * density).astype(BF)
    grad = dot(gt_ref[...], hidden_ref[0]).astype(BF)
    keep(scal[1], 0, grad, mine_ref, other_ref)


def keep(core, at, grad, mine_ref, other_ref):
    parts = grad.reshape(OWNERS, 2, HALF, D)
    rows = slice(at * HALF, (at + 1) * HALF)

    @pl.when(core == 0)
    def _():
        mine_ref[:, rows, :] = parts[:, 0]
        other_ref[:, rows, :] = parts[:, 1]

    @pl.when(core != 0)
    def _():
        mine_ref[:, rows, :] = parts[:, 1]
        other_ref[:, rows, :] = parts[:, 0]


def down_kernel(hidden_ref, down_ref, after_ref, vec_ref, out_ref):
    total = dot(hidden_ref[0], down_ref[0], NT)
    for j in range(1, 4):
        total = total + dot(hidden_ref[j], down_ref[j], NT)
    out_ref[0] = (after_ref[...] + total + vec_ref[5:6, :]).astype(BF)


def mlp_kernel(
    scal, gp_ref, down_ref, up_ref, n2_ref, g_ref, after_any, vec_ref, mixed_any,
    ga_ref, galow_ref, mine_ref, other_ref, gb_ref, gn_ref,
    dn2_acc, n2t_ref, gpre_ref, after_ref, mixed_ref, sem,
):
    j = pl.program_id(0)
    grids = g_ref.shape[0]
    core = scal[1]
    late = (
        pltpu.make_async_copy(after_any, after_ref, sem.at[0]),
        pltpu.make_async_copy(mixed_any, mixed_ref, sem.at[1]),
    )

    @pl.when(j == 0)
    def _():
        for copy in late:
            copy.start()
        for n in range(grids):
            rows = slice(n * CELLS, (n + 1) * CELLS)
            n2t_ref[:, rows] = n2_ref[rows, :].T
        gb_ref[...] = jnp.zeros_like(gb_ref)
        gn_ref[...] = jnp.zeros_like(gn_ref)

    @pl.when(j < 4)
    def _():
        colsum = jnp.zeros((1, D), F32)
        for n in range(grids):
            rows = slice(n * CELLS, (n + 1) * CELLS)
            gh = dot(g_ref[n], down_ref[0])
            gpre = (gh * gp_ref[0, rows, :].astype(F32)).astype(BF)
            gpre_ref[rows, :] = gpre
            colsum = colsum + jnp.sum(gpre.astype(F32), axis=0, keepdims=True)
            part = dot(gpre, up_ref[0], NT)

            @pl.when(j == 0)
            def _():
                dn2_acc[rows, :] = part

            @pl.when(j > 0)
            def _():
                dn2_acc[rows, :] += part

        gb_ref[pl.ds(j, 1), :] = colsum
        keep(core, 0, dot(n2t_ref[...], gpre_ref[...]).astype(BF), mine_ref, other_ref)

    @pl.when(j == 4)
    def _():
        for copy in late:
            copy.wait()
        sums = [jnp.zeros((1, D), F32)] * 4
        for n in range(grids):
            rows = slice(n * CELLS, (n + 1) * CELLS)
            u, rstd = norm_stats(after_ref[rows, :])
            c = dn2_acc[rows, :]
            g = g_ref[n].astype(F32)
            ga = g + norm_back(c, vec_ref[3:4, :], u, rstd)
            ga_ref[rows, :] = ga
            galow = ga.astype(BF)
            galow_ref[rows, :] = galow
            n2t_ref[:, rows] = galow.T
            parts = (ga, c * u, c, g)
            sums = [s + jnp.sum(v, axis=0, keepdims=True) for s, v in zip(sums, parts)]
        for i in range(4):
            gn_ref[2 + i : 3 + i, :] = sums[i]
        keep(core, 0, dot(n2t_ref[...], mixed_ref[...]).astype(BF), mine_ref, other_ref)


def attention_backward_kernel(
    scal, crop, ga_ref, galow_ref, mixed_ref, p_ref, q_ref, k_ref, v_ref, emb_ref, n1_ref,
    w_ref, vec_ref, gn_ref, gb_ref,
    ig_ref, table_out, gs_out, mine_ref, other_ref,
    dm_ref, dq_all, dk_all, dv_all, n1t_ref, table_ref, gs_ref,
):
    i = pl.program_id(0)
    grids = pl.num_programs(0) - 1
    core = scal[1]

    @pl.when(i == 0)
    def _():
        table_ref[...] = jnp.zeros_like(table_ref)
        gs_ref[...] = jnp.zeros_like(gs_ref)

    @pl.when(i < grids)
    def _():
        grid = scal[0] + i
        height, breadth, top, left = crop[grid, 0], crop[grid, 1], crop[grid, 2], crop[grid, 3]
        here = pl.ds(pl.multiple_of(i * CELLS, CELLS), CELLS)
        n1t_ref[:, here] = n1_ref[...].T
        dm_ref[...] = dot(galow_ref[...], w_ref[3]).astype(BF)
        outs = [[None] * (D // 128) for _ in range(3)]
        for h in range(HEADS):
            first, tiles = head_window(h)
            lanes = slice(first * 128, (first + tiles) * 128)
            mask = head_mask(h)
            qh = jnp.where(mask, q_ref[:, lanes], 0).astype(BF)
            kh = jnp.where(mask, k_ref[:, lanes], 0).astype(BF)
            dmh = jnp.where(mask, dm_ref[:, lanes], 0).astype(BF)
            p = p_ref[0, h]
            dp = dot(dmh, v_ref[:, lanes], NT)
            delta = jnp.sum(
                dmh.astype(F32) * mixed_ref[:, lanes].astype(F32), axis=-1, keepdims=True
            )
            ds = (p.astype(F32) * (dp - delta)).astype(BF)
            got = (dot(ds, kh), dot(ds, qh, TN), dot(p, dmh, TN))
            for o in range(3):
                for t in range(tiles):
                    part = got[o][:, t * 128 : (t + 1) * 128]
                    at = first + t
                    outs[o][at] = part if outs[o][at] is None else outs[o][at] + part
        for t in range(D // 128):
            lanes = slice(t * 128, (t + 1) * 128)
            dq_all[here, lanes] = (outs[0][t] * SCALE).astype(BF)
            dk_all[here, lanes] = (outs[1][t] * SCALE).astype(BF)
            dv_all[here, lanes] = outs[2][t].astype(BF)
        dq, dk, dv = dq_all[here, :], dk_all[here, :], dv_all[here, :]
        c = dot(dq, w_ref[0], NT) + dot(dk, w_ref[1], NT) + dot(dv, w_ref[2], NT)
        u, rstd = norm_stats(emb_ref[...])
        ge = ga_ref[...] + norm_back(c, vec_ref[0:1, :], u, rstd)
        high = ge.astype(BF)
        ig_ref[0] = high
        low = (ge - high.astype(F32)).astype(BF)
        target = crop_target(
            lax.broadcasted_iota(jnp.int32, (CELLS, 1), 0), height, breadth, top, left
        )
        cell = lax.broadcasted_iota(jnp.int32, (CELLS, CELLS), 1)
        onehot = jnp.where(cell == target, 1.0, 0.0).astype(BF)
        table_ref[...] += dot(onehot, high) + dot(onehot, low)
        for row, v in enumerate((dq.astype(F32), dv.astype(F32), c * u, c)):
            gs_ref[row : row + 1, :] += jnp.sum(v, axis=0, keepdims=True)

    @pl.when(i == grids)
    def _():
        for b, ref in enumerate((dq_all, dk_all, dv_all)):
            keep(core, b, dot(n1t_ref[...], ref[...]).astype(BF), mine_ref, other_ref)
        table_out[...] = table_ref[...]
        gs_out[...] = gs_ref[...]
        start = 3 * HALF
        table = table_ref[...].astype(BF).reshape(OWNERS, 2, 16, D)
        norm = jnp.concatenate([gs_ref[2:4, :], gn_ref[2:6, :]], axis=0).astype(BF)
        split = jnp.concatenate([gs_ref[0:2, :], gb_ref[0:4, :]], axis=0).astype(BF)
        wide, thin = D // OWNERS, D // (4 * OWNERS)
        side = D // 2

        def small(ref, half):
            ref[:, start : start + 16, :] = table[:, half]
            ref[:, start + 16 : start + 32, :] = jnp.zeros((OWNERS, 16, D), BF)
            for dp in range(OWNERS):
                for x in range(2):
                    lane = x * side
                    ref[dp, start + 16 : start + 22, lane : lane + wide] = norm[
                        :, dp * wide : (dp + 1) * wide
                    ]
                    at = (2 * x + half) * (D // 4) + dp * thin
                    ref[dp, start + 24 : start + 30, lane : lane + thin] = split[:, at : at + thin]

        @pl.when(core == 0)
        def _():
            small(mine_ref, 0)
            small(other_ref, 1)

        @pl.when(core != 0)
        def _():
            small(mine_ref, 1)
            small(other_ref, 0)


def sds(shape, dtype):
    return jax.ShapeDtypeStruct(shape, dtype)


def half_shape(blocks, extra=0):
    return sds((OWNERS, blocks * HALF + extra, D), BF)


def whole_block(shape, buffers=None):
    zeros = (0,) * len(shape)
    mode = None if buffers is None else pl.Buffered(buffers)
    return pl.BlockSpec(shape, lambda i, *_: zeros, pipeline_mode=mode)


def attention_forward(scal, crop, x, table, w, vec, grids):
    tokens = grids * CELLS
    rows = pl.BlockSpec((CELLS, D), lambda i, *_: (i, 0))
    spec = pltpu.PrefetchScalarGridSpec(
        num_scalar_prefetch=2,
        grid=(grids,),
        in_specs=[
            pl.BlockSpec((1, CELLS, D), lambda i, s, c: (s[0] + i, 0, 0)),
            whole_block((CELLS, D)),
            whole_block((4, D, D), 1),
            whole_block((16, D)),
        ],
        out_specs=[
            rows, rows, rows, rows, rows,
            pl.BlockSpec((1, HEADS, CELLS, CELLS), lambda i, *_: (i, 0, 0, 0)),
            rows, rows, rows,
        ],
    )
    low, full = sds((tokens, D), BF), sds((tokens, D), F32)
    return pl.pallas_call(
        attention_forward_kernel,
        grid_spec=spec,
        out_shape=[
            full, low, low, low, low, sds((grids, HEADS, CELLS, CELLS), BF), low, full, low,
        ],
        compiler_params=params(32 * MIB),
        cost_estimate=pl.CostEstimate(
            flops=8 * tokens * D * D + 64 * tokens * CELLS * 256,
            bytes_accessed=24 * tokens * D,
            transcendentals=tokens * CELLS * HEADS,
        ),
        name="attention_forward",
    )(scal, crop, x, table, w, vec)


def up_forward(scal, n2, w, vec, cotangent, grids):
    tokens = grids * CELLS
    block = pl.BlockSpec((1, tokens, D), lambda j, *_: (j, 0, 0))
    half = pl.BlockSpec((OWNERS, HALF, D), lambda j, *_: (0, j, 0))
    spec = pltpu.PrefetchScalarGridSpec(
        num_scalar_prefetch=1,
        grid=(4,),
        in_specs=[
            whole_block((tokens, D), 1),
            pl.BlockSpec((1, D, D), lambda j, *_: (j, 0, 0)),
            whole_block((16, D)),
            pl.BlockSpec((grids, CELLS, D), lambda j, s: (s[2], 0, 0), pipeline_mode=pl.Buffered(1)),
        ],
        out_specs=[block, block, half, half],
        scratch_shapes=[pltpu.VMEM((D, tokens), BF)],
    )
    return pl.pallas_call(
        up_kernel,
        grid_spec=spec,
        out_shape=[
            sds((4, tokens, D), BF), sds((4, tokens, D), BF), half_shape(4), half_shape(4),
        ],
        compiler_params=params(32 * MIB),
        cost_estimate=pl.CostEstimate(
            flops=16 * tokens * D * D, bytes_accessed=40 * tokens * D, transcendentals=8 * tokens * D
        ),
        name="up_forward",
    )(scal, n2, w, vec, cotangent)


def down_forward(hidden, down, after, vec, grids):
    tokens = grids * CELLS
    return pl.pallas_call(
        down_kernel,
        grid=(grids,),
        in_specs=[
            pl.BlockSpec((4, CELLS, D), lambda i: (0, i, 0)),
            whole_block((4, D, D), 1),
            pl.BlockSpec((CELLS, D), lambda i: (i, 0)),
            whole_block((16, D)),
        ],
        out_specs=pl.BlockSpec((1, CELLS, D), lambda i: (i, 0, 0)),
        out_shape=sds((grids, CELLS, D), BF),
        compiler_params=params(24 * MIB),
        cost_estimate=pl.CostEstimate(
            flops=8 * tokens * D * D, bytes_accessed=20 * tokens * D, transcendentals=0
        ),
        name="down_forward",
    )(hidden, down, after, vec)


def mlp_backward(scal, gp, down, up, n2, cotangent, after, vec, mixed, grids):
    tokens = grids * CELLS
    last = lambda j: jnp.minimum(j, 3)
    block = pl.BlockSpec((1, tokens, D), lambda j, *_: (last(j), 0, 0))
    weight = pl.BlockSpec((1, D, D), lambda j, *_: (last(j), 0, 0))
    half = pl.BlockSpec((OWNERS, HALF, D), lambda j, *_: (0, j, 0))
    rows = whole_block((tokens, D))
    any_spec = pl.BlockSpec(memory_space=pl.ANY)
    spec = pltpu.PrefetchScalarGridSpec(
        num_scalar_prefetch=1,
        grid=(5,),
        in_specs=[
            block, weight, weight, whole_block((tokens, D), 1),
            pl.BlockSpec((grids, CELLS, D), lambda j, s: (s[2], 0, 0), pipeline_mode=pl.Buffered(1)),
            any_spec, whole_block((16, D)), any_spec,
        ],
        out_specs=[rows, rows, half, half, whole_block((8, D)), whole_block((8, D))],
        scratch_shapes=[
            pltpu.VMEM((tokens, D), F32), pltpu.VMEM((D, tokens), BF), pltpu.VMEM((tokens, D), BF),
            pltpu.VMEM((tokens, D), F32), pltpu.VMEM((tokens, D), BF),
            pltpu.SemaphoreType.DMA((2,)),
        ],
    )
    return pl.pallas_call(
        mlp_kernel,
        grid_spec=spec,
        out_shape=[
            sds((tokens, D), F32), sds((tokens, D), BF),
            half_shape(5), half_shape(5), sds((8, D), F32), sds((8, D), F32),
        ],
        compiler_params=params(40 * MIB * tokens // 768),
        cost_estimate=pl.CostEstimate(
            flops=26 * tokens * D * D, bytes_accessed=36 * tokens * D, transcendentals=0
        ),
        name="mlp_backward",
    )(scal, gp, down, up, n2, cotangent, after, vec, mixed)


def attention_backward(scal, crop, ga, galow, mixed, p, q, k, v, emb, n1, w, vec, gn, gb, grids):
    tokens = grids * CELLS
    last = lambda i: jnp.minimum(i, grids - 1)
    rows = pl.BlockSpec((CELLS, D), lambda i, *_: (last(i), 0))
    half = half_shape(3, SMALL)
    few = whole_block((8, D))
    spec = pltpu.PrefetchScalarGridSpec(
        num_scalar_prefetch=2,
        grid=(grids + 1,),
        in_specs=[
            rows, rows, rows,
            pl.BlockSpec((1, HEADS, CELLS, CELLS), lambda i, *_: (last(i), 0, 0, 0)),
            rows, rows, rows, rows, rows,
            whole_block((4, D, D), 1),
            whole_block((16, D)), few, few,
        ],
        out_specs=[
            pl.BlockSpec((1, CELLS, D), lambda i, *_: (last(i), 0, 0)),
            whole_block((CELLS, D)),
            few,
            whole_block(half.shape, 1), whole_block(half.shape, 1),
        ],
        scratch_shapes=[pltpu.VMEM((CELLS, D), BF)]
        + [pltpu.VMEM((tokens, D), BF)] * 3
        + [pltpu.VMEM((D, tokens), BF), pltpu.VMEM((CELLS, D), F32), pltpu.VMEM((8, D), F32)],
    )
    return pl.pallas_call(
        attention_backward_kernel,
        grid_spec=spec,
        out_shape=[sds((grids, CELLS, D), BF), sds((CELLS, D), F32), sds((8, D), F32), half, half],
        compiler_params=params(40 * MIB),
        cost_estimate=pl.CostEstimate(
            flops=14 * tokens * D * D + 128 * tokens * CELLS * 256,
            bytes_accessed=32 * tokens * D,
            transcendentals=0,
        ),
        name="attention_backward",
    )(scal, crop, ga, galow, mixed, p, q, k, v, emb, n1, w, vec, gn, gb)


class Place:
    def __init__(self, dp_size, mp_size):
        self.z_size = dp_size // 2
        dp, mp = lax.axis_index("dp"), lax.axis_index("mp")
        self.dp, self.mp = dp, mp
        self.z, self.y = dp // 2, dp % 2
        self.x, self.c = mp // 2, mp % 2
        self.core_pairs = [(i, i ^ 1) for i in range(mp_size)]
        self.x_pairs = [(i, i ^ 2) for i in range(mp_size)]
        self.y_pairs = [(i, i ^ 1) for i in range(dp_size)]
        self.z_shift = [
            [(i, ((i // 2 + s) % self.z_size) * 2 + i % 2) for i in range(dp_size)]
            for s in range(self.z_size)
        ]

        self.corner_pairs = [
            (d * mp_size + m, (d ^ 1) * mp_size + (m ^ 2))
            for d in range(dp_size)
            for m in range(mp_size)
        ]

    def core(self, v):
        return lax.ppermute(v, "mp", self.core_pairs)

    def over_corner(self, v):
        return lax.ppermute(v, ("dp", "mp"), self.corner_pairs)

    def over_x(self, v):
        return lax.ppermute(v, "mp", self.x_pairs)

    def over_y(self, v):
        return lax.ppermute(v, "dp", self.y_pairs)

    def over_z(self, v, shift):
        return lax.ppermute(v, "dp", self.z_shift[shift])


def after_op(value, *earlier):
    return lax.optimization_barrier((value,) + earlier)[0]


def together(*values):
    leaves, tree = jax.tree.flatten(values)
    return jax.tree.unflatten(tree, lax.optimization_barrier(leaves))


def assemble_kernel(rows, extra, where_ref, *refs):
    pieces, outs = refs[:10], refs[10:]
    z, y, x, c = where_ref[0], where_ref[1], where_ref[2], where_ref[3]
    depth = pieces[0].shape[1]
    for core_rel in range(2):
        own, by_x, by_y, diag0, diag1 = pieces[core_rel * 5 : core_rel * 5 + 5]
        core = c if core_rel == 0 else 1 - c
        for s in range(depth):
            zs = lax.rem(z - s + depth, depth)
            for xr in range(2):
                for yr in range(2):
                    xs = x if xr == 0 else 1 - x
                    ys = y if yr == 0 else 1 - y
                    dp = zs * 2 + ys
                    row = pl.ds(pl.multiple_of(dp * rows, rows), rows)
                    lane = pl.ds(pl.multiple_of(xs * (D // 2), D // 2), D // 2)
                    if xr and yr:
                        first, second = diag0[s], diag1[s]
                    else:
                        src = (own, by_x, by_y)[xr + 2 * yr]
                        first, second = src[0, s], src[1, s]
                    outs[0][core * 2, row, lane] = first[:rows]
                    outs[0][core * 2 + 1, row, lane] = second[:rows]
                    if extra:
                        share = pl.ds(pl.multiple_of((dp * 2 + core) * extra, extra), extra)
                        outs[1][share, lane] = first[rows:]
                        outs[2][dp, xs, core] = second[rows:]


def assemble(where, pieces, extra, dp_size):
    rows = D // dp_size
    outs = [sds((4, D, D), BF)]
    if extra:
        outs += [sds((dp_size * 2 * extra, D), BF), sds((dp_size, 2, 2, extra, D // 2), BF)]
    vmem = pl.BlockSpec(memory_space=pltpu.VMEM)
    return pl.pallas_call(
        functools.partial(assemble_kernel, rows, extra),
        in_specs=[pl.BlockSpec(memory_space=pltpu.SMEM)] + [vmem] * 10,
        out_specs=[vmem] * len(outs),
        out_shape=outs,
        compiler_params=params(16 * MIB),
        cost_estimate=pl.CostEstimate(flops=0, bytes_accessed=16 * D * D, transcendentals=0),
        name="assemble",
    )(where, *pieces)


def gather_z(place, u):
    return [u] + [place.over_z(u, s) for s in range(1, place.z_size)]


def gather_xy(place, parts):
    own = jnp.stack(parts, axis=1)
    return own, place.over_x(own), place.over_y(own)


def gather_diagonal(place, by_x, by_y):
    return place.over_y(by_x[0]), place.over_x(by_y[1])


def join(a, b):
    return (a.astype(F32) + b.astype(F32)).astype(BF)


class Reduction:
    def __init__(self, place):
        self.place = place

    def over_core(self, mine, other):
        zs = self.place.z_size
        got = self.place.core(other)
        h = join(mine, got)
        return h.reshape(zs, 2, h.shape[1], D)

    def pick_y(self, v, at):
        return lax.dynamic_index_in_dim(v, at, axis=v.ndim - 3, keepdims=False)

    def pick_x(self, v, at):
        return jnp.where(at == 0, v[..., : D // 2], v[..., D // 2 :])

    def send_y(self, v):
        y = self.place.y
        sent = self.pick_y(v, 1 - y)
        return self.pick_y(v, y), self.place.over_y(sent), sent

    def send_x(self, v):
        x = self.place.x
        sent = self.pick_x(v, 1 - x)
        return self.pick_x(v, x), self.place.over_x(sent), sent

    def send_z(self, v):
        zs, z = self.place.z_size, self.place.z
        parts = [lax.dynamic_index_in_dim(v, (z + s) % zs, axis=0, keepdims=False) for s in range(zs)]
        return parts[0], [self.place.over_z(parts[s], s) for s in range(1, zs)], parts

    def sum_z(self, kept, got):
        total = kept.astype(F32)
        for v in got:
            total = total + v.astype(F32)
        return total


def collect_kernel(where_ref, own, by_core, by_x, by_both, out, sem):
    x, c = where_ref[2], where_ref[3]
    grids = own.shape[0]
    copies = []
    for n, (piece, mp) in enumerate(
        ((own, 2 * x + c), (by_core, 2 * x + 1 - c), (by_x, 2 - 2 * x + c), (by_both, 3 - 2 * x - c))
    ):
        copies.append(pltpu.make_async_copy(piece, out.at[pl.ds(mp * grids, grids)], sem.at[n]))
    for copy in copies:
        copy.start()
    for copy in copies:
        copy.wait()


def start_grids(place, own):
    return own, place.core(own), place.over_x(own)


def finish_grids(place, where, pieces):
    own, by_core, by_x = pieces
    by_both = place.core(by_x)
    hbm = pl.BlockSpec(memory_space=pl.ANY)
    return pl.pallas_call(
        collect_kernel,
        in_specs=[pl.BlockSpec(memory_space=pltpu.SMEM)] + [hbm] * 4,
        out_specs=pl.BlockSpec(memory_space=pltpu.VMEM),
        out_shape=sds((4 * own.shape[0],) + own.shape[1:], own.dtype),
        scratch_shapes=[pltpu.SemaphoreType.DMA((4,))],
        compiler_params=params(12 * MIB),
        cost_estimate=pl.CostEstimate(flops=0, bytes_accessed=8 * own.size, transcendentals=0),
        name="collect",
    )(where, own, by_core, by_x, by_both)


def sum_plane(place, value):
    value = value + place.core(value)
    value = (value + place.over_x(value)) + (place.over_y(value) + place.over_corner(value))
    return [value] + [place.over_z(value, s) for s in range(1, place.z_size)]


ROWS1, ROWS2, ROWS3 = 4 * HALF, 5 * HALF, 3 * HALF
ROWS = ROWS1 + ROWS2 + ROWS3


def totals_kernel(where, *refs):
    keep1, got1, keep2, *got2 = refs[:6]
    keep3, *got3 = refs[6:10]
    kept_ref, sent_ref, tail_ref, square_ref = refs[10:]
    x, c = where[2], where[3]

    def total(first, others):
        value = first[...].astype(F32)
        for ref in others:
            value = value + ref[...].astype(F32)
        return value

    whole3 = total(keep3, got3)
    parts = (total(keep1, [got1]), total(keep2, got2), whole3[:ROWS3])
    wide = D // 4
    row = 0
    square = jnp.zeros((1, D // 2), F32)
    for value in parts:
        rows = slice(row, row + value.shape[0])
        left, right = value[:, :wide], value[:, wide:]

        @pl.when(c == 0)
        def _():
            kept_ref[rows, :] = left
            sent_ref[rows, :] = right

        @pl.when(c != 0)
        def _():
            kept_ref[rows, :] = right
            sent_ref[rows, :] = left

        square = square + jnp.sum(value * value, axis=0, keepdims=True)
        row += value.shape[0]
    tail = whole3[ROWS3:]
    tail_ref[...] = tail
    lane = lax.broadcasted_iota(jnp.int32, (16, D // 2), 1)
    line = lax.broadcasted_iota(jnp.int32, (16, D // 2), 0)
    owner = jnp.where((x == 0) & (c == 0), 1.0, 0.0)
    codes = tail[16:32]
    small = jnp.where(line < 8, jnp.where(lane < D // OWNERS, codes * owner, 0.0), 0.0)
    small = jnp.where((line >= 8) & (lane < D // (4 * OWNERS)), codes, small)
    square = square + jnp.sum(tail[:16] * tail[:16] + small * small, axis=0, keepdims=True)
    square_ref[...] = jnp.full((8, 128), jnp.sum(square), F32)


def totals(where, keep1, got1, keep2, got2, keep3, got3):
    vmem = pl.BlockSpec(memory_space=pltpu.VMEM)
    ins = [keep1, got1, keep2, *got2, keep3, *got3]
    return pl.pallas_call(
        totals_kernel,
        in_specs=[pl.BlockSpec(memory_space=pltpu.SMEM)] + [vmem] * len(ins),
        out_specs=[vmem] * 4,
        out_shape=[
            sds((ROWS, D // 4), F32), sds((ROWS, D // 4), F32), sds((SMALL, D // 2), F32),
            sds((8, 128), F32),
        ],
        compiler_params=params(16 * MIB),
        name="totals",
    )(where, *ins)


def update_kernel(where, *refs):
    kept, got, tail, t_core, t_x, t_both = refs[:6]
    squares = refs[6:10]
    state, outs = refs[10:25], refs[25:]
    x, c = where[2], where[3]
    square = (squares[0][0:1, 0:1] + squares[2][0:1, 0:1]) + (
        squares[1][0:1, 0:1] + squares[3][0:1, 0:1]
    )
    norm = jnp.sqrt(square)
    factor = jnp.minimum(1.0, CLIP_LIMIT / (norm + 1e-06))
    outs[0][...] = norm

    def step(at, index, gradient, rate, decay):
        weight, first, second = (state[at + 5 * i][index] for i in range(3))
        new = adam_step(weight, gradient, first, second, rate, decay)
        for i in range(3):
            outs[1 + at + 5 * i][index] = new[i]

    def block(row):
        rows = slice(row, row + HALF)
        own, other = kept[rows, :], got[rows, :]
        top = jnp.where(c == 0, own, other)
        bottom = jnp.where(c == 0, other, own)
        return jnp.concatenate([top, bottom], axis=0) * factor

    front = [ROWS1 + ROWS2 + HALF * b for b in range(3)] + [ROWS1 + HALF * b for b in range(4)]
    for b, row in enumerate(front):
        step(0, b, block(row), RATE_MATRIX, DECAY_RATE)
    back = [ROWS1 + 4 * HALF] + [HALF * b for b in range(4)]
    for b, row in enumerate(back):
        step(1, b, block(row).T, RATE_MATRIX, DECAY_RATE)
    norm_grad = tail[16:22, : D // OWNERS] * factor
    outs[16][...] = norm_grad
    step(3, Ellipsis, norm_grad, RATE_VECTOR, 0.0)
    step(2, Ellipsis, tail[24:30, : D // (4 * OWNERS)] * factor, RATE_VECTOR, 0.0)
    own, by_core, by_x, by_both = tail[0:16, :], t_core[...], t_x[...], t_both[...]
    here = jnp.concatenate(
        [jnp.where(c == 0, own, by_core), jnp.where(c == 0, by_core, own)], axis=0
    )
    there = jnp.concatenate(
        [jnp.where(c == 0, by_x, by_both), jnp.where(c == 0, by_both, by_x)], axis=0
    )
    side = D // 2
    for half in range(2):
        gradient = jnp.where(x == half, here, there) * factor
        lanes = (slice(None), slice(half * side, (half + 1) * side))
        step(4, lanes, gradient, RATE_TABLE, DECAY_RATE)


def update(where, kept, got, tail, t_core, t_x, t_both, squares, state):
    vmem = pl.BlockSpec(memory_space=pltpu.VMEM)
    ins = [kept, got, tail, t_core, t_x, t_both, *squares, *state]
    shapes = [sds((1, 1), F32)] + [sds(v.shape, F32) for v in state] + [sds(state[3].shape, F32)]
    return pl.pallas_call(
        update_kernel,
        in_specs=[pl.BlockSpec(memory_space=pltpu.SMEM)] + [vmem] * len(ins),
        out_specs=[vmem] * len(shapes),
        out_shape=shapes,
        compiler_params=params(24 * MIB),
        name="update",
    )(where, *ins)


def adam_step(weight, gradient, first, second, rate, decay):
    first_new = BETA_FIRST * first + (1.0 - BETA_FIRST) * gradient
    second_new = BETA_SECOND * second + (1.0 - BETA_SECOND) * gradient * gradient
    first_hat = first_new / (1.0 - BETA_FIRST**STEP)
    second_hat = second_new / (1.0 - BETA_SECOND**STEP)
    weight_new = weight - rate * (first_hat / (jnp.sqrt(second_hat) + ADAM_EPS) + decay * weight)
    return (weight_new, first_new, second_new)


def body(
    dp_size, mp_size,
    block_input, cotangent, crop_boxes, front_weights, back_weights, split_biases, norm_params,
    pos_table, front_first, back_weight_first_moment, split_first, norm_first, table_first,
    front_second, back_second, split_second, norm_second, table_second,
):
    place = Place(dp_size, mp_size)
    direct = dp_size == 8 and mp_size == 4
    x, y, z, c = place.x, place.y, place.z, place.c
    grids = block_input.shape[0] // mp_size
    scal = jnp.stack([place.mp * grids, c, place.mp, place.dp]).astype(jnp.int32)
    where = jnp.stack([z, y, x, c]).astype(jnp.int32)
    turned = jnp.swapaxes(back_weights, 1, 2).astype(BF)
    low_front = front_weights.astype(BF)
    rows, lanes = low_front.shape[1], low_front.shape[2]

    if direct:
        shards = jnp.concatenate([low_front[:3], turned[:1], low_front[3:], turned[1:]])
        shards = shards.reshape(3, 2, 2, rows, lanes)
        mine = lax.dynamic_index_in_dim(shards, c, axis=1, keepdims=False)
        sent = lax.dynamic_index_in_dim(shards, 1 - c, axis=1, keepdims=False)
        got = place.core(sent)
        units = jnp.where(
            c == 0, jnp.concatenate([mine, got], -1), jnp.concatenate([got, mine], -1)
        )
        extra = pos_table.shape[0] // 2
        half = jnp.where(c == 0, pos_table[:extra], pos_table[extra:]).astype(BF)
        half = jnp.where(x == 0, half[:, : D // 2], half[:, D // 2 :])
        packed = jnp.zeros((extra, D // 2), BF)
        packed = lax.dynamic_update_slice(packed, norm_params.astype(BF), (0, 0))
        packed = lax.dynamic_update_slice(packed, split_biases.astype(BF), (0, 128))
        first_unit = jnp.concatenate([units[0], jnp.stack([half, packed])], axis=1)
        parts1 = gather_z(place, first_unit)
        parts1, unit2 = together(parts1, units[1])
        own1 = gather_xy(place, parts1)
        parts2 = gather_z(place, unit2)
        own1 = list(together(*own1))
        diag1 = gather_diagonal(place, own1[1], own1[2])
        far1 = [place.core(v) for v in own1]
        diag1, far1, parts2, unit3 = together(diag1, far1, parts2, units[2])
        own2 = list(gather_xy(place, parts2))
        parts3 = gather_z(place, unit3)
        far1 += [place.core(v) for v in diag1]
        w_attn, table, codes = assemble(where, [*own1, *diag1, *far1], extra, dp_size)
        norms = jnp.swapaxes(codes[:, 0, 0, 0:6, : norm_params.shape[1]], 0, 1).reshape(6, D)
        splits = codes[:, :, :, 0:6, 128 : 128 + split_biases.shape[1]]
        splits = jnp.transpose(splits, (3, 1, 2, 0, 4)).reshape(6, D)
    else:

        def whole(v):
            v = lax.all_gather(v, "dp", axis=1, tiled=True)
            return lax.all_gather(v, "mp", axis=2, tiled=True)

        w_attn = whole(jnp.concatenate([low_front[:3], turned[:1]]))
        w_up, w_down = whole(low_front[3:]), whole(turned[1:])
        table = lax.all_gather(pos_table.astype(BF), "dp", axis=0, tiled=True)
        norms = lax.all_gather(norm_params.astype(BF), "dp", axis=1, tiled=True)
        splits = lax.all_gather(split_biases.astype(BF), ("mp", "dp"), axis=1, tiled=True)
    gap = jnp.zeros((2, D), F32)
    vec = jnp.concatenate([norms.astype(F32), gap, splits.astype(F32), gap])

    cells_here, norm_here = pos_table.shape[0], norm_params.shape[1]
    split_here = split_biases.shape[1]
    if direct:
        w_attn, own2[0], parts3[0] = together(w_attn, own2[0], parts3[0])
    fwd = attention_forward(scal, crop_boxes, block_input, table, w_attn, vec, grids)
    if direct:
        fwd, own2, parts3 = together(fwd, own2, parts3)
        diag2 = gather_diagonal(place, own2[1], own2[2])
        own3 = list(gather_xy(place, parts3))
        far2 = [place.core(v) for v in own2]
        diag2, far2, own3[0] = together(diag2, far2, own3[0])
        far2 += [place.core(v) for v in diag2]
        (w_up,) = assemble(where, [*own2, *diag2, *far2], 0, dp_size)
    emb, n1, q, k, v, p, mixed, after, n2 = fwd
    up = up_forward(scal, n2, w_up, vec, cotangent, grids)
    if direct:
        red = Reduction(place)
        up, own3 = together(up, own3)
        hidden, gp, down_mine, down_other = up
        diag3 = gather_diagonal(place, own3[1], own3[2])
        far3 = [place.core(v) for v in own3]
        h1 = red.over_core(down_mine, down_other)
        diag3, far3, h1 = together(diag3, far3, h1)
        far3 += [place.core(v) for v in diag3]
        keep1, got1, sent1 = red.send_y(h1)
        (w_down,) = assemble(where, [*own3, *diag3, *far3], 0, dp_size)
        w_down, sent1 = together(w_down, sent1)
        out = down_forward(hidden, w_down, after, vec, grids)
        gp, out = together(gp, out)
        out_pieces = start_grids(place, out)
        back = mlp_backward(scal, gp, w_down, w_up, n2, cotangent, after, vec, mixed, grids)
        back, got1, out_pieces = together(back, got1, out_pieces)
        ga, galow, up_mine, up_other, gb, gn = back
        keep1, got1, sent1 = red.send_z(join(keep1, got1))
        h2 = red.over_core(up_mine, up_other)
        cut = h2.shape[2] // 2
        keep2a, got2a, sent2a = red.send_y(h2[:, :, :cut])
        keep2b, got2b, sent2b = red.send_x(h2[:, :, cut:])
        galow, sent1, sent2a, sent2b = together(galow, sent1, sent2a, sent2b)
        back = attention_backward(
            scal, crop_boxes, ga, galow, mixed, p, q, k, v, emb, n1, w_attn, vec, gn, gb, grids
        )
        back, got1, got2a, got2b = together(back, got1, got2a, got2b)
        ig, dtable, gs, mine3, other3 = back
        h3 = red.over_core(mine3, other3)
        keep1, got1, _ = red.send_x(red.sum_z(keep1, got1).astype(BF))
        keep2a, got2a, _ = red.send_x(join(keep2a, got2a))
        keep2b, got2b, _ = red.send_y(join(keep2b, got2b))
        cut = h3.shape[2] // 2
        keep3a, got3a, _ = red.send_y(h3[:, :, :cut])
        keep3b, got3b, _ = red.send_x(h3[:, :, cut:])
        keep3a, keep3b, got1, got2a, got2b = together(keep3a, keep3b, got1, got2a, got2b)
        h2 = jnp.concatenate([join(keep2a, got2a), join(keep2b, got2b)], axis=1)
        keep2, got2, _ = red.send_z(h2)
        keep3a, got3a, got3b = together(keep3a, got3a, got3b)
        keep3a, got3a, _ = red.send_x(join(keep3a, got3a))
        keep3b, got3b, _ = red.send_y(join(keep3b, got3b))
        got3a, got3b, got2 = together(got3a, got3b, got2)
        h3 = jnp.concatenate([join(keep3a, got3a), join(keep3b, got3b)], axis=1)
        keep3, got3, _ = red.send_z(h3)
        ig, keep3 = together(ig, keep3)
        ig_pieces = start_grids(place, ig)
        block_output = finish_grids(place, where, out_pieces)
        got3, block_output = together(got3, block_output)
        kept, sent, tail, square = totals(where, keep1, got1, keep2, got2, keep3, got3)
        squares = sum_plane(place, square)
        got = place.core(sent)
        t_own = tail[:16]
        t_x = place.over_x(t_own)
        t_core, t_both = place.core(t_own), place.core(t_x)
        ig_pieces, t_x = together(ig_pieces, t_x)
        input_grad = finish_grids(place, where, ig_pieces)
        squares, input_grad = together(squares, input_grad)
        state = (
            front_weights, back_weights, split_biases, norm_params, pos_table,
            front_first, back_weight_first_moment, split_first, norm_first, table_first,
            front_second, back_second, split_second, norm_second, table_second,
        )
        new = update(where, kept, got, tail, t_core, t_x, t_both, squares, state)
        return (block_output, input_grad, new[0][0, 0], *new[1:])
    else:
        hidden, gp, down_mine, down_other = up
        out = down_forward(hidden, w_down, after, vec, grids)
        ga, galow, up_mine, up_other, gb, gn = mlp_backward(
            scal, gp, w_down, w_up, n2, cotangent, after, vec, mixed, grids
        )
        ig, dtable, gs, mine3, other3 = attention_backward(
            scal, crop_boxes, ga, galow, mixed, p, q, k, v, emb, n1, w_attn, vec, gn, gb, grids
        )

        def share(mine, other, blocks):
            low, high = jnp.where(c == 0, mine, other), jnp.where(c == 0, other, mine)
            full = jnp.stack([low, high], 1)[:, :, : blocks * HALF].astype(F32)
            full = full.reshape(OWNERS, 2, blocks, HALF, D)
            full = jnp.transpose(full, (2, 0, 1, 3, 4)).reshape(blocks, D, D)
            full = lax.psum_scatter(full, "dp", scatter_dimension=1, tiled=True)
            return lax.psum_scatter(full, "mp", scatter_dimension=2, tiled=True)

        down_share = share(down_mine, down_other, 4)
        up_share = share(up_mine, up_other, 5)
        out_share, up_share = up_share[4:], up_share[:4]
        qkv_share = share(mine3, other3, 3)
        block_output = lax.all_gather(out, "mp", axis=0, tiled=True)
        input_grad = lax.all_gather(ig, "mp", axis=0, tiled=True)
        norm_grad = jnp.concatenate([gs[2:4], gn[2:6]])
        split_grad = jnp.concatenate([gs[0:2], gb[0:4]])
        dtable = lax.psum(dtable, ("dp", "mp"))
        norm_grad = lax.psum(norm_grad, ("dp", "mp"))
        split_grad = lax.psum(split_grad, ("dp", "mp"))
        table_share = lax.dynamic_slice(dtable, (place.dp * cells_here, 0), (cells_here, D))
        norm_share = lax.dynamic_slice(norm_grad, (0, place.dp * norm_here), (6, norm_here))
        split_share = lax.dynamic_slice(
            split_grad, (0, (place.mp * dp_size + place.dp) * split_here), (6, split_here)
        )
        table_square = jnp.sum(table_share * table_share) / mp_size
    front_share = jnp.concatenate([qkv_share, up_share])
    back_share = jnp.concatenate([out_share, down_share])
    owner = (place.mp == 0).astype(F32)
    square = (
        jnp.sum(qkv_share * qkv_share)
        + jnp.sum(out_share * out_share)
        + jnp.sum(up_share * up_share)
        + jnp.sum(down_share * down_share)
        + jnp.sum(split_share * split_share)
        + owner * jnp.sum(norm_share * norm_share)
        + table_square
    )
    clip_norm = jnp.sqrt(lax.psum(square, ("dp", "mp")))
    factor = jnp.minimum(1.0, CLIP_LIMIT / (clip_norm + 1e-06))
    norm_clipped = norm_share * factor
    new_front, front_first_new, front_second_new = adam_step(
        front_weights, front_share * factor, front_first, front_second, RATE_MATRIX, DECAY_RATE
    )
    new_back, back_first_new, back_second_new = adam_step(
        back_weights,
        jnp.swapaxes(back_share, 1, 2) * factor,
        back_weight_first_moment,
        back_second,
        RATE_MATRIX,
        DECAY_RATE,
    )
    new_split, split_first_new, split_second_new = adam_step(
        split_biases, split_share * factor, split_first, split_second, RATE_VECTOR, 0.0
    )
    new_norm, norm_first_new, norm_second_new = adam_step(
        norm_params, norm_clipped, norm_first, norm_second, RATE_VECTOR, 0.0
    )
    new_table, table_first_new, table_second_new = adam_step(
        pos_table, table_share * factor, table_first, table_second, RATE_TABLE, DECAY_RATE
    )
    return (
        block_output, input_grad, clip_norm,
        new_front, new_back, new_split, new_norm, new_table,
        front_first_new, back_first_new, split_first_new, norm_first_new, table_first_new,
        front_second_new, back_second_new, split_second_new, norm_second_new, table_second_new,
        norm_clipped,
    )


def solution(mesh):
    front, back = P(None, "dp", "mp"), P(None, "mp", "dp")
    split, norm, table = P(None, ("mp", "dp")), P(None, "dp"), P("dp", None)
    state = (front, back, split, norm, table)
    rows = P("dp", None, None)
    return jax.shard_map(
        functools.partial(body, mesh.shape["dp"], mesh.shape["mp"]),
        mesh=mesh,
        in_specs=(rows, rows, P("dp", None)) + state * 3,
        out_specs=(rows, rows, P()) + state * 3 + (norm,),
        check_vma=False,
    )
```

```python
import functools

import jax
import jax.numpy as jnp
from jax import lax
from jax.experimental import pallas as pl
from jax.experimental.pallas import tpu as pltpu
from jax.sharding import PartitionSpec as P

D = 768
HEADS = 16
HEAD = D // HEADS
SIDE = 16
CELLS = 256
STEP = 5
CORES = 2

NORM_EPS = 1e-05
BETA_FIRST = 0.9
BETA_SECOND = 0.95
ADAM_EPS = 1e-08
RATE_MATRIX = 0.05
RATE_TABLE = 0.2
RATE_VECTOR = 0.5
DECAY_RATE = 0.1
CLIP_LIMIT = 0.01
MASK_FILL = -1e30
SCALE = HEAD ** (-0.5)
LOG2E = 1.4426950408889634
INV_SQRT_2PI = 0.3989422804014327

OWNERS = 8
HALF = D // (2 * OWNERS)
SMALL = 32

BF = jnp.bfloat16
F32 = jnp.float32
MIB = 1024 * 1024
NN = (((1,), (0,)), ((), ()))
NT = (((1,), (1,)), ((), ()))
TN = (((0,), (0,)), ((), ()))


NO_COST = pl.CostEstimate(flops=0, bytes_accessed=0, transcendentals=0)


def dot(a, b, dims=NN):
    return lax.dot_general(a, b, dims, preferred_element_type=F32)


def params(limit):
    return pltpu.CompilerParams(vmem_limit_bytes=limit)


def norm_stats(v):
    mean = jnp.mean(v, axis=-1, keepdims=True)
    centred = v - mean
    spread = jnp.mean(centred * centred, axis=-1, keepdims=True)
    rstd = lax.rsqrt(spread + NORM_EPS)
    return centred * rstd, rstd


def norm_back(c, gain, u, rstd):
    cg = c * gain
    mean_cg = jnp.mean(cg, axis=-1, keepdims=True)
    mean_cgu = jnp.mean(cg * u, axis=-1, keepdims=True)
    return rstd * (cg - mean_cg - u * mean_cgu)


def head_window(h):
    low = h * HEAD
    first = low // 128
    last = (low + HEAD - 1) // 128
    return first, last + 1 - first


def head_mask(h):
    first, tiles = head_window(h)
    lane = lax.broadcasted_iota(jnp.int32, (1, tiles * 128), 1) + first * 128
    return (lane >= h * HEAD) & (lane < (h + 1) * HEAD)


def crop_target(position, height, breadth, top, left):
    row = (position >> 4) - top
    col = (position & (SIDE - 1)) - left
    inside = (row >= 0) & (row < height) & (col >= 0) & (col < breadth)
    return jnp.where(inside, row * breadth + col, -1)


def load_weights(core, mine_ref, other_ref, w_ref, copy_ref, sem, token_ref):
    copy = pltpu.make_async_copy(w_ref, copy_ref, sem)

    @pl.when(pl.program_id(0) == 0)
    def _():
        token_ref[...] = jnp.zeros_like(token_ref)

        def fill(low, high):
            for b in range(2):
                rows = slice(b * D, (b + 1) * D)
                w_ref[b] = low[rows, :]
                w_ref[2 + b] = high[rows, :]

        @pl.when(core == 0)
        def _():
            fill(mine_ref, other_ref)

        @pl.when(core != 0)
        def _():
            fill(other_ref, mine_ref)

        copy.start()

    @pl.when(pl.program_id(0) == pl.num_programs(0) - 1)
    def _():
        copy.wait()


def attention_forward_kernel(
    scal, crop, x_ref, mine_ref, other_ref,
    emb_ref, n1_ref, q_ref, k_ref, v_ref, p_ref, mixed_ref, after_ref, n2_ref, wcopy_ref, vec_ref, token_ref,
    w_ref, table_ref, sem,
):
    load_weights(scal[1], mine_ref, other_ref, w_ref, wcopy_ref, sem, token_ref)
    part = CELLS // (2 * OWNERS)

    @pl.when(pl.program_id(0) == 0)
    def _():
        for at, ref in ((scal[1], mine_ref), (1 - scal[1], other_ref)):
            for dp in range(OWNERS):
                row = pl.ds(pl.multiple_of((2 * dp + at) * part, part), part)
                table_ref[row, :] = ref[2 * D + dp * part : 2 * D + (dp + 1) * part, :]
        vec_ref[...] = jnp.zeros_like(vec_ref)
        wide, thin = D // OWNERS, D // (4 * OWNERS)
        first = 2 * D + CELLS // 2

        def unpack(ref, core):
            for dp in range(OWNERS):
                rows = slice(first + dp * part, first + dp * part + 6)
                if core == 0:
                    vec_ref[0:6, dp * wide : (dp + 1) * wide] = ref[rows, 0:wide].astype(F32)
                for x in range(2):
                    lane = x * (D // 2) + 128
                    at = (2 * x + core) * (D // 4) + dp * thin
                    vec_ref[8:14, at : at + thin] = ref[rows, lane : lane + thin].astype(F32)

        @pl.when(scal[1] == 0)
        def _():
            unpack(mine_ref, 0)
            unpack(other_ref, 1)

        @pl.when(scal[1] != 0)
        def _():
            unpack(other_ref, 0)
            unpack(mine_ref, 1)

    grid = scal[0] + pl.program_id(0)
    height, breadth, top, left = crop[grid, 0], crop[grid, 1], crop[grid, 2], crop[grid, 3]
    target = crop_target(
        lax.broadcasted_iota(jnp.int32, (1, CELLS), 1), height, breadth, top, left
    )
    cell = lax.broadcasted_iota(jnp.int32, (CELLS, CELLS), 0)
    onehot = jnp.where(cell == target, 1.0, 0.0).astype(BF)
    emb = x_ref[0].astype(F32) + dot(onehot, table_ref[...])
    emb_ref[...] = emb
    u, _ = norm_stats(emb)
    n1 = (u * vec_ref[0:1, :] + vec_ref[1:2, :]).astype(BF)
    n1_ref[...] = n1
    q_ref[...] = (dot(n1, w_ref[0]) + vec_ref[8:9, :]).astype(BF)
    k_ref[...] = dot(n1, w_ref[1]).astype(BF)
    v_ref[...] = (dot(n1, w_ref[2]) + vec_ref[9:10, :]).astype(BF)
    valid = lax.broadcasted_iota(jnp.int32, (1, CELLS), 1) < height * breadth
    tiles_out = [None] * (D // 128)
    for h in range(HEADS):
        first, tiles = head_window(h)
        lanes = slice(first * 128, (first + tiles) * 128)
        mask = head_mask(h)
        qh = jnp.where(mask, q_ref[:, lanes], 0).astype(BF)
        vh = jnp.where(mask, v_ref[:, lanes], 0).astype(BF)
        s = jnp.where(valid, dot(qh, k_ref[:, lanes], NT), MASK_FILL)
        top_score = jnp.max(s, axis=-1, keepdims=True)
        e = jnp.exp2((s - top_score) * (SCALE * LOG2E))
        p = (e * (1.0 / jnp.sum(e, axis=-1, keepdims=True))).astype(BF)
        p_ref[0, h] = p
        o = dot(p, vh)
        for t in range(tiles):
            part = o[:, t * 128 : (t + 1) * 128]
            at = first + t
            tiles_out[at] = part if tiles_out[at] is None else tiles_out[at] + part
    for t in range(D // 128):
        mixed_ref[:, t * 128 : (t + 1) * 128] = tiles_out[t].astype(BF)
    attention = dot(mixed_ref[...], w_ref[3], NT)
    after = emb_ref[...] + attention + vec_ref[2:3, :]
    after_ref[...] = after
    u2, _ = norm_stats(after)
    n2_ref[...] = (u2 * vec_ref[3:4, :] + vec_ref[4:5, :]).astype(BF)


def up_kernel(
    scal, n2_ref, low_ref, high_ref, vec_ref, g_ref,
    hidden_ref, gp_ref, mine_ref, other_ref, wcopy_ref, token_ref, gt_ref, w_ref, sem,
):
    j = pl.program_id(0)
    load_weights(scal[1], low_ref, high_ref, w_ref, wcopy_ref, sem, token_ref)
    grids = g_ref.shape[0]

    @pl.when(j == 0)
    def _():
        for n in range(grids):
            gt_ref[:, n * CELLS : (n + 1) * CELLS] = g_ref[n].T

    bias = vec_ref[pl.ds(10 + j, 1), :]
    for n in range(grids):
        rows = slice(n * CELLS, (n + 1) * CELLS)
        pre = dot(n2_ref[rows, :], w_ref[j]) + bias
        phi = 0.5 + 0.5 * lax.erf(pre * (0.5**0.5))
        density = jnp.exp2(pre * pre * (-0.5 * LOG2E)) * INV_SQRT_2PI
        hidden_ref[0, rows, :] = (pre * phi).astype(BF)
        gp_ref[0, rows, :] = (phi + pre * density).astype(BF)
    grad = dot(gt_ref[...], hidden_ref[0]).astype(BF)
    keep(scal[1], 0, grad, mine_ref, other_ref)


def keep(core, at, grad, mine_ref, other_ref):
    parts = grad.reshape(OWNERS, 2, HALF, D)
    rows = slice(at * HALF, (at + 1) * HALF)

    @pl.when(core == 0)
    def _():
        mine_ref[:, rows, :] = parts[:, 0]
        other_ref[:, rows, :] = parts[:, 1]

    @pl.when(core != 0)
    def _():
        mine_ref[:, rows, :] = parts[:, 1]
        other_ref[:, rows, :] = parts[:, 0]


def down_kernel(
    scal, hidden_ref, low_ref, high_ref, after_ref, vec_ref, out_ref, wcopy_ref, token_ref, down_ref, sem
):
    load_weights(scal[1], low_ref, high_ref, down_ref, wcopy_ref, sem, token_ref)
    total = dot(hidden_ref[0], down_ref[0], NT)
    for j in range(1, 4):
        total = total + dot(hidden_ref[j], down_ref[j], NT)
    out_ref[0] = (after_ref[...] + total + vec_ref[5:6, :]).astype(BF)


def mlp_kernel(
    scal, gp_ref, down_ref, up_ref, n2_ref, g_ref, after_any, vec_ref, mixed_any,
    ga_ref, galow_ref, mine_ref, other_ref, gb_ref, gn_ref, token_ref,
    dn2_acc, n2t_ref, gpre_ref, after_ref, mixed_ref, sem,
):
    j = pl.program_id(0)
    grids = g_ref.shape[0]
    core = scal[1]
    late = (
        pltpu.make_async_copy(after_any, after_ref, sem.at[0]),
        pltpu.make_async_copy(mixed_any, mixed_ref, sem.at[1]),
    )

    @pl.when(j == 0)
    def _():
        for copy in late:
            copy.start()
        for n in range(grids):
            rows = slice(n * CELLS, (n + 1) * CELLS)
            n2t_ref[:, rows] = n2_ref[rows, :].T
        gb_ref[...] = jnp.zeros_like(gb_ref)
        gn_ref[...] = jnp.zeros_like(gn_ref)
        token_ref[...] = jnp.zeros_like(token_ref)

    @pl.when(j < 4)
    def _():
        colsum = jnp.zeros((1, D), F32)
        for n in range(grids):
            rows = slice(n * CELLS, (n + 1) * CELLS)
            gh = dot(g_ref[n], down_ref[0])
            gpre = (gh * gp_ref[0, rows, :].astype(F32)).astype(BF)
            gpre_ref[rows, :] = gpre
            colsum = colsum + jnp.sum(gpre.astype(F32), axis=0, keepdims=True)
            part = dot(gpre, up_ref[0], NT)

            @pl.when(j == 0)
            def _():
                dn2_acc[rows, :] = part

            @pl.when(j > 0)
            def _():
                dn2_acc[rows, :] += part

        gb_ref[pl.ds(j, 1), :] = colsum
        keep(core, 0, dot(n2t_ref[...], gpre_ref[...]).astype(BF), mine_ref, other_ref)

    @pl.when(j == 4)
    def _():
        for copy in late:
            copy.wait()
        sums = [jnp.zeros((1, D), F32)] * 4
        for n in range(grids):
            rows = slice(n * CELLS, (n + 1) * CELLS)
            u, rstd = norm_stats(after_ref[rows, :])
            c = dn2_acc[rows, :]
            g = g_ref[n].astype(F32)
            ga = g + norm_back(c, vec_ref[3:4, :], u, rstd)
            ga_ref[rows, :] = ga
            galow = ga.astype(BF)
            galow_ref[rows, :] = galow
            n2t_ref[:, rows] = galow.T
            parts = (ga, c * u, c, g)
            sums = [s + jnp.sum(v, axis=0, keepdims=True) for s, v in zip(sums, parts)]
        for i in range(4):
            gn_ref[2 + i : 3 + i, :] = sums[i]
        keep(core, 0, dot(n2t_ref[...], mixed_ref[...]).astype(BF), mine_ref, other_ref)


def attention_backward_kernel(
    scal, crop, ga_ref, galow_ref, mixed_ref, p_ref, q_ref, k_ref, v_ref, emb_ref, n1_ref,
    w_ref, vec_ref, gn_ref, gb_ref,
    ig_ref, table_out, gs_out, mine_ref, other_ref, token_ref,
    dm_ref, dq_all, dk_all, dv_all, n1t_ref, table_ref, gs_ref,
):
    i = pl.program_id(0)
    grids = pl.num_programs(0) - 1
    core = scal[1]

    @pl.when(i == 0)
    def _():
        table_ref[...] = jnp.zeros_like(table_ref)
        gs_ref[...] = jnp.zeros_like(gs_ref)
        token_ref[...] = jnp.zeros_like(token_ref)

    @pl.when(i < grids)
    def _():
        grid = scal[0] + i
        height, breadth, top, left = crop[grid, 0], crop[grid, 1], crop[grid, 2], crop[grid, 3]
        here = pl.ds(pl.multiple_of(i * CELLS, CELLS), CELLS)
        n1t_ref[:, here] = n1_ref[...].T
        dm_ref[...] = dot(galow_ref[...], w_ref[3]).astype(BF)
        outs = [[None] * (D // 128) for _ in range(3)]
        for h in range(HEADS):
            first, tiles = head_window(h)
            lanes = slice(first * 128, (first + tiles) * 128)
            mask = head_mask(h)
            qh = jnp.where(mask, q_ref[:, lanes], 0).astype(BF)
            kh = jnp.where(mask, k_ref[:, lanes], 0).astype(BF)
            dmh = jnp.where(mask, dm_ref[:, lanes], 0).astype(BF)
            p = p_ref[0, h]
            dp = dot(dmh, v_ref[:, lanes], NT)
            delta = jnp.sum(
                dmh.astype(F32) * mixed_ref[:, lanes].astype(F32), axis=-1, keepdims=True
            )
            ds = (p.astype(F32) * (dp - delta)).astype(BF)
            got = (dot(ds, kh), dot(ds, qh, TN), dot(p, dmh, TN))
            for o in range(3):
                for t in range(tiles):
                    part = got[o][:, t * 128 : (t + 1) * 128]
                    at = first + t
                    outs[o][at] = part if outs[o][at] is None else outs[o][at] + part
        for t in range(D // 128):
            lanes = slice(t * 128, (t + 1) * 128)
            dq_all[here, lanes] = (outs[0][t] * SCALE).astype(BF)
            dk_all[here, lanes] = (outs[1][t] * SCALE).astype(BF)
            dv_all[here, lanes] = outs[2][t].astype(BF)
        dq, dk, dv = dq_all[here, :], dk_all[here, :], dv_all[here, :]
        c = dot(dq, w_ref[0], NT) + dot(dk, w_ref[1], NT) + dot(dv, w_ref[2], NT)
        u, rstd = norm_stats(emb_ref[...])
        ge = ga_ref[...] + norm_back(c, vec_ref[0:1, :], u, rstd)
        high = ge.astype(BF)
        ig_ref[0] = high
        low = (ge - high.astype(F32)).astype(BF)
        target = crop_target(
            lax.broadcasted_iota(jnp.int32, (CELLS, 1), 0), height, breadth, top, left
        )
        cell = lax.broadcasted_iota(jnp.int32, (CELLS, CELLS), 1)
        onehot = jnp.where(cell == target, 1.0, 0.0).astype(BF)
        table_ref[...] += dot(onehot, high) + dot(onehot, low)
        for row, v in enumerate((dq.astype(F32), dv.astype(F32), c * u, c)):
            gs_ref[row : row + 1, :] += jnp.sum(v, axis=0, keepdims=True)

    @pl.when(i == grids)
    def _():
        for b, ref in enumerate((dq_all, dk_all, dv_all)):
            keep(core, b, dot(n1t_ref[...], ref[...]).astype(BF), mine_ref, other_ref)
        table_out[...] = table_ref[...]
        gs_out[...] = gs_ref[...]
        start = 3 * HALF
        table = table_ref[...].astype(BF).reshape(OWNERS, 2, 16, D)
        norm = jnp.concatenate([gs_ref[2:4, :], gn_ref[2:6, :]], axis=0).astype(BF)
        split = jnp.concatenate([gs_ref[0:2, :], gb_ref[0:4, :]], axis=0).astype(BF)
        wide, thin = D // OWNERS, D // (4 * OWNERS)
        side = D // 2

        def small(ref, half):
            ref[:, start : start + 16, :] = table[:, half]
            ref[:, start + 16 : start + 32, :] = jnp.zeros((OWNERS, 16, D), BF)
            for dp in range(OWNERS):
                for x in range(2):
                    lane = x * side
                    ref[dp, start + 16 : start + 22, lane : lane + wide] = norm[
                        :, dp * wide : (dp + 1) * wide
                    ]
                    at = (2 * x + half) * (D // 4) + dp * thin
                    ref[dp, start + 24 : start + 30, lane : lane + thin] = split[:, at : at + thin]

        @pl.when(core == 0)
        def _():
            small(mine_ref, 0)
            small(other_ref, 1)

        @pl.when(core != 0)
        def _():
            small(mine_ref, 1)
            small(other_ref, 0)


def sds(shape, dtype):
    return jax.ShapeDtypeStruct(shape, dtype)


TOKEN = sds((8, 128), F32)


def in_hbm(shape):
    return pltpu.HBM(shape.shape, shape.dtype)


def behind(value, token):
    return lax.optimization_barrier((value, token))


ANY = pl.BlockSpec(memory_space=pl.ANY)


def half_shape(blocks, extra=0):
    return sds((OWNERS, blocks * HALF + extra, D), BF)


def whole_block(shape, buffers=None):
    zeros = (0,) * len(shape)
    mode = None if buffers is None else pl.Buffered(buffers)
    return pl.BlockSpec(shape, lambda i, *_: zeros, pipeline_mode=mode)


def attention_forward(scal, crop, x, mine, other, grids, deps=()):
    tokens = grids * CELLS
    rows = pl.BlockSpec((CELLS, D), lambda i, *_: (i, 0))
    spec = pltpu.PrefetchScalarGridSpec(
        num_scalar_prefetch=2,
        grid=(grids,),
        in_specs=[
            pl.BlockSpec((1, CELLS, D), lambda i, s, c: (s[0] + i, 0, 0)),
            whole_block(mine.shape, 1),
            whole_block(mine.shape, 1),
        ] + [ANY] * len(deps),
        out_specs=[
            rows, rows, rows, rows, rows,
            pl.BlockSpec((1, HEADS, CELLS, CELLS), lambda i, *_: (i, 0, 0, 0)),
            rows, rows, rows,
            pl.BlockSpec(memory_space=pl.ANY),
            whole_block((16, D)),
            whole_block((8, 128)),
        ],
        scratch_shapes=[
            pltpu.VMEM((4, D, D), BF), pltpu.VMEM((CELLS, D), BF), pltpu.SemaphoreType.DMA,
        ],
    )
    low, full = pltpu.HBM((tokens, D), BF), pltpu.HBM((tokens, D), F32)
    return pl.pallas_call(
        ignoring(attention_forward_kernel, 5, len(deps)),
        grid_spec=spec,
        out_shape=[
            full, low, low, low, low, pltpu.HBM((grids, HEADS, CELLS, CELLS), BF), low, full,
            sds((tokens, D), BF), pltpu.HBM((4, D, D), BF), sds((16, D), F32), TOKEN,
        ],
        compiler_params=params(40 * MIB),
        cost_estimate=NO_COST,
        name="attention_forward",
    )(scal, crop, x, mine, other, *deps)


def up_forward(scal, n2, mine, other, vec, cotangent, grids, deps=()):
    tokens = grids * CELLS
    block = pl.BlockSpec((1, tokens, D), lambda j, *_: (j, 0, 0))
    half = pl.BlockSpec((OWNERS, HALF, D), lambda j, *_: (0, j, 0))
    spec = pltpu.PrefetchScalarGridSpec(
        num_scalar_prefetch=1,
        grid=(4,),
        in_specs=[
            whole_block((tokens, D), 1),
            whole_block((2 * D, D), 1),
            whole_block((2 * D, D), 1),
            whole_block((16, D)),
            pl.BlockSpec((grids, CELLS, D), lambda j, s: (s[2], 0, 0), pipeline_mode=pl.Buffered(1)),
        ] + [ANY] * len(deps),
        out_specs=[block, block, half, half, pl.BlockSpec(memory_space=pl.ANY), whole_block((8, 128))],
        scratch_shapes=[
            pltpu.VMEM((D, tokens), BF), pltpu.VMEM((4, D, D), BF), pltpu.SemaphoreType.DMA,
        ],
    )
    return pl.pallas_call(
        ignoring(up_kernel, 6, len(deps)),
        grid_spec=spec,
        out_shape=[
            sds((4, tokens, D), BF), pltpu.HBM((4, tokens, D), BF), half_shape(4), in_hbm(half_shape(4)),
            pltpu.HBM((4, D, D), BF), TOKEN,
        ],
        compiler_params=params(40 * MIB * tokens // 768),
        cost_estimate=NO_COST,
        name="up_forward",
    )(scal, n2, mine, other, vec, cotangent, *deps)


def down_forward(scal, hidden, mine, other, after, vec, grids, deps=()):
    tokens = grids * CELLS
    spec = pltpu.PrefetchScalarGridSpec(
        num_scalar_prefetch=1,
        grid=(grids,),
        in_specs=[
            pl.BlockSpec((4, CELLS, D), lambda i, *_: (0, i, 0)),
            whole_block((2 * D, D), 1),
            whole_block((2 * D, D), 1),
            pl.BlockSpec((CELLS, D), lambda i, *_: (i, 0)),
            whole_block((16, D)),
        ] + [ANY] * len(deps),
        out_specs=[
            pl.BlockSpec((1, CELLS, D), lambda i, *_: (i, 0, 0)),
            pl.BlockSpec(memory_space=pl.ANY),
            whole_block((8, 128)),
        ],
        scratch_shapes=[pltpu.VMEM((4, D, D), BF), pltpu.SemaphoreType.DMA],
    )
    return pl.pallas_call(
        ignoring(down_kernel, 6, len(deps)),
        grid_spec=spec,
        out_shape=[pltpu.HBM((grids, CELLS, D), BF), pltpu.HBM((4, D, D), BF), TOKEN],
        compiler_params=params(24 * MIB),
        cost_estimate=NO_COST,
        name="down_forward",
    )(scal, hidden, mine, other, after, vec, *deps)


def mlp_backward(scal, gp, down, up, n2, cotangent, after, vec, mixed, grids, deps=()):
    tokens = grids * CELLS
    last = lambda j: jnp.minimum(j, 3)
    block = pl.BlockSpec((1, tokens, D), lambda j, *_: (last(j), 0, 0))
    weight = pl.BlockSpec((1, D, D), lambda j, *_: (last(j), 0, 0))
    half = pl.BlockSpec((OWNERS, HALF, D), lambda j, *_: (0, j, 0))
    rows = whole_block((tokens, D))
    any_spec = pl.BlockSpec(memory_space=pl.ANY)
    spec = pltpu.PrefetchScalarGridSpec(
        num_scalar_prefetch=1,
        grid=(5,),
        in_specs=[
            block, weight, weight, whole_block((tokens, D), 1),
            pl.BlockSpec((grids, CELLS, D), lambda j, s: (s[2], 0, 0), pipeline_mode=pl.Buffered(1)),
            any_spec, whole_block((16, D)), any_spec,
        ] + [ANY] * len(deps),
        out_specs=[rows, rows, half, half, whole_block((8, D)), whole_block((8, D)), whole_block((8, 128))],
        scratch_shapes=[
            pltpu.VMEM((tokens, D), F32), pltpu.VMEM((D, tokens), BF), pltpu.VMEM((tokens, D), BF),
            pltpu.VMEM((tokens, D), F32), pltpu.VMEM((tokens, D), BF),
            pltpu.SemaphoreType.DMA((2,)),
        ],
    )
    return pl.pallas_call(
        ignoring(mlp_kernel, 9, len(deps)),
        grid_spec=spec,
        out_shape=[
            sds((tokens, D), F32), sds((tokens, D), BF),
            half_shape(5), in_hbm(half_shape(5)), sds((8, D), F32), sds((8, D), F32), TOKEN,
        ],
        compiler_params=params(40 * MIB * tokens // 768),
        cost_estimate=NO_COST,
        name="mlp_backward",
    )(scal, gp, down, up, n2, cotangent, after, vec, mixed, *deps)


def attention_backward(scal, crop, ga, galow, mixed, p, q, k, v, emb, n1, w, vec, gn, gb, grids, deps=()):
    tokens = grids * CELLS
    last = lambda i: jnp.minimum(i, grids - 1)
    rows = pl.BlockSpec((CELLS, D), lambda i, *_: (last(i), 0))
    half = half_shape(3, SMALL)
    few = whole_block((8, D))
    spec = pltpu.PrefetchScalarGridSpec(
        num_scalar_prefetch=2,
        grid=(grids + 1,),
        in_specs=[
            rows, rows, rows,
            pl.BlockSpec((1, HEADS, CELLS, CELLS), lambda i, *_: (last(i), 0, 0, 0)),
            rows, rows, rows, rows, rows,
            whole_block((4, D, D), 1),
            whole_block((16, D)), few, few,
        ] + [ANY] * len(deps),
        out_specs=[
            pl.BlockSpec((1, CELLS, D), lambda i, *_: (last(i), 0, 0)),
            whole_block((CELLS, D)),
            few,
            whole_block(half.shape, 1), whole_block(half.shape, 1),
            whole_block((8, 128)),
        ],
        scratch_shapes=[pltpu.VMEM((CELLS, D), BF)]
        + [pltpu.VMEM((tokens, D), BF)] * 3
        + [pltpu.VMEM((D, tokens), BF), pltpu.VMEM((CELLS, D), F32), pltpu.VMEM((8, D), F32)],
    )
    return pl.pallas_call(
        ignoring(attention_backward_kernel, 15, len(deps)),
        grid_spec=spec,
        out_shape=[
            pltpu.HBM((grids, CELLS, D), BF), sds((CELLS, D), F32), sds((8, D), F32), half, in_hbm(half), TOKEN,
        ],
        compiler_params=params(40 * MIB),
        cost_estimate=NO_COST,
        name="attention_backward",
    )(scal, crop, ga, galow, mixed, p, q, k, v, emb, n1, w, vec, gn, gb, *deps)


class Place:
    def __init__(self, dp_size, mp_size):
        self.z_size = dp_size // 2
        dp, mp = lax.axis_index("dp"), lax.axis_index("mp")
        self.dp, self.mp = dp, mp
        self.z, self.y = dp // 2, dp % 2
        self.x, self.c = mp // 2, mp % 2
        self.core_pairs = [(i, i ^ 1) for i in range(mp_size)]
        self.x_pairs = [(i, i ^ 2) for i in range(mp_size)]
        self.y_pairs = [(i, i ^ 1) for i in range(dp_size)]
        self.z_shift = [
            [(i, ((i // 2 + s) % self.z_size) * 2 + i % 2) for i in range(dp_size)]
            for s in range(self.z_size)
        ]

        self.corner_pairs = [
            (d * mp_size + m, (d ^ 1) * mp_size + (m ^ 2))
            for d in range(dp_size)
            for m in range(mp_size)
        ]

    def core(self, v):
        return lax.ppermute(v, "mp", self.core_pairs)

    def over_corner(self, v):
        return lax.ppermute(v, ("dp", "mp"), self.corner_pairs)

    def over_x(self, v):
        return lax.ppermute(v, "mp", self.x_pairs)

    def over_y(self, v):
        return lax.ppermute(v, "dp", self.y_pairs)

    def over_z(self, v, shift):
        return lax.ppermute(v, "dp", self.z_shift[shift])


def ignoring(kernel, at, count):
    return lambda *refs: kernel(*refs[:at], *refs[at + count :])


def assemble_kernel(rows, extra, depth, views, where, *refs):
    count = 1 + max(at for at, _ in views)
    out, token = refs[count:]
    token[...] = jnp.zeros_like(token)
    z, y, x = where[0], where[1], where[2]
    unit = rows + extra
    held = [(refs[at], row) for at, row in views]
    for s in range(depth):
        zs = lax.rem(z - s + depth, depth)
        for xr in range(2):
            for yr in range(2):
                xs = x if xr == 0 else 1 - x
                ys = y if yr == 0 else 1 - y
                dp = zs * 2 + ys
                lane = pl.ds(pl.multiple_of(xs * (D // 2), D // 2), D // 2)
                for b in range(2):
                    if xr and yr:
                        ref, first = held[3 + b]
                        first += s * unit
                    else:
                        ref, first = held[xr + 2 * yr]
                        first += (b * depth + s) * unit
                    row = pl.ds(pl.multiple_of(b * D + dp * rows, rows), rows)
                    out[row, lane] = ref[first : first + rows, :]
                    if extra:
                        at = 2 * D + b * depth * 2 * extra + dp * extra
                        row = pl.ds(pl.multiple_of(at, extra), extra)
                        out[row, lane] = ref[first + rows : first + unit, :]


def assemble(where, views, pieces, extra, dp_size, deps=()):
    kernel = functools.partial(assemble_kernel, D // dp_size, extra, dp_size // 2, views)
    shape = sds((2 * D + 2 * dp_size * extra, D), BF)
    return call(kernel, "assemble", where, pieces, [shape], deps)


def gather_z(place, u):
    return [u] + [place.over_z(u, s) for s in range(1, place.z_size)]


def call(kernel, name, where, ins, shapes, deps=(), limit=16):
    vmem = pl.BlockSpec(memory_space=pltpu.VMEM)
    return pl.pallas_call(
        ignoring(kernel, 1 + len(ins), len(deps)),
        in_specs=[pl.BlockSpec(memory_space=pltpu.SMEM)] + [vmem] * len(ins) + [ANY] * len(deps),
        out_specs=[vmem] * (len(shapes) + 1),
        out_shape=[*shapes, TOKEN],
        compiler_params=params(limit * MIB),
        cost_estimate=NO_COST,
        name=name,
    )(where, *ins, *deps)


def pack_kernel(count, has_next, unit_at, where, *refs):
    parts, refs = refs[:count], refs[count:]
    half, lows = 0, None
    if has_next:
        by_x, by_y, refs = refs[0], refs[1], refs[2:]
        half = has_next
    token = refs[-1]
    token[...] = jnp.zeros_like(token)
    outs = refs[:-1]
    if unit_at:
        units, outs = outs[0], outs[1:]
        outs[-1][...] = units[unit_at]
        outs = outs[:-1]
    if half:
        first_x, first_y = half[0], half[1]
        size = half[2]
        outs[-2][:size, :] = by_x[first_x : first_x + size, :]
        outs[-1][:size, :] = by_y[first_y : first_y + size, :]
    if count:
        unit = parts[0].shape[1]
        for b in range(2):
            for s in range(count):
                value = parts[s][b]
                at = (b * count + s) * unit
                outs[0][at : at + unit, :] = value
                if half:
                    outs[-2][size + at : size + at + unit, :] = value
                    outs[-1][size + at : size + at + unit, :] = value


def pack(where, parts, by_x, by_y, half, units=None, unit_at=0, deps=()):
    count = len(parts)
    shapes = []
    rows = 2 * count * parts[0].shape[1] if count else 0
    if count:
        shapes.append(sds((rows, D // 2), BF))
    ins = list(parts)
    if half:
        ins += [by_x, by_y]
        shapes += [sds((half[2] + rows, D // 2), BF)] * 2
    if unit_at:
        ins.append(units)
        shapes.append(sds(units.shape[1:], BF))
    kernel = functools.partial(pack_kernel, count, half, unit_at)
    return call(kernel, "pack", where, ins, shapes, deps)


def add(a, b):
    return a.astype(F32) + b.astype(F32)


def dp_of(z, y):
    return z * 2 + y


def split_y(y, value_at, depth, send, keep):
    for z in range(depth):
        send[z] = value_at(dp_of(z, 1 - y)).astype(BF)
        keep[z] = value_at(dp_of(z, y)).astype(BF)


def split_x(x, value, send, keep):
    side = D // 2
    left, right = value[:, :side].astype(BF), value[:, side:].astype(BF)

    @pl.when(x == 0)
    def _():
        send[...] = right
        keep[...] = left

    @pl.when(x != 0)
    def _():
        send[...] = left
        keep[...] = right


def first_y_kernel(where, mine, got, send, keep, token):
    token[...] = jnp.zeros_like(token)
    split_y(where[1], lambda dp: add(mine[dp], got[dp]), OWNERS // 2, send, keep)


def first_y(where, mine, got, deps=()):
    rows = mine.shape[1]
    shape = sds((OWNERS // 2, rows, D), BF)
    return call(first_y_kernel, "first_y", where, [mine, got], [shape, shape], deps)


def first_both_kernel(cut, where, mine, got, send_y, keep_y, send_x, keep_x, token):
    token[...] = jnp.zeros_like(token)
    depth = OWNERS // 2
    split_y(where[1], lambda dp: add(mine[dp, :cut], got[dp, :cut]), depth, send_y, keep_y)
    for dp in range(OWNERS):
        split_x(where[2], add(mine[dp, cut:], got[dp, cut:]), send_x.at[dp], keep_x.at[dp])


def first_both(where, mine, got, deps=()):
    rows = mine.shape[1]
    cut = (2 * rows // 3) // 16 * 16
    over_y = sds((OWNERS // 2, cut, D), BF)
    over_x = sds((OWNERS, rows - cut, D // 2), BF)
    kernel = functools.partial(first_both_kernel, cut)
    return call(kernel, "first_both", where, [mine, got], [over_y, over_y, over_x, over_x], deps)


def first_x_kernel(where, mine, got, send, keep, token):
    token[...] = jnp.zeros_like(token)
    for dp in range(OWNERS):
        split_x(where[2], add(mine[dp], got[dp]), send.at[dp], keep.at[dp])


def first_x(where, mine, got, deps=()):
    shape = sds((OWNERS, mine.shape[1], D // 2), BF)
    return call(first_x_kernel, "first_x", where, [mine, got], [shape, shape], deps)


def second_y_kernel(where, mine, got, send, keep, token):
    token[...] = jnp.zeros_like(token)
    split_y(where[1], lambda dp: add(mine[dp], got[dp]), OWNERS // 2, send, keep)


def second_y(where, mine, got, deps=()):
    shape = sds((OWNERS // 2,) + mine.shape[1:], BF)
    return call(second_y_kernel, "second_y", where, [mine, got], [shape, shape], deps)


def second_both_kernel(where, keep_y, got_y, keep_x, got_x, send_a, left_a, send_b, left_b, token):
    token[...] = jnp.zeros_like(token)
    depth = OWNERS // 2
    for z in range(depth):
        split_x(where[2], add(keep_y[z], got_y[z]), send_a.at[z], left_a.at[z])
    split_y(where[1], lambda dp: add(keep_x[dp], got_x[dp]), depth, send_b, left_b)


def second_both(where, keep_y, got_y, keep_x, got_x, deps=()):
    over_x = sds((OWNERS // 2, keep_y.shape[1], D // 2), BF)
    over_y = sds((OWNERS // 2, keep_x.shape[1], D // 2), BF)
    ins = [keep_y, got_y, keep_x, got_x]
    return call(second_both_kernel, "second_both", where, ins, [over_x, over_x, over_y, over_y], deps)


def split_z_kernel(pairs, where, *refs):
    ins, outs = refs[: 2 * pairs], refs[2 * pairs : -1]
    refs[-1][...] = jnp.zeros_like(refs[-1])
    depth = ins[0].shape[0]
    for s in range(depth):
        z = lax.rem(where[0] + s, depth)
        row = 0
        for i in range(pairs):
            value = add(ins[2 * i][z], ins[2 * i + 1][z]).astype(BF)
            outs[s][row : row + value.shape[0], :] = value
            row += value.shape[0]


def split_z(where, *ins, deps=()):
    depth, width = ins[0].shape[0], ins[0].shape[2]
    rows = sum(v.shape[1] for v in ins[::2])
    kernel = functools.partial(split_z_kernel, len(ins) // 2)
    return call(kernel, "split_z", where, list(ins), [sds((rows, width), BF)] * depth, deps)


def z_to_x_kernel(where, keep, *refs):
    got, (send, left, token) = refs[:-3], refs[-3:]
    token[...] = jnp.zeros_like(token)
    total = keep[...].astype(F32)
    for ref in got:
        total = total + ref[...].astype(F32)
    split_x(where[2], total, send, left)


def z_to_x(where, keep, got, deps=()):
    shape = sds((keep.shape[0], D // 2), BF)
    return call(z_to_x_kernel, "z_to_x", where, [keep, *got], [shape, shape], deps)


def pair_kernel(where, own, by_x, out, token):
    token[...] = jnp.zeros_like(token)
    out[0] = own[...]
    out[1] = by_x[...]


def collect_kernel(where, here, there, out, token):
    token[...] = jnp.zeros_like(token)
    x, c = where[2], where[3]
    grids = here.shape[1]
    for piece, core in ((here, c), (there, 1 - c)):
        for half in range(2):
            mp = 2 * (x if half == 0 else 1 - x) + core
            for n in range(grids):
                out[mp * grids + n] = piece[half, n]


def pair_grids(where, own, by_x, deps=()):
    return call(pair_kernel, "pair", where, [own, by_x], [sds((2,) + own.shape, own.dtype)], deps)


def finish_grids(place, where, here):
    shape = sds((here.shape[0] * 2 * here.shape[1],) + here.shape[2:], here.dtype)
    return call(collect_kernel, "collect", where, [here, place.core(here)], [shape])


def plane_kernel(where, own, by_x, by_y, by_corner, out, token):
    token[...] = jnp.zeros_like(token)
    out[0:16, :] = own[0:16, :]
    out[16:32, :] = by_x[0:16, :]
    here = own[16:24, :] + by_x[16:24, :]
    out[32:40, :] = here + (by_y[...] + by_corner[...])


def sum_plane(place, where, packed, square):
    ins = [packed, place.over_x(packed), place.over_y(square), place.over_corner(square)]
    here, _ = call(plane_kernel, "plane", where, ins, [sds((40, D // 2), F32)])
    there = place.core(here)
    value = here[32:40, :128] + there[32:40, :128]
    return here, there, [value] + [place.over_z(value, s) for s in range(1, place.z_size)]


ROWS1, ROWS2, ROWS3 = 4 * HALF, 5 * HALF, 3 * HALF
ROWS = ROWS1 + ROWS2 + ROWS3


def totals_kernel(where, *refs):
    keep1, got1, keep2, *got2 = refs[:6]
    keep3, *got3 = refs[6:10]
    kept_ref, sent_ref, tail_ref, packed_ref, square_ref, token = refs[10:]
    token[...] = jnp.zeros_like(token)
    x, c = where[2], where[3]

    def total(first, others):
        value = first[...].astype(F32)
        for ref in others:
            value = value + ref[...].astype(F32)
        return value

    whole3 = total(keep3, got3)
    parts = (total(keep1, [got1]), total(keep2, got2), whole3[:ROWS3])
    wide = D // 4
    row = 0
    square = jnp.zeros((1, D // 2), F32)
    for value in parts:
        rows = slice(row, row + value.shape[0])
        left, right = value[:, :wide], value[:, wide:]

        @pl.when(c == 0)
        def _():
            kept_ref[rows, :] = left
            sent_ref[rows, :] = right

        @pl.when(c != 0)
        def _():
            kept_ref[rows, :] = right
            sent_ref[rows, :] = left

        square = square + jnp.sum(value * value, axis=0, keepdims=True)
        row += value.shape[0]
    tail = whole3[ROWS3:]
    tail_ref[...] = tail
    lane = lax.broadcasted_iota(jnp.int32, (16, D // 2), 1)
    line = lax.broadcasted_iota(jnp.int32, (16, D // 2), 0)
    owner = jnp.where((x == 0) & (c == 0), 1.0, 0.0)
    codes = tail[16:32]
    small = jnp.where(line < 8, jnp.where(lane < D // OWNERS, codes * owner, 0.0), 0.0)
    small = jnp.where((line >= 8) & (lane < D // (4 * OWNERS)), codes, small)
    square = square + jnp.sum(tail[:16] * tail[:16] + small * small, axis=0, keepdims=True)
    square_ref[...] = jnp.full((8, D // 2), jnp.sum(square), F32)
    packed_ref[0:16, :] = tail[:16]
    packed_ref[16:24, :] = square_ref[...]


def totals(where, keep1, got1, keep2, got2, keep3, got3, deps=()):
    ins = [keep1, got1, keep2, *got2, keep3, *got3]
    half = sds((ROWS, D // 4), F32)
    shapes = [half, half] + [sds((rows, D // 2), F32) for rows in (SMALL, 24, 8)]
    return call(totals_kernel, "totals", where, ins, shapes, deps)


def update_kernel(where, *refs):
    kept, got, tail, plane, other_plane = refs[:5]
    squares = refs[5:9]
    state, outs = refs[9:24], refs[24:]
    x, c = where[2], where[3]
    square = (squares[0][0:1, 0:1] + squares[2][0:1, 0:1]) + (
        squares[1][0:1, 0:1] + squares[3][0:1, 0:1]
    )
    norm = jnp.sqrt(square)
    factor = jnp.minimum(1.0, CLIP_LIMIT / (norm + 1e-06))
    outs[0][...] = norm

    def step(at, index, gradient, rate, decay):
        weight, first, second = (state[at + 5 * i][index] for i in range(3))
        new = adam_step(weight, gradient, first, second, rate, decay)
        for i in range(3):
            outs[1 + at + 5 * i][index] = new[i]

    def block(row):
        rows = slice(row, row + HALF)
        own, other = kept[rows, :], got[rows, :]
        top = jnp.where(c == 0, own, other)
        bottom = jnp.where(c == 0, other, own)
        return jnp.concatenate([top, bottom], axis=0) * factor

    front = [ROWS1 + ROWS2 + HALF * b for b in range(3)] + [ROWS1 + HALF * b for b in range(4)]
    for b, row in enumerate(front):
        step(0, b, block(row), RATE_MATRIX, DECAY_RATE)
    back = [ROWS1 + 4 * HALF] + [HALF * b for b in range(4)]
    for b, row in enumerate(back):
        step(1, b, block(row).T, RATE_MATRIX, DECAY_RATE)
    norm_grad = tail[16:22, : D // OWNERS] * factor
    outs[16][...] = norm_grad
    step(3, Ellipsis, norm_grad, RATE_VECTOR, 0.0)
    step(2, Ellipsis, tail[24:30, : D // (4 * OWNERS)] * factor, RATE_VECTOR, 0.0)
    own, by_x = plane[0:16, :], plane[16:32, :]
    by_core, by_both = other_plane[0:16, :], other_plane[16:32, :]
    here = jnp.concatenate(
        [jnp.where(c == 0, own, by_core), jnp.where(c == 0, by_core, own)], axis=0
    )
    there = jnp.concatenate(
        [jnp.where(c == 0, by_x, by_both), jnp.where(c == 0, by_both, by_x)], axis=0
    )
    side = D // 2
    for half in range(2):
        gradient = jnp.where(x == half, here, there) * factor
        lanes = (slice(None), slice(half * side, (half + 1) * side))
        step(4, lanes, gradient, RATE_TABLE, DECAY_RATE)


def update(where, kept, got, tail, here, there, squares, state, deps):
    vmem = pl.BlockSpec(memory_space=pltpu.VMEM)
    ins = [kept, got, tail, here, there, *squares, *state]
    shapes = [sds((1, 1), F32)] + [sds(v.shape, F32) for v in state] + [sds(state[3].shape, F32)]
    return pl.pallas_call(
        ignoring(update_kernel, 1 + len(ins), len(deps)),
        in_specs=[pl.BlockSpec(memory_space=pltpu.SMEM)] + [vmem] * len(ins) + [ANY] * len(deps),
        out_specs=[vmem] * len(shapes),
        out_shape=shapes,
        compiler_params=params(24 * MIB),
        cost_estimate=NO_COST,
        name="update",
    )(where, *ins, *deps)


def adam_step(weight, gradient, first, second, rate, decay):
    first_new = BETA_FIRST * first + (1.0 - BETA_FIRST) * gradient
    second_new = BETA_SECOND * second + (1.0 - BETA_SECOND) * gradient * gradient
    first_hat = first_new / (1.0 - BETA_FIRST**STEP)
    second_hat = second_new / (1.0 - BETA_SECOND**STEP)
    weight_new = weight - rate * (first_hat / (jnp.sqrt(second_hat) + ADAM_EPS) + decay * weight)
    return (weight_new, first_new, second_new)


def body(
    dp_size, mp_size,
    block_input, cotangent, crop_boxes, front_weights, back_weights, split_biases, norm_params,
    pos_table, front_first, back_weight_first_moment, split_first, norm_first, table_first,
    front_second, back_second, split_second, norm_second, table_second,
):
    place = Place(dp_size, mp_size)
    direct = dp_size == 8 and mp_size == 4
    x, y, z, c = place.x, place.y, place.z, place.c
    grids = block_input.shape[0] // mp_size
    scal = jnp.stack([place.mp * grids, c, place.mp, place.dp]).astype(jnp.int32)
    where = jnp.stack([z, y, x, c]).astype(jnp.int32)
    turned = jnp.swapaxes(back_weights, 1, 2).astype(BF)
    low_front = front_weights.astype(BF)
    rows, lanes = low_front.shape[1], low_front.shape[2]

    if direct:
        shards = jnp.concatenate([low_front[:3], turned[:1], low_front[3:], turned[1:]])
        shards = shards.reshape(3, 2, 2, rows, lanes)
        mine = lax.dynamic_index_in_dim(shards, c, axis=1, keepdims=False)
        sent = lax.dynamic_index_in_dim(shards, 1 - c, axis=1, keepdims=False)
        got = place.core(sent)
        units = jnp.where(
            c == 0, jnp.concatenate([mine, got], -1), jnp.concatenate([got, mine], -1)
        )
        extra = pos_table.shape[0] // 2
        half = jnp.where(c == 0, pos_table[:extra], pos_table[extra:]).astype(BF)
        half = jnp.where(x == 0, half[:, : D // 2], half[:, D // 2 :])
        packed = jnp.zeros((extra, D // 2), BF)
        packed = lax.dynamic_update_slice(packed, norm_params.astype(BF), (0, 0))
        packed = lax.dynamic_update_slice(packed, split_biases.astype(BF), (0, 128))
        first_unit = jnp.concatenate([units[0], jnp.stack([half, packed])], axis=1)
        own1, unit2, _ = pack(where, gather_z(place, first_unit), None, None, None, units, 1)
        x1, y1 = place.over_x(own1), place.over_y(own1)
        size1, size2 = own1.shape[0] // 2, units.shape[1] * units.shape[2] * place.z_size // 2
        own2, sent_y, sent_x, unit3, _ = pack(
            where, gather_z(place, unit2), x1, y1, (0, size1, size1), units, 2
        )
        y2, x2 = place.over_y(sent_y), place.over_x(sent_x)
        own3, sent_y, sent_x, token3 = pack(
            where, gather_z(place, unit3), x2, y2, (size1, size1 + size2, size2)
        )
        y3, x3 = place.over_y(sent_y), place.over_x(sent_x)
        attn_mine, _ = assemble(
            where, ((0, 0), (1, 0), (2, 0), (4, 0), (3, 0)), (own1, x1, y1, x2, y2), extra, dp_size,
            (token3,),
        )
        attn_other = place.core(attn_mine)
        first_deps = (token3,)
    else:

        def halves(v):
            v = lax.all_gather(v, "dp", axis=1, tiled=True)
            v = lax.all_gather(v, "mp", axis=2, tiled=True).reshape(2, 2 * D, D)
            return jnp.where(c == 0, v[0], v[1]), jnp.where(c == 0, v[1], v[0])

        attn_mine, attn_other = halves(jnp.concatenate([low_front[:3], turned[:1]]))
        up_pair, down_pair = halves(low_front[3:]), halves(turned[1:])
        table = lax.all_gather(pos_table.astype(BF), "dp", axis=0, tiled=True)
        table = table.reshape(OWNERS, 2, CELLS // (2 * OWNERS), D)
        table = jnp.swapaxes(table, 0, 1).reshape(2, CELLS // 2, D)
        norms = lax.all_gather(norm_params.astype(BF), "dp", axis=1, tiled=True)
        splits = lax.all_gather(split_biases.astype(BF), ("mp", "dp"), axis=1, tiled=True)
        norms = jnp.swapaxes(norms.reshape(6, OWNERS, D // OWNERS), 0, 1)
        splits = jnp.transpose(splits.reshape(6, 2, 2, OWNERS, -1), (2, 3, 0, 1, 4))
        codes = jnp.zeros((2, OWNERS, CELLS // (2 * OWNERS), D), BF)
        codes = codes.at[:, :, 0:6, : norms.shape[2]].set(norms)
        for side in range(2):
            lane = side * (D // 2) + 128
            codes = codes.at[:, :, 0:6, lane : lane + splits.shape[4]].set(splits[:, :, :, side])
        table = jnp.concatenate([table, codes.reshape(2, -1, D)], axis=1)
        attn_mine = jnp.concatenate([attn_mine, jnp.where(c == 0, table[0], table[1])])
        attn_other = jnp.concatenate([attn_other, jnp.where(c == 0, table[1], table[0])])
        first_deps = ()

    emb, normed1, q, k, v, p, mixed, after, normed2, w_attn, vec, token = attention_forward(
        scal, crop_boxes, block_input, attn_mine, attn_other, grids, first_deps
    )
    deps = ()
    if direct:
        sent_y, sent_x, token4 = pack(where, [], x3, y3, (size2, 2 * size2, size2), deps=(token,))
        y4, x4 = place.over_y(sent_y), place.over_x(sent_x)
        half, _ = assemble(
            where, ((0, 0), (1, size1), (2, size1), (4, 0), (3, 0)), (own2, x2, y2, x3, y3), 0, dp_size,
            (token4,),
        )
        up_pair = half, place.core(half)
        deps = (token4,)
    hidden, gp, down_mine, down_other, w_up, token = up_forward(
        scal, normed2, *up_pair, vec, cotangent, grids, deps
    )
    if direct:
        half, token = assemble(
            where, ((0, 0), (1, size2), (2, size2), (4, 0), (3, 0)), (own3, x3, y3, x4, y4), 0, dp_size,
            (token,),
        )
        down_pair = half, place.core(half)
        down_other, token = behind(down_other, token)
        sent, keep1, token = first_y(where, down_mine, place.core(down_other))
        got1 = place.over_y(sent)
        deps = (token,)
    out, w_down, token = down_forward(scal, hidden, *down_pair, after, vec, grids, deps)
    if direct:
        out_x = place.over_x(out)
        deps = (token,)
    ga, galow, up_mine, up_other, gb, gn, token = mlp_backward(
        scal, gp, w_down, w_up, normed2, cotangent, after, vec, mixed, grids, deps
    )
    if direct:
        out_pair, token = pair_grids(where, out, out_x, (token,))
        keep1, *sent, token1 = split_z(where, keep1, got1, deps=(token,))
        got1 = [place.over_z(sent[s - 1], s) for s in range(1, place.z_size)]
        up_other, token1 = behind(up_other, token1)
        sent_x, keep2, token2 = first_x(where, up_mine, place.core(up_other), (token1,))
        got2 = place.over_x(sent_x)
        block_output, token3 = finish_grids(place, where, out_pair)
        deps = (token1, token2, token3)
    ig, dtable, gs, mine3, other3, token = attention_backward(
        scal, crop_boxes, ga, galow, mixed, p, q, k, v, emb, normed1, w_attn, vec, gn, gb, grids, deps
    )
    cells_here, norm_here = pos_table.shape[0], norm_params.shape[1]
    split_here = split_biases.shape[1]
    if direct:
        sent1, keep1, token1 = z_to_x(where, keep1, got1, (token,))
        got1 = place.over_x(sent1)
        sent_y, keep2, token2 = second_y(where, keep2, got2, (token1,))
        got2 = place.over_y(sent_y)
        ig_x = place.over_x(ig)
        other3, token2 = behind(other3, token2)
        sent_y, keep3a, sent_x, keep3b, token3 = first_both(
            where, mine3, place.core(other3), (token1, token2)
        )
        got3a, got3b = place.over_y(sent_y), place.over_x(sent_x)
        keep2, *sent, token = split_z(where, keep2, got2, deps=(token3,))
        got2 = [place.over_z(sent[s - 1], s) for s in range(1, place.z_size)]
        sent_x, keep3a, sent_y, keep3b, token = second_both(
            where, keep3a, got3a, keep3b, got3b, (token,)
        )
        got3a, got3b = place.over_x(sent_x), place.over_y(sent_y)
        keep3, *sent, token = split_z(where, keep3a, got3a, keep3b, got3b, deps=(token, *got2))
        got3 = [place.over_z(sent[s - 1], s) for s in range(1, place.z_size)]
        ig_pair, token = pair_grids(where, ig, ig_x, (token,))
        input_grad, token = finish_grids(place, where, ig_pair)
        kept, sent, tail, packed, square, _ = totals(
            where, keep1, got1, keep2, got2, keep3, got3, (token,)
        )
        got = place.core(sent)
        here, there, squares = sum_plane(place, where, packed, square)
        state = (
            front_weights, back_weights, split_biases, norm_params, pos_table,
            front_first, back_weight_first_moment, split_first, norm_first, table_first,
            front_second, back_second, split_second, norm_second, table_second,
        )
        state = [pltpu.with_memory_space_constraint(v, pltpu.HBM) for v in state]
        new = update(where, kept, got, tail, here, there, squares, state, ())
        return (block_output, input_grad, new[0][0, 0], *new[1:])
    else:

        def share(mine, other, blocks):
            low, high = jnp.where(c == 0, mine, other), jnp.where(c == 0, other, mine)
            full = jnp.stack([low, high], 1)[:, :, : blocks * HALF].astype(F32)
            full = full.reshape(OWNERS, 2, blocks, HALF, D)
            full = jnp.transpose(full, (2, 0, 1, 3, 4)).reshape(blocks, D, D)
            full = lax.psum_scatter(full, "dp", scatter_dimension=1, tiled=True)
            return lax.psum_scatter(full, "mp", scatter_dimension=2, tiled=True)

        down_share = share(down_mine, down_other, 4)
        up_share = share(up_mine, up_other, 5)
        out_share, up_share = up_share[4:], up_share[:4]
        qkv_share = share(mine3, other3, 3)
        block_output = lax.all_gather(out, "mp", axis=0, tiled=True)
        input_grad = lax.all_gather(ig, "mp", axis=0, tiled=True)
        norm_grad = jnp.concatenate([gs[2:4], gn[2:6]])
        split_grad = jnp.concatenate([gs[0:2], gb[0:4]])
        dtable = lax.psum(dtable, ("dp", "mp"))
        norm_grad = lax.psum(norm_grad, ("dp", "mp"))
        split_grad = lax.psum(split_grad, ("dp", "mp"))
        table_share = lax.dynamic_slice(dtable, (place.dp * cells_here, 0), (cells_here, D))
        norm_share = lax.dynamic_slice(norm_grad, (0, place.dp * norm_here), (6, norm_here))
        split_share = lax.dynamic_slice(
            split_grad, (0, (place.mp * dp_size + place.dp) * split_here), (6, split_here)
        )
        table_square = jnp.sum(table_share * table_share) / mp_size
    front_share = jnp.concatenate([qkv_share, up_share])
    back_share = jnp.concatenate([out_share, down_share])
    owner = (place.mp == 0).astype(F32)
    square = (
        jnp.sum(qkv_share * qkv_share)
        + jnp.sum(out_share * out_share)
        + jnp.sum(up_share * up_share)
        + jnp.sum(down_share * down_share)
        + jnp.sum(split_share * split_share)
        + owner * jnp.sum(norm_share * norm_share)
        + table_square
    )
    clip_norm = jnp.sqrt(lax.psum(square, ("dp", "mp")))
    factor = jnp.minimum(1.0, CLIP_LIMIT / (clip_norm + 1e-06))
    norm_clipped = norm_share * factor
    new_front, front_first_new, front_second_new = adam_step(
        front_weights, front_share * factor, front_first, front_second, RATE_MATRIX, DECAY_RATE
    )
    new_back, back_first_new, back_second_new = adam_step(
        back_weights,
        jnp.swapaxes(back_share, 1, 2) * factor,
        back_weight_first_moment,
        back_second,
        RATE_MATRIX,
        DECAY_RATE,
    )
    new_split, split_first_new, split_second_new = adam_step(
        split_biases, split_share * factor, split_first, split_second, RATE_VECTOR, 0.0
    )
    new_norm, norm_first_new, norm_second_new = adam_step(
        norm_params, norm_clipped, norm_first, norm_second, RATE_VECTOR, 0.0
    )
    new_table, table_first_new, table_second_new = adam_step(
        pos_table, table_share * factor, table_first, table_second, RATE_TABLE, DECAY_RATE
    )
    return (
        block_output, input_grad, clip_norm,
        new_front, new_back, new_split, new_norm, new_table,
        front_first_new, back_first_new, split_first_new, norm_first_new, table_first_new,
        front_second_new, back_second_new, split_second_new, norm_second_new, table_second_new,
        norm_clipped,
    )


def solution(mesh):
    front, back = P(None, "dp", "mp"), P(None, "mp", "dp")
    split, norm, table = P(None, ("mp", "dp")), P(None, "dp"), P("dp", None)
    state = (front, back, split, norm, table)
    rows = P("dp", None, None)
    return jax.shard_map(
        functools.partial(body, mesh.shape["dp"], mesh.shape["mp"]),
        mesh=mesh,
        in_specs=(rows, rows, P("dp", None)) + state * 3,
        out_specs=(rows, rows, P()) + state * 3 + (norm,),
        check_vma=False,
    )
```

```python
import functools

import jax
import jax.numpy as jnp
from jax import lax
from jax.experimental import pallas as pl
from jax.experimental.pallas import tpu as pltpu
from jax.sharding import PartitionSpec as P

D = 768
HEADS = 16
HEAD = D // HEADS
SIDE = 16
CELLS = 256
STEP = 5
CORES = 2

NORM_EPS = 1e-05
BETA_FIRST = 0.9
BETA_SECOND = 0.95
ADAM_EPS = 1e-08
RATE_MATRIX = 0.05
RATE_TABLE = 0.2
RATE_VECTOR = 0.5
DECAY_RATE = 0.1
CLIP_LIMIT = 0.01
MASK_FILL = -1e30
SCALE = HEAD ** (-0.5)
LOG2E = 1.4426950408889634
INV_SQRT_2PI = 0.3989422804014327

OWNERS = 8
HALF = D // (2 * OWNERS)
SMALL = 32

BF = jnp.bfloat16
F32 = jnp.float32
MIB = 1024 * 1024
NN = (((1,), (0,)), ((), ()))
NT = (((1,), (1,)), ((), ()))
TN = (((0,), (0,)), ((), ()))


NO_COST = pl.CostEstimate(flops=0, bytes_accessed=0, transcendentals=0)


def dot(a, b, dims=NN):
    return lax.dot_general(a, b, dims, preferred_element_type=F32)


def params(limit):
    return pltpu.CompilerParams(vmem_limit_bytes=limit)


def norm_stats(v):
    mean = jnp.mean(v, axis=-1, keepdims=True)
    centred = v - mean
    spread = jnp.mean(centred * centred, axis=-1, keepdims=True)
    rstd = lax.rsqrt(spread + NORM_EPS)
    return centred * rstd, rstd


def norm_back(c, gain, u, rstd):
    cg = c * gain
    mean_cg = jnp.mean(cg, axis=-1, keepdims=True)
    mean_cgu = jnp.mean(cg * u, axis=-1, keepdims=True)
    return rstd * (cg - mean_cg - u * mean_cgu)


def head_window(h):
    low = h * HEAD
    first = low // 128
    last = (low + HEAD - 1) // 128
    return first, last + 1 - first


def head_mask(h):
    first, tiles = head_window(h)
    lane = lax.broadcasted_iota(jnp.int32, (1, tiles * 128), 1) + first * 128
    return (lane >= h * HEAD) & (lane < (h + 1) * HEAD)


def crop_target(position, height, breadth, top, left):
    row = (position >> 4) - top
    col = (position & (SIDE - 1)) - left
    inside = (row >= 0) & (row < height) & (col >= 0) & (col < breadth)
    return jnp.where(inside, row * breadth + col, -1)


def load_weights(core, mine_ref, other_ref, w_ref, copy_ref, sem, token_ref):
    copy = pltpu.make_async_copy(w_ref, copy_ref, sem)

    @pl.when(pl.program_id(0) == 0)
    def _():
        token_ref[...] = jnp.zeros_like(token_ref)

        def fill(low, high):
            for b in range(2):
                rows = slice(b * D, (b + 1) * D)
                w_ref[b] = low[rows, :]
                w_ref[2 + b] = high[rows, :]

        @pl.when(core == 0)
        def _():
            fill(mine_ref, other_ref)

        @pl.when(core != 0)
        def _():
            fill(other_ref, mine_ref)

        copy.start()

    @pl.when(pl.program_id(0) == pl.num_programs(0) - 1)
    def _():
        copy.wait()


def attention_forward_kernel(
    scal, crop, x_ref, mine_ref, other_ref,
    emb_ref, n1_ref, q_ref, k_ref, v_ref, p_ref, mixed_ref, after_ref, n2_ref, wcopy_ref, vec_ref, token_ref,
    w_ref, table_ref, sem,
):
    load_weights(scal[1], mine_ref, other_ref, w_ref, wcopy_ref, sem, token_ref)
    part = CELLS // (2 * OWNERS)

    @pl.when(pl.program_id(0) == 0)
    def _():
        for at, ref in ((scal[1], mine_ref), (1 - scal[1], other_ref)):
            for dp in range(OWNERS):
                row = pl.ds(pl.multiple_of((2 * dp + at) * part, part), part)
                table_ref[row, :] = ref[2 * D + dp * part : 2 * D + (dp + 1) * part, :]
        vec_ref[...] = jnp.zeros_like(vec_ref)
        wide, thin = D // OWNERS, D // (4 * OWNERS)
        first = 2 * D + CELLS // 2

        def unpack(ref, core):
            for dp in range(OWNERS):
                rows = slice(first + dp * part, first + dp * part + 6)
                if core == 0:
                    vec_ref[0:6, dp * wide : (dp + 1) * wide] = ref[rows, 0:wide].astype(F32)
                for x in range(2):
                    lane = x * (D // 2) + 128
                    at = (2 * x + core) * (D // 4) + dp * thin
                    vec_ref[8:14, at : at + thin] = ref[rows, lane : lane + thin].astype(F32)

        @pl.when(scal[1] == 0)
        def _():
            unpack(mine_ref, 0)
            unpack(other_ref, 1)

        @pl.when(scal[1] != 0)
        def _():
            unpack(other_ref, 0)
            unpack(mine_ref, 1)

    grid = scal[0] + pl.program_id(0)
    height, breadth, top, left = crop[grid, 0], crop[grid, 1], crop[grid, 2], crop[grid, 3]
    target = crop_target(
        lax.broadcasted_iota(jnp.int32, (1, CELLS), 1), height, breadth, top, left
    )
    cell = lax.broadcasted_iota(jnp.int32, (CELLS, CELLS), 0)
    onehot = jnp.where(cell == target, 1.0, 0.0).astype(BF)
    emb = x_ref[0].astype(F32) + dot(onehot, table_ref[...])
    emb_ref[...] = emb
    u, _ = norm_stats(emb)
    n1 = (u * vec_ref[0:1, :] + vec_ref[1:2, :]).astype(BF)
    n1_ref[...] = n1
    q_ref[...] = (dot(n1, w_ref[0]) + vec_ref[8:9, :]).astype(BF)
    k_ref[...] = dot(n1, w_ref[1]).astype(BF)
    v_ref[...] = (dot(n1, w_ref[2]) + vec_ref[9:10, :]).astype(BF)
    valid = lax.broadcasted_iota(jnp.int32, (1, CELLS), 1) < height * breadth
    tiles_out = [None] * (D // 128)
    for h in range(HEADS):
        first, tiles = head_window(h)
        lanes = slice(first * 128, (first + tiles) * 128)
        mask = head_mask(h)
        qh = jnp.where(mask, q_ref[:, lanes], 0).astype(BF)
        s = jnp.where(valid, dot(qh, k_ref[:, lanes], NT), MASK_FILL)
        top_score = jnp.max(s, axis=-1, keepdims=True)
        e = jnp.exp2((s - top_score) * (SCALE * LOG2E))
        p_ref[0, h] = (e * (1.0 / jnp.sum(e, axis=-1, keepdims=True))).astype(BF)
    for h in range(HEADS):
        first, tiles = head_window(h)
        lanes = slice(first * 128, (first + tiles) * 128)
        mask = head_mask(h)
        vh = jnp.where(mask, v_ref[:, lanes], 0).astype(BF)
        o = dot(p_ref[0, h], vh)
        for t in range(tiles):
            part = o[:, t * 128 : (t + 1) * 128]
            at = first + t
            tiles_out[at] = part if tiles_out[at] is None else tiles_out[at] + part
    for t in range(D // 128):
        mixed_ref[:, t * 128 : (t + 1) * 128] = tiles_out[t].astype(BF)
    attention = dot(mixed_ref[...], w_ref[3], NT)
    after = emb_ref[...] + attention + vec_ref[2:3, :]
    after_ref[...] = after
    u2, _ = norm_stats(after)
    n2_ref[...] = (u2 * vec_ref[3:4, :] + vec_ref[4:5, :]).astype(BF)


def up_kernel(
    scal, n2_ref, low_ref, high_ref, vec_ref, g_ref,
    hidden_ref, gp_ref, mine_ref, other_ref, wcopy_ref, token_ref, gt_ref, w_ref, sem,
):
    j = pl.program_id(0)
    load_weights(scal[1], low_ref, high_ref, w_ref, wcopy_ref, sem, token_ref)
    grids = g_ref.shape[0]

    @pl.when(j == 0)
    def _():
        for n in range(grids):
            gt_ref[:, n * CELLS : (n + 1) * CELLS] = g_ref[n].T

    bias = vec_ref[pl.ds(10 + j, 1), :]
    for n in range(grids):
        rows = slice(n * CELLS, (n + 1) * CELLS)
        pre = dot(n2_ref[rows, :], w_ref[j]) + bias
        phi = 0.5 + 0.5 * lax.erf(pre * (0.5**0.5))
        density = jnp.exp2(pre * pre * (-0.5 * LOG2E)) * INV_SQRT_2PI
        hidden_ref[0, rows, :] = (pre * phi).astype(BF)
        gp_ref[0, rows, :] = (phi + pre * density).astype(BF)
    grad = dot(gt_ref[...], hidden_ref[0]).astype(BF)
    keep(scal[1], 0, grad, mine_ref, other_ref)


def keep(core, at, grad, mine_ref, other_ref):
    parts = grad.reshape(OWNERS, 2, HALF, D)
    rows = slice(at * HALF, (at + 1) * HALF)

    @pl.when(core == 0)
    def _():
        mine_ref[:, rows, :] = parts[:, 0]
        other_ref[:, rows, :] = parts[:, 1]

    @pl.when(core != 0)
    def _():
        mine_ref[:, rows, :] = parts[:, 1]
        other_ref[:, rows, :] = parts[:, 0]


def down_kernel(
    scal, hidden_ref, low_ref, high_ref, after_ref, vec_ref, out_ref, wcopy_ref, token_ref, down_ref, sem
):
    load_weights(scal[1], low_ref, high_ref, down_ref, wcopy_ref, sem, token_ref)
    total = dot(hidden_ref[0], down_ref[0], NT)
    for j in range(1, 4):
        total = total + dot(hidden_ref[j], down_ref[j], NT)
    out_ref[0] = (after_ref[...] + total + vec_ref[5:6, :]).astype(BF)


def mlp_kernel(
    scal, gp_ref, down_ref, up_ref, n2_ref, g_ref, after_any, vec_ref, mixed_any,
    ga_ref, galow_ref, mine_ref, other_ref, gb_ref, gn_ref, token_ref,
    dn2_acc, n2t_ref, gpre_ref, after_ref, mixed_ref, sem,
):
    j = pl.program_id(0)
    grids = g_ref.shape[0]
    core = scal[1]
    late = (
        pltpu.make_async_copy(after_any, after_ref, sem.at[0]),
        pltpu.make_async_copy(mixed_any, mixed_ref, sem.at[1]),
    )

    @pl.when(j == 0)
    def _():
        for copy in late:
            copy.start()
        for n in range(grids):
            rows = slice(n * CELLS, (n + 1) * CELLS)
            n2t_ref[:, rows] = n2_ref[rows, :].T
        dn2_acc[...] = jnp.zeros_like(dn2_acc)
        gb_ref[...] = jnp.zeros_like(gb_ref)
        gn_ref[...] = jnp.zeros_like(gn_ref)
        token_ref[...] = jnp.zeros_like(token_ref)

    @pl.when(j < 4)
    def _():
        colsum = jnp.zeros((1, D), F32)
        for n in range(grids):
            rows = slice(n * CELLS, (n + 1) * CELLS)
            gh = dot(g_ref[n], down_ref[0])
            gpre = (gh * gp_ref[0, rows, :].astype(F32)).astype(BF)
            gpre_ref[rows, :] = gpre
            colsum = colsum + jnp.sum(gpre.astype(F32), axis=0, keepdims=True)
        for n in range(grids):
            rows = slice(n * CELLS, (n + 1) * CELLS)
            dn2_acc[rows, :] += dot(gpre_ref[rows, :], up_ref[0], NT)
        gb_ref[pl.ds(j, 1), :] = colsum
        keep(core, 0, dot(n2t_ref[...], gpre_ref[...]).astype(BF), mine_ref, other_ref)

    @pl.when(j == 4)
    def _():
        for copy in late:
            copy.wait()
        sums = [jnp.zeros((1, D), F32)] * 4
        for n in range(grids):
            rows = slice(n * CELLS, (n + 1) * CELLS)
            u, rstd = norm_stats(after_ref[rows, :])
            c = dn2_acc[rows, :]
            g = g_ref[n].astype(F32)
            ga = g + norm_back(c, vec_ref[3:4, :], u, rstd)
            ga_ref[rows, :] = ga
            galow = ga.astype(BF)
            galow_ref[rows, :] = galow
            n2t_ref[:, rows] = galow.T
            parts = (ga, c * u, c, g)
            sums = [s + jnp.sum(v, axis=0, keepdims=True) for s, v in zip(sums, parts)]
        for i in range(4):
            gn_ref[2 + i : 3 + i, :] = sums[i]
        keep(core, 0, dot(n2t_ref[...], mixed_ref[...]).astype(BF), mine_ref, other_ref)


def attention_backward_kernel(
    scal, crop, ga_ref, galow_ref, mixed_ref, p_ref, q_ref, k_ref, v_ref, emb_ref, n1_ref,
    w_ref, vec_ref, gn_ref, gb_ref,
    ig_ref, table_out, gs_out, mine_ref, other_ref, token_ref,
    dm_ref, ds_ref, dq_all, dk_all, dv_all, n1t_ref, table_ref, gs_ref,
):
    i = pl.program_id(0)
    grids = pl.num_programs(0) - 1
    core = scal[1]

    @pl.when(i == 0)
    def _():
        table_ref[...] = jnp.zeros_like(table_ref)
        gs_ref[...] = jnp.zeros_like(gs_ref)
        token_ref[...] = jnp.zeros_like(token_ref)

    @pl.when(i < grids)
    def _():
        grid = scal[0] + i
        height, breadth, top, left = crop[grid, 0], crop[grid, 1], crop[grid, 2], crop[grid, 3]
        here = pl.ds(pl.multiple_of(i * CELLS, CELLS), CELLS)
        n1t_ref[:, here] = n1_ref[...].T
        dm_ref[...] = dot(galow_ref[...], w_ref[3]).astype(BF)
        outs = [[None] * (D // 128) for _ in range(3)]
        for h in range(HEADS):
            first, tiles = head_window(h)
            lanes = slice(first * 128, (first + tiles) * 128)
            mask = head_mask(h)
            dmh = jnp.where(mask, dm_ref[:, lanes], 0).astype(BF)
            dp = dot(dmh, v_ref[:, lanes], NT)
            delta = jnp.sum(
                dmh.astype(F32) * mixed_ref[:, lanes].astype(F32), axis=-1, keepdims=True
            )
            ds_ref[h] = (p_ref[0, h].astype(F32) * (dp - delta)).astype(BF)
        for h in range(HEADS):
            first, tiles = head_window(h)
            lanes = slice(first * 128, (first + tiles) * 128)
            mask = head_mask(h)
            qh = jnp.where(mask, q_ref[:, lanes], 0).astype(BF)
            kh = jnp.where(mask, k_ref[:, lanes], 0).astype(BF)
            dmh = jnp.where(mask, dm_ref[:, lanes], 0).astype(BF)
            ds = ds_ref[h]
            got = (dot(ds, kh), dot(ds, qh, TN), dot(p_ref[0, h], dmh, TN))
            for o in range(3):
                for t in range(tiles):
                    part = got[o][:, t * 128 : (t + 1) * 128]
                    at = first + t
                    outs[o][at] = part if outs[o][at] is None else outs[o][at] + part
        for t in range(D // 128):
            lanes = slice(t * 128, (t + 1) * 128)
            dq_all[here, lanes] = (outs[0][t] * SCALE).astype(BF)
            dk_all[here, lanes] = (outs[1][t] * SCALE).astype(BF)
            dv_all[here, lanes] = outs[2][t].astype(BF)
        dq, dk, dv = dq_all[here, :], dk_all[here, :], dv_all[here, :]
        c = dot(dq, w_ref[0], NT) + dot(dk, w_ref[1], NT) + dot(dv, w_ref[2], NT)
        u, rstd = norm_stats(emb_ref[...])
        ge = ga_ref[...] + norm_back(c, vec_ref[0:1, :], u, rstd)
        high = ge.astype(BF)
        ig_ref[0] = high
        low = (ge - high.astype(F32)).astype(BF)
        target = crop_target(
            lax.broadcasted_iota(jnp.int32, (CELLS, 1), 0), height, breadth, top, left
        )
        cell = lax.broadcasted_iota(jnp.int32, (CELLS, CELLS), 1)
        onehot = jnp.where(cell == target, 1.0, 0.0).astype(BF)
        table_ref[...] += dot(onehot, high) + dot(onehot, low)
        for row, v in enumerate((dq.astype(F32), dv.astype(F32), c * u, c)):
            gs_ref[row : row + 1, :] += jnp.sum(v, axis=0, keepdims=True)

    @pl.when(i == grids)
    def _():
        for b, ref in enumerate((dq_all, dk_all, dv_all)):
            keep(core, b, dot(n1t_ref[...], ref[...]).astype(BF), mine_ref, other_ref)
        table_out[...] = table_ref[...]
        gs_out[...] = gs_ref[...]
        start = 3 * HALF
        table = table_ref[...].astype(BF).reshape(OWNERS, 2, 16, D)
        norm = jnp.concatenate([gs_ref[2:4, :], gn_ref[2:6, :]], axis=0).astype(BF)
        split = jnp.concatenate([gs_ref[0:2, :], gb_ref[0:4, :]], axis=0).astype(BF)
        wide, thin = D // OWNERS, D // (4 * OWNERS)
        side = D // 2

        def small(ref, half):
            ref[:, start : start + 16, :] = table[:, half]
            ref[:, start + 16 : start + 32, :] = jnp.zeros((OWNERS, 16, D), BF)
            for dp in range(OWNERS):
                for x in range(2):
                    lane = x * side
                    ref[dp, start + 16 : start + 22, lane : lane + wide] = norm[
                        :, dp * wide : (dp + 1) * wide
                    ]
                    at = (2 * x + half) * (D // 4) + dp * thin
                    ref[dp, start + 24 : start + 30, lane : lane + thin] = split[:, at : at + thin]

        @pl.when(core == 0)
        def _():
            small(mine_ref, 0)
            small(other_ref, 1)

        @pl.when(core != 0)
        def _():
            small(mine_ref, 1)
            small(other_ref, 0)


def sds(shape, dtype):
    return jax.ShapeDtypeStruct(shape, dtype)


TOKEN = sds((8, 128), F32)


def in_hbm(shape):
    return pltpu.HBM(shape.shape, shape.dtype)


def behind(value, token):
    return lax.optimization_barrier((value, token))


ANY = pl.BlockSpec(memory_space=pl.ANY)


def half_shape(blocks, extra=0):
    return sds((OWNERS, blocks * HALF + extra, D), BF)


def whole_block(shape, buffers=None):
    zeros = (0,) * len(shape)
    mode = None if buffers is None else pl.Buffered(buffers)
    return pl.BlockSpec(shape, lambda i, *_: zeros, pipeline_mode=mode)


def attention_forward(scal, crop, x, mine, other, grids, deps=()):
    tokens = grids * CELLS
    rows = pl.BlockSpec((CELLS, D), lambda i, *_: (i, 0))
    spec = pltpu.PrefetchScalarGridSpec(
        num_scalar_prefetch=2,
        grid=(grids,),
        in_specs=[
            pl.BlockSpec((1, CELLS, D), lambda i, s, c: (s[0] + i, 0, 0)),
            whole_block(mine.shape, 1),
            whole_block(mine.shape, 1),
        ] + [ANY] * len(deps),
        out_specs=[
            rows, rows, rows, rows, rows,
            pl.BlockSpec((1, HEADS, CELLS, CELLS), lambda i, *_: (i, 0, 0, 0)),
            rows, rows, rows,
            pl.BlockSpec(memory_space=pl.ANY),
            whole_block((16, D)),
            whole_block((8, 128)),
        ],
        scratch_shapes=[
            pltpu.VMEM((4, D, D), BF), pltpu.VMEM((CELLS, D), BF), pltpu.SemaphoreType.DMA,
        ],
    )
    low, full = pltpu.HBM((tokens, D), BF), pltpu.HBM((tokens, D), F32)
    return pl.pallas_call(
        ignoring(attention_forward_kernel, 5, len(deps)),
        grid_spec=spec,
        out_shape=[
            full, low, low, low, low, pltpu.HBM((grids, HEADS, CELLS, CELLS), BF), low, full,
            sds((tokens, D), BF), pltpu.HBM((4, D, D), BF), sds((16, D), F32), TOKEN,
        ],
        compiler_params=params(40 * MIB),
        cost_estimate=NO_COST,
        name="attention_forward",
    )(scal, crop, x, mine, other, *deps)


def up_forward(scal, n2, mine, other, vec, cotangent, grids, deps=()):
    tokens = grids * CELLS
    block = pl.BlockSpec((1, tokens, D), lambda j, *_: (j, 0, 0))
    half = pl.BlockSpec((OWNERS, HALF, D), lambda j, *_: (0, j, 0))
    spec = pltpu.PrefetchScalarGridSpec(
        num_scalar_prefetch=1,
        grid=(4,),
        in_specs=[
            whole_block((tokens, D), 1),
            whole_block((2 * D, D), 1),
            whole_block((2 * D, D), 1),
            whole_block((16, D)),
            pl.BlockSpec((grids, CELLS, D), lambda j, s: (s[2], 0, 0), pipeline_mode=pl.Buffered(1)),
        ] + [ANY] * len(deps),
        out_specs=[block, block, half, half, pl.BlockSpec(memory_space=pl.ANY), whole_block((8, 128))],
        scratch_shapes=[
            pltpu.VMEM((D, tokens), BF), pltpu.VMEM((4, D, D), BF), pltpu.SemaphoreType.DMA,
        ],
    )
    return pl.pallas_call(
        ignoring(up_kernel, 6, len(deps)),
        grid_spec=spec,
        out_shape=[
            sds((4, tokens, D), BF), pltpu.HBM((4, tokens, D), BF), half_shape(4), in_hbm(half_shape(4)),
            pltpu.HBM((4, D, D), BF), TOKEN,
        ],
        compiler_params=params(40 * MIB * tokens // 768),
        cost_estimate=NO_COST,
        name="up_forward",
    )(scal, n2, mine, other, vec, cotangent, *deps)


def down_forward(scal, hidden, mine, other, after, vec, grids, deps=()):
    tokens = grids * CELLS
    spec = pltpu.PrefetchScalarGridSpec(
        num_scalar_prefetch=1,
        grid=(grids,),
        in_specs=[
            pl.BlockSpec((4, CELLS, D), lambda i, *_: (0, i, 0)),
            whole_block((2 * D, D), 1),
            whole_block((2 * D, D), 1),
            pl.BlockSpec((CELLS, D), lambda i, *_: (i, 0)),
            whole_block((16, D)),
        ] + [ANY] * len(deps),
        out_specs=[
            pl.BlockSpec((1, CELLS, D), lambda i, *_: (i, 0, 0)),
            pl.BlockSpec(memory_space=pl.ANY),
            whole_block((8, 128)),
        ],
        scratch_shapes=[pltpu.VMEM((4, D, D), BF), pltpu.SemaphoreType.DMA],
    )
    return pl.pallas_call(
        ignoring(down_kernel, 6, len(deps)),
        grid_spec=spec,
        out_shape=[pltpu.HBM((grids, CELLS, D), BF), pltpu.HBM((4, D, D), BF), TOKEN],
        compiler_params=params(24 * MIB),
        cost_estimate=NO_COST,
        name="down_forward",
    )(scal, hidden, mine, other, after, vec, *deps)


def mlp_backward(scal, gp, down, up, n2, cotangent, after, vec, mixed, grids, deps=()):
    tokens = grids * CELLS
    last = lambda j: jnp.minimum(j, 3)
    block = pl.BlockSpec((1, tokens, D), lambda j, *_: (last(j), 0, 0))
    weight = pl.BlockSpec((1, D, D), lambda j, *_: (last(j), 0, 0))
    half = pl.BlockSpec((OWNERS, HALF, D), lambda j, *_: (0, j, 0))
    rows = whole_block((tokens, D))
    any_spec = pl.BlockSpec(memory_space=pl.ANY)
    spec = pltpu.PrefetchScalarGridSpec(
        num_scalar_prefetch=1,
        grid=(5,),
        in_specs=[
            block, weight, weight, whole_block((tokens, D), 1),
            pl.BlockSpec((grids, CELLS, D), lambda j, s: (s[2], 0, 0), pipeline_mode=pl.Buffered(1)),
            any_spec, whole_block((16, D)), any_spec,
        ] + [ANY] * len(deps),
        out_specs=[rows, rows, half, half, whole_block((8, D)), whole_block((8, D)), whole_block((8, 128))],
        scratch_shapes=[
            pltpu.VMEM((tokens, D), F32), pltpu.VMEM((D, tokens), BF), pltpu.VMEM((tokens, D), BF),
            pltpu.VMEM((tokens, D), F32), pltpu.VMEM((tokens, D), BF),
            pltpu.SemaphoreType.DMA((2,)),
        ],
    )
    return pl.pallas_call(
        ignoring(mlp_kernel, 9, len(deps)),
        grid_spec=spec,
        out_shape=[
            sds((tokens, D), F32), sds((tokens, D), BF),
            half_shape(5), in_hbm(half_shape(5)), sds((8, D), F32), sds((8, D), F32), TOKEN,
        ],
        compiler_params=params(40 * MIB * tokens // 768),
        cost_estimate=NO_COST,
        name="mlp_backward",
    )(scal, gp, down, up, n2, cotangent, after, vec, mixed, *deps)


def attention_backward(scal, crop, ga, galow, mixed, p, q, k, v, emb, n1, w, vec, gn, gb, grids, deps=()):
    tokens = grids * CELLS
    last = lambda i: jnp.minimum(i, grids - 1)
    rows = pl.BlockSpec((CELLS, D), lambda i, *_: (last(i), 0))
    half = half_shape(3, SMALL)
    few = whole_block((8, D))
    spec = pltpu.PrefetchScalarGridSpec(
        num_scalar_prefetch=2,
        grid=(grids + 1,),
        in_specs=[
            rows, rows, rows,
            pl.BlockSpec((1, HEADS, CELLS, CELLS), lambda i, *_: (last(i), 0, 0, 0)),
            rows, rows, rows, rows, rows,
            whole_block((4, D, D), 1),
            whole_block((16, D)), few, few,
        ] + [ANY] * len(deps),
        out_specs=[
            pl.BlockSpec((1, CELLS, D), lambda i, *_: (last(i), 0, 0)),
            whole_block((CELLS, D)),
            few,
            whole_block(half.shape, 1), whole_block(half.shape, 1),
            whole_block((8, 128)),
        ],
        scratch_shapes=[pltpu.VMEM((CELLS, D), BF), pltpu.VMEM((HEADS, CELLS, CELLS), BF)]
        + [pltpu.VMEM((tokens, D), BF)] * 3
        + [pltpu.VMEM((D, tokens), BF), pltpu.VMEM((CELLS, D), F32), pltpu.VMEM((8, D), F32)],
    )
    return pl.pallas_call(
        ignoring(attention_backward_kernel, 15, len(deps)),
        grid_spec=spec,
        out_shape=[
            pltpu.HBM((grids, CELLS, D), BF), sds((CELLS, D), F32), sds((8, D), F32), half, in_hbm(half), TOKEN,
        ],
        compiler_params=params(40 * MIB),
        cost_estimate=NO_COST,
        name="attention_backward",
    )(scal, crop, ga, galow, mixed, p, q, k, v, emb, n1, w, vec, gn, gb, *deps)


class Place:
    def __init__(self, dp_size, mp_size):
        self.z_size = dp_size // 2
        dp, mp = lax.axis_index("dp"), lax.axis_index("mp")
        self.dp, self.mp = dp, mp
        self.z, self.y = dp // 2, dp % 2
        self.x, self.c = mp // 2, mp % 2
        self.core_pairs = [(i, i ^ 1) for i in range(mp_size)]
        self.x_pairs = [(i, i ^ 2) for i in range(mp_size)]
        self.y_pairs = [(i, i ^ 1) for i in range(dp_size)]
        self.z_shift = [
            [(i, ((i // 2 + s) % self.z_size) * 2 + i % 2) for i in range(dp_size)]
            for s in range(self.z_size)
        ]

        self.corner_pairs = [
            (d * mp_size + m, (d ^ 1) * mp_size + (m ^ 2))
            for d in range(dp_size)
            for m in range(mp_size)
        ]

    def core(self, v):
        return lax.ppermute(v, "mp", self.core_pairs)

    def over_corner(self, v):
        return lax.ppermute(v, ("dp", "mp"), self.corner_pairs)

    def over_x(self, v):
        return lax.ppermute(v, "mp", self.x_pairs)

    def over_y(self, v):
        return lax.ppermute(v, "dp", self.y_pairs)

    def over_z(self, v, shift):
        return lax.ppermute(v, "dp", self.z_shift[shift])


def ignoring(kernel, at, count):
    return lambda *refs: kernel(*refs[:at], *refs[at + count :])


def assemble_kernel(rows, extra, depth, views, where, *refs):
    count = 1 + max(at for at, _ in views)
    out, token = refs[count:]
    token[...] = jnp.zeros_like(token)
    z, y, x = where[0], where[1], where[2]
    unit = rows + extra
    held = [(refs[at], row) for at, row in views]
    for s in range(depth):
        zs = lax.rem(z - s + depth, depth)
        for xr in range(2):
            for yr in range(2):
                xs = x if xr == 0 else 1 - x
                ys = y if yr == 0 else 1 - y
                dp = zs * 2 + ys
                lane = pl.ds(pl.multiple_of(xs * (D // 2), D // 2), D // 2)
                for b in range(2):
                    if xr and yr:
                        ref, first = held[3 + b]
                        first += s * unit
                    else:
                        ref, first = held[xr + 2 * yr]
                        first += (b * depth + s) * unit
                    row = pl.ds(pl.multiple_of(b * D + dp * rows, rows), rows)
                    out[row, lane] = ref[first : first + rows, :]
                    if extra:
                        at = 2 * D + b * depth * 2 * extra + dp * extra
                        row = pl.ds(pl.multiple_of(at, extra), extra)
                        out[row, lane] = ref[first + rows : first + unit, :]


def assemble(where, views, pieces, extra, dp_size, deps=()):
    kernel = functools.partial(assemble_kernel, D // dp_size, extra, dp_size // 2, views)
    shape = sds((2 * D + 2 * dp_size * extra, D), BF)
    return call(kernel, "assemble", where, pieces, [shape], deps)


def gather_z(place, u):
    return [u] + [place.over_z(u, s) for s in range(1, place.z_size)]


def call(kernel, name, where, ins, shapes, deps=(), limit=16):
    vmem = pl.BlockSpec(memory_space=pltpu.VMEM)
    return pl.pallas_call(
        ignoring(kernel, 1 + len(ins), len(deps)),
        in_specs=[pl.BlockSpec(memory_space=pltpu.SMEM)] + [vmem] * len(ins) + [ANY] * len(deps),
        out_specs=[vmem] * (len(shapes) + 1),
        out_shape=[*shapes, TOKEN],
        compiler_params=params(limit * MIB),
        cost_estimate=NO_COST,
        name=name,
    )(where, *ins, *deps)


def pack_kernel(count, has_next, unit_at, where, *refs):
    parts, refs = refs[:count], refs[count:]
    half, lows = 0, None
    if has_next:
        by_x, by_y, refs = refs[0], refs[1], refs[2:]
        half = has_next
    token = refs[-1]
    token[...] = jnp.zeros_like(token)
    outs = refs[:-1]
    if unit_at:
        units, outs = outs[0], outs[1:]
        outs[-1][...] = units[unit_at]
        outs = outs[:-1]
    if half:
        first_x, first_y = half[0], half[1]
        size = half[2]
        outs[-2][:size, :] = by_x[first_x : first_x + size, :]
        outs[-1][:size, :] = by_y[first_y : first_y + size, :]
    if count:
        unit = parts[0].shape[1]
        for b in range(2):
            for s in range(count):
                value = parts[s][b]
                at = (b * count + s) * unit
                outs[0][at : at + unit, :] = value
                if half:
                    outs[-2][size + at : size + at + unit, :] = value
                    outs[-1][size + at : size + at + unit, :] = value


def pack(where, parts, by_x, by_y, half, units=None, unit_at=0, deps=()):
    count = len(parts)
    shapes = []
    rows = 2 * count * parts[0].shape[1] if count else 0
    if count:
        shapes.append(sds((rows, D // 2), BF))
    ins = list(parts)
    if half:
        ins += [by_x, by_y]
        shapes += [sds((half[2] + rows, D // 2), BF)] * 2
    if unit_at:
        ins.append(units)
        shapes.append(sds(units.shape[1:], BF))
    kernel = functools.partial(pack_kernel, count, half, unit_at)
    return call(kernel, "pack", where, ins, shapes, deps)


def add(a, b):
    return a.astype(F32) + b.astype(F32)


def dp_of(z, y):
    return z * 2 + y


def split_y(y, value_at, depth, send, keep):
    for z in range(depth):
        send[z] = value_at(dp_of(z, 1 - y)).astype(BF)
        keep[z] = value_at(dp_of(z, y)).astype(BF)


def split_x(x, value, send, keep):
    side = D // 2
    left, right = value[:, :side].astype(BF), value[:, side:].astype(BF)

    @pl.when(x == 0)
    def _():
        send[...] = right
        keep[...] = left

    @pl.when(x != 0)
    def _():
        send[...] = left
        keep[...] = right


def first_y_kernel(where, mine, got, send, keep, token):
    token[...] = jnp.zeros_like(token)
    split_y(where[1], lambda dp: add(mine[dp], got[dp]), OWNERS // 2, send, keep)


def first_y(where, mine, got, deps=()):
    rows = mine.shape[1]
    shape = sds((OWNERS // 2, rows, D), BF)
    return call(first_y_kernel, "first_y", where, [mine, got], [shape, shape], deps)


def first_both_kernel(cut, where, mine, got, send_y, keep_y, send_x, keep_x, token):
    token[...] = jnp.zeros_like(token)
    depth = OWNERS // 2
    split_y(where[1], lambda dp: add(mine[dp, :cut], got[dp, :cut]), depth, send_y, keep_y)
    for dp in range(OWNERS):
        split_x(where[2], add(mine[dp, cut:], got[dp, cut:]), send_x.at[dp], keep_x.at[dp])


def first_both(where, mine, got, deps=()):
    rows = mine.shape[1]
    cut = (2 * rows // 3) // 16 * 16
    over_y = sds((OWNERS // 2, cut, D), BF)
    over_x = sds((OWNERS, rows - cut, D // 2), BF)
    kernel = functools.partial(first_both_kernel, cut)
    return call(kernel, "first_both", where, [mine, got], [over_y, over_y, over_x, over_x], deps)


def first_x_kernel(where, mine, got, send, keep, token):
    token[...] = jnp.zeros_like(token)
    for dp in range(OWNERS):
        split_x(where[2], add(mine[dp], got[dp]), send.at[dp], keep.at[dp])


def first_x(where, mine, got, deps=()):
    shape = sds((OWNERS, mine.shape[1], D // 2), BF)
    return call(first_x_kernel, "first_x", where, [mine, got], [shape, shape], deps)


def second_y_kernel(where, mine, got, send, keep, token):
    token[...] = jnp.zeros_like(token)
    split_y(where[1], lambda dp: add(mine[dp], got[dp]), OWNERS // 2, send, keep)


def second_y(where, mine, got, deps=()):
    shape = sds((OWNERS // 2,) + mine.shape[1:], BF)
    return call(second_y_kernel, "second_y", where, [mine, got], [shape, shape], deps)


def second_both_kernel(where, keep_y, got_y, keep_x, got_x, send_a, left_a, send_b, left_b, token):
    token[...] = jnp.zeros_like(token)
    depth = OWNERS // 2
    for z in range(depth):
        split_x(where[2], add(keep_y[z], got_y[z]), send_a.at[z], left_a.at[z])
    split_y(where[1], lambda dp: add(keep_x[dp], got_x[dp]), depth, send_b, left_b)


def second_both(where, keep_y, got_y, keep_x, got_x, deps=()):
    over_x = sds((OWNERS // 2, keep_y.shape[1], D // 2), BF)
    over_y = sds((OWNERS // 2, keep_x.shape[1], D // 2), BF)
    ins = [keep_y, got_y, keep_x, got_x]
    return call(second_both_kernel, "second_both", where, ins, [over_x, over_x, over_y, over_y], deps)


def split_z_kernel(pairs, where, *refs):
    ins, outs = refs[: 2 * pairs], refs[2 * pairs : -1]
    refs[-1][...] = jnp.zeros_like(refs[-1])
    depth = ins[0].shape[0]
    for s in range(depth):
        z = lax.rem(where[0] + s, depth)
        row = 0
        for i in range(pairs):
            value = add(ins[2 * i][z], ins[2 * i + 1][z]).astype(BF)
            outs[s][row : row + value.shape[0], :] = value
            row += value.shape[0]


def split_z(where, *ins, deps=()):
    depth, width = ins[0].shape[0], ins[0].shape[2]
    rows = sum(v.shape[1] for v in ins[::2])
    kernel = functools.partial(split_z_kernel, len(ins) // 2)
    return call(kernel, "split_z", where, list(ins), [sds((rows, width), BF)] * depth, deps)


def z_to_x_kernel(where, keep, *refs):
    got, (send, left, token) = refs[:-3], refs[-3:]
    token[...] = jnp.zeros_like(token)
    total = keep[...].astype(F32)
    for ref in got:
        total = total + ref[...].astype(F32)
    split_x(where[2], total, send, left)


def z_to_x(where, keep, got, deps=()):
    shape = sds((keep.shape[0], D // 2), BF)
    return call(z_to_x_kernel, "z_to_x", where, [keep, *got], [shape, shape], deps)


def pair_kernel(where, own, by_x, out, token):
    token[...] = jnp.zeros_like(token)
    out[0] = own[...]
    out[1] = by_x[...]


def collect_kernel(where, here, there, out, token):
    token[...] = jnp.zeros_like(token)
    x, c = where[2], where[3]
    grids = here.shape[1]
    for piece, core in ((here, c), (there, 1 - c)):
        for half in range(2):
            mp = 2 * (x if half == 0 else 1 - x) + core
            for n in range(grids):
                out[mp * grids + n] = piece[half, n]


def pair_grids(where, own, by_x, deps=()):
    return call(pair_kernel, "pair", where, [own, by_x], [sds((2,) + own.shape, own.dtype)], deps)


def finish_grids(where, here, there, deps=()):
    shape = sds((here.shape[0] * 2 * here.shape[1],) + here.shape[2:], here.dtype)
    return call(collect_kernel, "collect", where, [here, there], [shape], deps)


def plane_kernel(where, own, by_x, by_y, by_corner, out, token):
    token[...] = jnp.zeros_like(token)
    out[0:16, :] = own[0:16, :]
    out[16:32, :] = by_x[0:16, :]
    here = own[16:24, :] + by_x[16:24, :]
    out[32:40, :] = here + (by_y[...] + by_corner[...])


def sum_plane(place, where, packed, square):
    ins = [packed, place.over_x(packed), place.over_y(square), place.over_corner(square)]
    here, _ = call(plane_kernel, "plane", where, ins, [sds((40, D // 2), F32)])
    there = place.core(here)
    value = here[32:40, :128] + there[32:40, :128]
    return here, there, [value] + [place.over_z(value, s) for s in range(1, place.z_size)]


ROWS1, ROWS2, ROWS3 = 4 * HALF, 5 * HALF, 3 * HALF
ROWS = ROWS1 + ROWS2 + ROWS3


def totals_kernel(where, *refs):
    keep1, got1, keep2, *got2 = refs[:6]
    keep3, *got3 = refs[6:10]
    kept_ref, sent_ref, tail_ref, packed_ref, square_ref, token = refs[10:]
    token[...] = jnp.zeros_like(token)
    x, c = where[2], where[3]

    def total(first, others):
        value = first[...].astype(F32)
        for ref in others:
            value = value + ref[...].astype(F32)
        return value

    whole3 = total(keep3, got3)
    parts = (total(keep1, [got1]), total(keep2, got2), whole3[:ROWS3])
    wide = D // 4
    row = 0
    square = jnp.zeros((1, D // 2), F32)
    for value in parts:
        rows = slice(row, row + value.shape[0])
        left, right = value[:, :wide], value[:, wide:]

        @pl.when(c == 0)
        def _():
            kept_ref[rows, :] = left
            sent_ref[rows, :] = right

        @pl.when(c != 0)
        def _():
            kept_ref[rows, :] = right
            sent_ref[rows, :] = left

        square = square + jnp.sum(value * value, axis=0, keepdims=True)
        row += value.shape[0]
    tail = whole3[ROWS3:]
    tail_ref[...] = tail
    lane = lax.broadcasted_iota(jnp.int32, (16, D // 2), 1)
    line = lax.broadcasted_iota(jnp.int32, (16, D // 2), 0)
    owner = jnp.where((x == 0) & (c == 0), 1.0, 0.0)
    codes = tail[16:32]
    small = jnp.where(line < 8, jnp.where(lane < D // OWNERS, codes * owner, 0.0), 0.0)
    small = jnp.where((line >= 8) & (lane < D // (4 * OWNERS)), codes, small)
    square = square + jnp.sum(tail[:16] * tail[:16] + small * small, axis=0, keepdims=True)
    square_ref[...] = jnp.full((8, D // 2), jnp.sum(square), F32)
    packed_ref[0:16, :] = tail[:16]
    packed_ref[16:24, :] = square_ref[...]


def totals(where, keep1, got1, keep2, got2, keep3, got3, deps=()):
    ins = [keep1, got1, keep2, *got2, keep3, *got3]
    half = sds((ROWS, D // 4), F32)
    shapes = [half, half] + [sds((rows, D // 2), F32) for rows in (SMALL, 24, 8)]
    return call(totals_kernel, "totals", where, ins, shapes, deps)


def update_kernel(where, *refs):
    kept, got, tail, plane, other_plane = refs[:5]
    squares = refs[5:9]
    state, outs = refs[9:24], refs[24:]
    x, c = where[2], where[3]
    square = (squares[0][0:1, 0:1] + squares[2][0:1, 0:1]) + (
        squares[1][0:1, 0:1] + squares[3][0:1, 0:1]
    )
    norm = jnp.sqrt(square)
    factor = jnp.minimum(1.0, CLIP_LIMIT / (norm + 1e-06))
    outs[0][...] = norm

    def step(at, index, gradient, rate, decay):
        weight, first, second = (state[at + 5 * i][index] for i in range(3))
        new = adam_step(weight, gradient, first, second, rate, decay)
        for i in range(3):
            outs[1 + at + 5 * i][index] = new[i]

    def block(row):
        rows = slice(row, row + HALF)
        own, other = kept[rows, :], got[rows, :]
        top = jnp.where(c == 0, own, other)
        bottom = jnp.where(c == 0, other, own)
        return jnp.concatenate([top, bottom], axis=0) * factor

    front = [ROWS1 + ROWS2 + HALF * b for b in range(3)] + [ROWS1 + HALF * b for b in range(4)]
    for b, row in enumerate(front):
        step(0, b, block(row), RATE_MATRIX, DECAY_RATE)
    back = [ROWS1 + 4 * HALF] + [HALF * b for b in range(4)]
    for b, row in enumerate(back):
        step(1, b, block(row).T, RATE_MATRIX, DECAY_RATE)
    norm_grad = tail[16:22, : D // OWNERS] * factor
    outs[16][...] = norm_grad
    step(3, Ellipsis, norm_grad, RATE_VECTOR, 0.0)
    step(2, Ellipsis, tail[24:30, : D // (4 * OWNERS)] * factor, RATE_VECTOR, 0.0)
    own, by_x = plane[0:16, :], plane[16:32, :]
    by_core, by_both = other_plane[0:16, :], other_plane[16:32, :]
    here = jnp.concatenate(
        [jnp.where(c == 0, own, by_core), jnp.where(c == 0, by_core, own)], axis=0
    )
    there = jnp.concatenate(
        [jnp.where(c == 0, by_x, by_both), jnp.where(c == 0, by_both, by_x)], axis=0
    )
    side = D // 2
    for half in range(2):
        gradient = jnp.where(x == half, here, there) * factor
        lanes = (slice(None), slice(half * side, (half + 1) * side))
        step(4, lanes, gradient, RATE_TABLE, DECAY_RATE)


def update(where, kept, got, tail, here, there, squares, state, deps):
    vmem = pl.BlockSpec(memory_space=pltpu.VMEM)
    ins = [kept, got, tail, here, there, *squares, *state]
    shapes = [sds((1, 1), F32)] + [sds(v.shape, F32) for v in state] + [sds(state[3].shape, F32)]
    return pl.pallas_call(
        ignoring(update_kernel, 1 + len(ins), len(deps)),
        in_specs=[pl.BlockSpec(memory_space=pltpu.SMEM)] + [vmem] * len(ins) + [ANY] * len(deps),
        out_specs=[vmem] * len(shapes),
        out_shape=shapes,
        compiler_params=params(24 * MIB),
        cost_estimate=NO_COST,
        name="update",
    )(where, *ins, *deps)


def adam_step(weight, gradient, first, second, rate, decay):
    first_new = BETA_FIRST * first + (1.0 - BETA_FIRST) * gradient
    second_new = BETA_SECOND * second + (1.0 - BETA_SECOND) * gradient * gradient
    first_hat = first_new / (1.0 - BETA_FIRST**STEP)
    second_hat = second_new / (1.0 - BETA_SECOND**STEP)
    weight_new = weight - rate * (first_hat / (jnp.sqrt(second_hat) + ADAM_EPS) + decay * weight)
    return (weight_new, first_new, second_new)


def body(
    dp_size, mp_size,
    block_input, cotangent, crop_boxes, front_weights, back_weights, split_biases, norm_params,
    pos_table, front_first, back_weight_first_moment, split_first, norm_first, table_first,
    front_second, back_second, split_second, norm_second, table_second,
):
    place = Place(dp_size, mp_size)
    direct = dp_size == 8 and mp_size == 4
    x, y, z, c = place.x, place.y, place.z, place.c
    grids = block_input.shape[0] // mp_size
    scal = jnp.stack([place.mp * grids, c, place.mp, place.dp]).astype(jnp.int32)
    where = jnp.stack([z, y, x, c]).astype(jnp.int32)
    turned = jnp.swapaxes(back_weights, 1, 2).astype(BF)
    low_front = front_weights.astype(BF)
    rows, lanes = low_front.shape[1], low_front.shape[2]

    if direct:
        shards = jnp.concatenate([low_front[:3], turned[:1], low_front[3:], turned[1:]])
        shards = shards.reshape(3, 2, 2, rows, lanes)
        mine = lax.dynamic_index_in_dim(shards, c, axis=1, keepdims=False)
        sent = lax.dynamic_index_in_dim(shards, 1 - c, axis=1, keepdims=False)
        got = place.core(sent)
        units = jnp.where(
            c == 0, jnp.concatenate([mine, got], -1), jnp.concatenate([got, mine], -1)
        )
        extra = pos_table.shape[0] // 2
        half = jnp.where(c == 0, pos_table[:extra], pos_table[extra:]).astype(BF)
        half = jnp.where(x == 0, half[:, : D // 2], half[:, D // 2 :])
        packed = jnp.zeros((extra, D // 2), BF)
        packed = lax.dynamic_update_slice(packed, norm_params.astype(BF), (0, 0))
        packed = lax.dynamic_update_slice(packed, split_biases.astype(BF), (0, 128))
        first_unit = jnp.concatenate([units[0], jnp.stack([half, packed])], axis=1)
        own1, unit2, _ = pack(where, gather_z(place, first_unit), None, None, None, units, 1)
        x1, y1 = place.over_x(own1), place.over_y(own1)
        size1, size2 = own1.shape[0] // 2, units.shape[1] * units.shape[2] * place.z_size // 2
        own2, sent_y, sent_x, unit3, _ = pack(
            where, gather_z(place, unit2), x1, y1, (0, size1, size1), units, 2
        )
        y2, x2 = place.over_y(sent_y), place.over_x(sent_x)
        own3, sent_y, sent_x, token3 = pack(
            where, gather_z(place, unit3), x2, y2, (size1, size1 + size2, size2)
        )
        y3, x3 = place.over_y(sent_y), place.over_x(sent_x)
        attn_mine, _ = assemble(
            where, ((0, 0), (1, 0), (2, 0), (4, 0), (3, 0)), (own1, x1, y1, x2, y2), extra, dp_size,
            (token3,),
        )
        attn_other = place.core(attn_mine)
        first_deps = (token3,)
    else:

        def halves(v):
            v = lax.all_gather(v, "dp", axis=1, tiled=True)
            v = lax.all_gather(v, "mp", axis=2, tiled=True).reshape(2, 2 * D, D)
            return jnp.where(c == 0, v[0], v[1]), jnp.where(c == 0, v[1], v[0])

        attn_mine, attn_other = halves(jnp.concatenate([low_front[:3], turned[:1]]))
        up_pair, down_pair = halves(low_front[3:]), halves(turned[1:])
        table = lax.all_gather(pos_table.astype(BF), "dp", axis=0, tiled=True)
        table = table.reshape(OWNERS, 2, CELLS // (2 * OWNERS), D)
        table = jnp.swapaxes(table, 0, 1).reshape(2, CELLS // 2, D)
        norms = lax.all_gather(norm_params.astype(BF), "dp", axis=1, tiled=True)
        splits = lax.all_gather(split_biases.astype(BF), ("mp", "dp"), axis=1, tiled=True)
        norms = jnp.swapaxes(norms.reshape(6, OWNERS, D // OWNERS), 0, 1)
        splits = jnp.transpose(splits.reshape(6, 2, 2, OWNERS, -1), (2, 3, 0, 1, 4))
        codes = jnp.zeros((2, OWNERS, CELLS // (2 * OWNERS), D), BF)
        codes = codes.at[:, :, 0:6, : norms.shape[2]].set(norms)
        for side in range(2):
            lane = side * (D // 2) + 128
            codes = codes.at[:, :, 0:6, lane : lane + splits.shape[4]].set(splits[:, :, :, side])
        table = jnp.concatenate([table, codes.reshape(2, -1, D)], axis=1)
        attn_mine = jnp.concatenate([attn_mine, jnp.where(c == 0, table[0], table[1])])
        attn_other = jnp.concatenate([attn_other, jnp.where(c == 0, table[1], table[0])])
        first_deps = ()

    emb, normed1, q, k, v, p, mixed, after, normed2, w_attn, vec, token = attention_forward(
        scal, crop_boxes, block_input, attn_mine, attn_other, grids, first_deps
    )
    deps = ()
    if direct:
        sent_y, sent_x, token4 = pack(where, [], x3, y3, (size2, 2 * size2, size2), deps=(token,))
        y4, x4 = place.over_y(sent_y), place.over_x(sent_x)
        half, _ = assemble(
            where, ((0, 0), (1, size1), (2, size1), (4, 0), (3, 0)), (own2, x2, y2, x3, y3), 0, dp_size,
            (token4,),
        )
        up_pair = half, place.core(half)
        deps = (token4,)
    hidden, gp, down_mine, down_other, w_up, token = up_forward(
        scal, normed2, *up_pair, vec, cotangent, grids, deps
    )
    if direct:
        half, token = assemble(
            where, ((0, 0), (1, size2), (2, size2), (4, 0), (3, 0)), (own3, x3, y3, x4, y4), 0, dp_size,
            (token,),
        )
        down_pair = half, place.core(half)
        down_other, token = behind(down_other, token)
        sent, keep1, token = first_y(where, down_mine, place.core(down_other))
        got1 = place.over_y(sent)
        deps = (token,)
    out, w_down, token = down_forward(scal, hidden, *down_pair, after, vec, grids, deps)
    if direct:
        out_x = place.over_x(out)
        deps = (token,)
    ga, galow, up_mine, up_other, gb, gn, token = mlp_backward(
        scal, gp, w_down, w_up, normed2, cotangent, after, vec, mixed, grids, deps
    )
    if direct:
        out_pair, token = pair_grids(where, out, out_x, (token,))
        keep1, *sent, token1 = split_z(where, keep1, got1, deps=(token,))
        got1 = [place.over_z(sent[s - 1], s) for s in range(1, place.z_size)]
        up_other, token1 = behind(up_other, token1)
        sent_x, keep2, token2 = first_x(where, up_mine, place.core(up_other), (token1,))
        got2 = place.over_x(sent_x)
        out_far = place.core(out_pair)
        deps = (token1, token2)
    ig, dtable, gs, mine3, other3, token = attention_backward(
        scal, crop_boxes, ga, galow, mixed, p, q, k, v, emb, normed1, w_attn, vec, gn, gb, grids, deps
    )
    cells_here, norm_here = pos_table.shape[0], norm_params.shape[1]
    split_here = split_biases.shape[1]
    if direct:
        sent1, keep1, token1 = z_to_x(where, keep1, got1, (token,))
        got1 = place.over_x(sent1)
        sent_y, keep2, token2 = second_y(where, keep2, got2, (token1,))
        got2 = place.over_y(sent_y)
        ig_x = place.over_x(ig)
        other3, token2 = behind(other3, token2)
        sent_y, keep3a, sent_x, keep3b, token3 = first_both(
            where, mine3, place.core(other3), (token1, token2)
        )
        got3a, got3b = place.over_y(sent_y), place.over_x(sent_x)
        block_output, token3 = finish_grids(where, out_pair, out_far, (token3,))
        keep2, *sent, token = split_z(where, keep2, got2, deps=(token3,))
        got2 = [place.over_z(sent[s - 1], s) for s in range(1, place.z_size)]
        sent_x, keep3a, sent_y, keep3b, token = second_both(
            where, keep3a, got3a, keep3b, got3b, (token,)
        )
        got3a, got3b = place.over_x(sent_x), place.over_y(sent_y)
        keep3, *sent, token = split_z(where, keep3a, got3a, keep3b, got3b, deps=(token, *got2))
        got3 = [place.over_z(sent[s - 1], s) for s in range(1, place.z_size)]
        ig_pair, token = pair_grids(where, ig, ig_x, (token,))
        input_grad, token = finish_grids(where, ig_pair, place.core(ig_pair))
        kept, sent, tail, packed, square, _ = totals(
            where, keep1, got1, keep2, got2, keep3, got3, (token,)
        )
        got = place.core(sent)
        here, there, squares = sum_plane(place, where, packed, square)
        state = (
            front_weights, back_weights, split_biases, norm_params, pos_table,
            front_first, back_weight_first_moment, split_first, norm_first, table_first,
            front_second, back_second, split_second, norm_second, table_second,
        )
        state = [pltpu.with_memory_space_constraint(v, pltpu.HBM) for v in state]
        new = update(where, kept, got, tail, here, there, squares, state, ())
        return (block_output, input_grad, new[0][0, 0], *new[1:])
    else:

        def share(mine, other, blocks):
            low, high = jnp.where(c == 0, mine, other), jnp.where(c == 0, other, mine)
            full = jnp.stack([low, high], 1)[:, :, : blocks * HALF].astype(F32)
            full = full.reshape(OWNERS, 2, blocks, HALF, D)
            full = jnp.transpose(full, (2, 0, 1, 3, 4)).reshape(blocks, D, D)
            full = lax.psum_scatter(full, "dp", scatter_dimension=1, tiled=True)
            return lax.psum_scatter(full, "mp", scatter_dimension=2, tiled=True)

        down_share = share(down_mine, down_other, 4)
        up_share = share(up_mine, up_other, 5)
        out_share, up_share = up_share[4:], up_share[:4]
        qkv_share = share(mine3, other3, 3)
        block_output = lax.all_gather(out, "mp", axis=0, tiled=True)
        input_grad = lax.all_gather(ig, "mp", axis=0, tiled=True)
        norm_grad = jnp.concatenate([gs[2:4], gn[2:6]])
        split_grad = jnp.concatenate([gs[0:2], gb[0:4]])
        dtable = lax.psum(dtable, ("dp", "mp"))
        norm_grad = lax.psum(norm_grad, ("dp", "mp"))
        split_grad = lax.psum(split_grad, ("dp", "mp"))
        table_share = lax.dynamic_slice(dtable, (place.dp * cells_here, 0), (cells_here, D))
        norm_share = lax.dynamic_slice(norm_grad, (0, place.dp * norm_here), (6, norm_here))
        split_share = lax.dynamic_slice(
            split_grad, (0, (place.mp * dp_size + place.dp) * split_here), (6, split_here)
        )
        table_square = jnp.sum(table_share * table_share) / mp_size
    front_share = jnp.concatenate([qkv_share, up_share])
    back_share = jnp.concatenate([out_share, down_share])
    owner = (place.mp == 0).astype(F32)
    square = (
        jnp.sum(qkv_share * qkv_share)
        + jnp.sum(out_share * out_share)
        + jnp.sum(up_share * up_share)
        + jnp.sum(down_share * down_share)
        + jnp.sum(split_share * split_share)
        + owner * jnp.sum(norm_share * norm_share)
        + table_square
    )
    clip_norm = jnp.sqrt(lax.psum(square, ("dp", "mp")))
    factor = jnp.minimum(1.0, CLIP_LIMIT / (clip_norm + 1e-06))
    norm_clipped = norm_share * factor
    new_front, front_first_new, front_second_new = adam_step(
        front_weights, front_share * factor, front_first, front_second, RATE_MATRIX, DECAY_RATE
    )
    new_back, back_first_new, back_second_new = adam_step(
        back_weights,
        jnp.swapaxes(back_share, 1, 2) * factor,
        back_weight_first_moment,
        back_second,
        RATE_MATRIX,
        DECAY_RATE,
    )
    new_split, split_first_new, split_second_new = adam_step(
        split_biases, split_share * factor, split_first, split_second, RATE_VECTOR, 0.0
    )
    new_norm, norm_first_new, norm_second_new = adam_step(
        norm_params, norm_clipped, norm_first, norm_second, RATE_VECTOR, 0.0
    )
    new_table, table_first_new, table_second_new = adam_step(
        pos_table, table_share * factor, table_first, table_second, RATE_TABLE, DECAY_RATE
    )
    return (
        block_output, input_grad, clip_norm,
        new_front, new_back, new_split, new_norm, new_table,
        front_first_new, back_first_new, split_first_new, norm_first_new, table_first_new,
        front_second_new, back_second_new, split_second_new, norm_second_new, table_second_new,
        norm_clipped,
    )


def solution(mesh):
    front, back = P(None, "dp", "mp"), P(None, "mp", "dp")
    split, norm, table = P(None, ("mp", "dp")), P(None, "dp"), P("dp", None)
    state = (front, back, split, norm, table)
    rows = P("dp", None, None)
    return jax.shard_map(
        functools.partial(body, mesh.shape["dp"], mesh.shape["mp"]),
        mesh=mesh,
        in_specs=(rows, rows, P("dp", None)) + state * 3,
        out_specs=(rows, rows, P()) + state * 3 + (norm,),
        check_vma=False,
    )
```

```python
import functools

import jax
import jax.numpy as jnp
from jax import lax
from jax.experimental import pallas as pl
from jax.experimental.pallas import tpu as pltpu
from jax.sharding import PartitionSpec as P

D = 768
HEADS = 16
HEAD = D // HEADS
SIDE = 16
CELLS = 256
STEP = 5
CORES = 2

NORM_EPS = 1e-05
BETA_FIRST = 0.9
BETA_SECOND = 0.95
ADAM_EPS = 1e-08
RATE_MATRIX = 0.05
RATE_TABLE = 0.2
RATE_VECTOR = 0.5
DECAY_RATE = 0.1
CLIP_LIMIT = 0.01
MASK_FILL = -1e30
SCALE = HEAD ** (-0.5)
LOG2E = 1.4426950408889634
INV_SQRT_2PI = 0.3989422804014327

OWNERS = 8
HALF = D // (2 * OWNERS)
SMALL = 32

BF = jnp.bfloat16
F32 = jnp.float32
MIB = 1024 * 1024
NN = (((1,), (0,)), ((), ()))
NT = (((1,), (1,)), ((), ()))
TN = (((0,), (0,)), ((), ()))


NO_COST = pl.CostEstimate(flops=0, bytes_accessed=0, transcendentals=0)


def dot(a, b, dims=NN):
    return lax.dot_general(a, b, dims, preferred_element_type=F32)


def params(limit):
    return pltpu.CompilerParams(vmem_limit_bytes=limit)


def norm_stats(v):
    mean = jnp.mean(v, axis=-1, keepdims=True)
    centred = v - mean
    spread = jnp.mean(centred * centred, axis=-1, keepdims=True)
    rstd = lax.rsqrt(spread + NORM_EPS)
    return centred * rstd, rstd


def norm_back(c, gain, u, rstd):
    cg = c * gain
    mean_cg = jnp.mean(cg, axis=-1, keepdims=True)
    mean_cgu = jnp.mean(cg * u, axis=-1, keepdims=True)
    return rstd * (cg - mean_cg - u * mean_cgu)


def head_window(h):
    low = h * HEAD
    first = low // 128
    last = (low + HEAD - 1) // 128
    return first, last + 1 - first


def head_mask(h):
    first, tiles = head_window(h)
    lane = lax.broadcasted_iota(jnp.int32, (1, tiles * 128), 1) + first * 128
    return (lane >= h * HEAD) & (lane < (h + 1) * HEAD)


def crop_target(position, height, breadth, top, left):
    row = (position >> 4) - top
    col = (position & (SIDE - 1)) - left
    inside = (row >= 0) & (row < height) & (col >= 0) & (col < breadth)
    return jnp.where(inside, row * breadth + col, -1)


def load_weights(core, mine_ref, other_ref, w_ref, copy_ref, sem, token_ref):
    copy = pltpu.make_async_copy(w_ref, copy_ref, sem)

    @pl.when(pl.program_id(0) == 0)
    def _():
        token_ref[...] = jnp.zeros_like(token_ref)

        def fill(low, high):
            for b in range(2):
                rows = slice(b * D, (b + 1) * D)
                w_ref[b] = low[rows, :]
                w_ref[2 + b] = high[rows, :]

        @pl.when(core == 0)
        def _():
            fill(mine_ref, other_ref)

        @pl.when(core != 0)
        def _():
            fill(other_ref, mine_ref)

        copy.start()

    @pl.when(pl.program_id(0) == pl.num_programs(0) - 1)
    def _():
        copy.wait()


def attention_forward_kernel(
    scal, crop, x_ref, mine_ref, other_ref,
    emb_ref, n1_ref, q_ref, k_ref, v_ref, p_ref, mixed_ref, after_ref, n2_ref, wcopy_ref, vec_ref, token_ref,
    w_ref, table_ref, sem,
):
    load_weights(scal[1], mine_ref, other_ref, w_ref, wcopy_ref, sem, token_ref)
    part = CELLS // (2 * OWNERS)

    @pl.when(pl.program_id(0) == 0)
    def _():
        for at, ref in ((scal[1], mine_ref), (1 - scal[1], other_ref)):
            for dp in range(OWNERS):
                row = pl.ds(pl.multiple_of((2 * dp + at) * part, part), part)
                table_ref[row, :] = ref[2 * D + dp * part : 2 * D + (dp + 1) * part, :]
        vec_ref[...] = jnp.zeros_like(vec_ref)
        wide, thin = D // OWNERS, D // (4 * OWNERS)
        first = 2 * D + CELLS // 2

        def unpack(ref, core):
            for dp in range(OWNERS):
                rows = slice(first + dp * part, first + dp * part + 6)
                if core == 0:
                    vec_ref[0:6, dp * wide : (dp + 1) * wide] = ref[rows, 0:wide].astype(F32)
                for x in range(2):
                    lane = x * (D // 2) + 128
                    at = (2 * x + core) * (D // 4) + dp * thin
                    vec_ref[8:14, at : at + thin] = ref[rows, lane : lane + thin].astype(F32)

        @pl.when(scal[1] == 0)
        def _():
            unpack(mine_ref, 0)
            unpack(other_ref, 1)

        @pl.when(scal[1] != 0)
        def _():
            unpack(other_ref, 0)
            unpack(mine_ref, 1)

    grid = scal[0] + pl.program_id(0)
    height, breadth, top, left = crop[grid, 0], crop[grid, 1], crop[grid, 2], crop[grid, 3]
    target = crop_target(
        lax.broadcasted_iota(jnp.int32, (1, CELLS), 1), height, breadth, top, left
    )
    cell = lax.broadcasted_iota(jnp.int32, (CELLS, CELLS), 0)
    onehot = jnp.where(cell == target, 1.0, 0.0).astype(BF)
    emb = x_ref[0].astype(F32) + dot(onehot, table_ref[...])
    emb_ref[...] = emb
    u, _ = norm_stats(emb)
    n1 = (u * vec_ref[0:1, :] + vec_ref[1:2, :]).astype(BF)
    n1_ref[...] = n1
    q_ref[...] = (dot(n1, w_ref[0]) + vec_ref[8:9, :]).astype(BF)
    k_ref[...] = dot(n1, w_ref[1]).astype(BF)
    v_ref[...] = (dot(n1, w_ref[2]) + vec_ref[9:10, :]).astype(BF)
    valid = lax.broadcasted_iota(jnp.int32, (1, CELLS), 1) < height * breadth
    tiles_out = [None] * (D // 128)
    for h in range(HEADS):
        first, tiles = head_window(h)
        lanes = slice(first * 128, (first + tiles) * 128)
        mask = head_mask(h)
        qh = jnp.where(mask, q_ref[:, lanes], 0).astype(BF)
        s = jnp.where(valid, dot(qh, k_ref[:, lanes], NT), MASK_FILL)
        top_score = jnp.max(s, axis=-1, keepdims=True)
        e = jnp.exp2((s - top_score) * (SCALE * LOG2E))
        p_ref[0, h] = (e * (1.0 / jnp.sum(e, axis=-1, keepdims=True))).astype(BF)
    for h in range(HEADS):
        first, tiles = head_window(h)
        lanes = slice(first * 128, (first + tiles) * 128)
        mask = head_mask(h)
        vh = jnp.where(mask, v_ref[:, lanes], 0).astype(BF)
        o = dot(p_ref[0, h], vh)
        for t in range(tiles):
            part = o[:, t * 128 : (t + 1) * 128]
            at = first + t
            tiles_out[at] = part if tiles_out[at] is None else tiles_out[at] + part
    for t in range(D // 128):
        mixed_ref[:, t * 128 : (t + 1) * 128] = tiles_out[t].astype(BF)
    attention = dot(mixed_ref[...], w_ref[3], NT)
    after = emb_ref[...] + attention + vec_ref[2:3, :]
    after_ref[...] = after
    u2, _ = norm_stats(after)
    n2_ref[...] = (u2 * vec_ref[3:4, :] + vec_ref[4:5, :]).astype(BF)


def up_kernel(
    scal, n2_ref, low_ref, high_ref, vec_ref, g_ref,
    hidden_ref, gp_ref, mine_ref, other_ref, wcopy_ref, token_ref, gt_ref, w_ref, sem,
):
    j = pl.program_id(0)
    load_weights(scal[1], low_ref, high_ref, w_ref, wcopy_ref, sem, token_ref)
    grids = g_ref.shape[0]

    @pl.when(j == 0)
    def _():
        for n in range(grids):
            gt_ref[:, n * CELLS : (n + 1) * CELLS] = g_ref[n].T

    bias = vec_ref[pl.ds(10 + j, 1), :]
    for n in range(grids):
        rows = slice(n * CELLS, (n + 1) * CELLS)
        pre = dot(n2_ref[rows, :], w_ref[j]) + bias
        phi = 0.5 + 0.5 * lax.erf(pre * (0.5**0.5))
        density = jnp.exp2(pre * pre * (-0.5 * LOG2E)) * INV_SQRT_2PI
        hidden_ref[0, rows, :] = (pre * phi).astype(BF)
        gp_ref[0, rows, :] = (phi + pre * density).astype(BF)
    grad = dot(gt_ref[...], hidden_ref[0]).astype(BF)
    keep(scal[1], 0, grad, mine_ref, other_ref)


def keep(core, at, grad, mine_ref, other_ref):
    parts = grad.reshape(OWNERS, 2, HALF, D)
    rows = slice(at * HALF, (at + 1) * HALF)

    @pl.when(core == 0)
    def _():
        mine_ref[:, rows, :] = parts[:, 0]
        other_ref[:, rows, :] = parts[:, 1]

    @pl.when(core != 0)
    def _():
        mine_ref[:, rows, :] = parts[:, 1]
        other_ref[:, rows, :] = parts[:, 0]


def down_kernel(
    scal, hidden_ref, low_ref, high_ref, after_ref, vec_ref, out_ref, wcopy_ref, token_ref, down_ref, sem
):
    load_weights(scal[1], low_ref, high_ref, down_ref, wcopy_ref, sem, token_ref)
    total = dot(hidden_ref[0], down_ref[0], NT)
    for j in range(1, 4):
        total = total + dot(hidden_ref[j], down_ref[j], NT)
    out_ref[0] = (after_ref[...] + total + vec_ref[5:6, :]).astype(BF)


def mlp_kernel(
    scal, gp_ref, down_ref, up_ref, n2_ref, g_ref, after_any, vec_ref, mixed_any,
    ga_ref, galow_ref, mine_ref, other_ref, gb_ref, gn_ref, token_ref,
    dn2_acc, n2t_ref, gpre_ref, after_ref, mixed_ref, sem,
):
    j = pl.program_id(0)
    grids = g_ref.shape[0]
    core = scal[1]
    late = (
        pltpu.make_async_copy(after_any, after_ref, sem.at[0]),
        pltpu.make_async_copy(mixed_any, mixed_ref, sem.at[1]),
    )

    @pl.when(j == 0)
    def _():
        for copy in late:
            copy.start()
        for n in range(grids):
            rows = slice(n * CELLS, (n + 1) * CELLS)
            n2t_ref[:, rows] = n2_ref[rows, :].T
        dn2_acc[...] = jnp.zeros_like(dn2_acc)
        gb_ref[...] = jnp.zeros_like(gb_ref)
        gn_ref[...] = jnp.zeros_like(gn_ref)
        token_ref[...] = jnp.zeros_like(token_ref)

    @pl.when(j < 4)
    def _():
        colsum = jnp.zeros((1, D), F32)
        for n in range(grids):
            rows = slice(n * CELLS, (n + 1) * CELLS)
            gh = dot(g_ref[n], down_ref[0])
            gpre = (gh * gp_ref[0, rows, :].astype(F32)).astype(BF)
            gpre_ref[rows, :] = gpre
            colsum = colsum + jnp.sum(gpre.astype(F32), axis=0, keepdims=True)
        for n in range(grids):
            rows = slice(n * CELLS, (n + 1) * CELLS)
            dn2_acc[rows, :] += dot(gpre_ref[rows, :], up_ref[0], NT)
        gb_ref[pl.ds(j, 1), :] = colsum
        keep(core, 0, dot(n2t_ref[...], gpre_ref[...]).astype(BF), mine_ref, other_ref)

    @pl.when(j == 4)
    def _():
        for copy in late:
            copy.wait()
        sums = [jnp.zeros((1, D), F32)] * 4
        for n in range(grids):
            rows = slice(n * CELLS, (n + 1) * CELLS)
            u, rstd = norm_stats(after_ref[rows, :])
            c = dn2_acc[rows, :]
            g = g_ref[n].astype(F32)
            ga = g + norm_back(c, vec_ref[3:4, :], u, rstd)
            ga_ref[rows, :] = ga
            galow = ga.astype(BF)
            galow_ref[rows, :] = galow
            n2t_ref[:, rows] = galow.T
            parts = (ga, c * u, c, g)
            sums = [s + jnp.sum(v, axis=0, keepdims=True) for s, v in zip(sums, parts)]
        for i in range(4):
            gn_ref[2 + i : 3 + i, :] = sums[i]
        keep(core, 0, dot(n2t_ref[...], mixed_ref[...]).astype(BF), mine_ref, other_ref)


def attention_backward_kernel(
    scal, crop, ga_ref, galow_ref, mixed_ref, p_ref, q_ref, k_ref, v_ref, emb_ref, n1_ref,
    w_ref, vec_ref, gn_ref, gb_ref,
    ig_ref, table_out, gs_out, mine_ref, other_ref, token_ref,
    dm_ref, ds_ref, dq_all, dk_all, dv_all, n1t_ref, table_ref, gs_ref,
):
    i = pl.program_id(0)
    grids = pl.num_programs(0) - 1
    core = scal[1]

    @pl.when(i == 0)
    def _():
        table_ref[...] = jnp.zeros_like(table_ref)
        gs_ref[...] = jnp.zeros_like(gs_ref)
        token_ref[...] = jnp.zeros_like(token_ref)

    @pl.when(i < grids)
    def _():
        grid = scal[0] + i
        height, breadth, top, left = crop[grid, 0], crop[grid, 1], crop[grid, 2], crop[grid, 3]
        here = pl.ds(pl.multiple_of(i * CELLS, CELLS), CELLS)
        n1t_ref[:, here] = n1_ref[...].T
        dm_ref[...] = dot(galow_ref[...], w_ref[3]).astype(BF)
        outs = [[None] * (D // 128) for _ in range(3)]
        for h in range(HEADS):
            first, tiles = head_window(h)
            lanes = slice(first * 128, (first + tiles) * 128)
            mask = head_mask(h)
            dmh = jnp.where(mask, dm_ref[:, lanes], 0).astype(BF)
            dp = dot(dmh, v_ref[:, lanes], NT)
            delta = jnp.sum(
                dmh.astype(F32) * mixed_ref[:, lanes].astype(F32), axis=-1, keepdims=True
            )
            ds_ref[h] = (p_ref[0, h].astype(F32) * (dp - delta)).astype(BF)
        for h in range(HEADS):
            first, tiles = head_window(h)
            lanes = slice(first * 128, (first + tiles) * 128)
            mask = head_mask(h)
            qh = jnp.where(mask, q_ref[:, lanes], 0).astype(BF)
            kh = jnp.where(mask, k_ref[:, lanes], 0).astype(BF)
            dmh = jnp.where(mask, dm_ref[:, lanes], 0).astype(BF)
            ds = ds_ref[h]
            got = (dot(ds, kh), dot(ds, qh, TN), dot(p_ref[0, h], dmh, TN))
            for o in range(3):
                for t in range(tiles):
                    part = got[o][:, t * 128 : (t + 1) * 128]
                    at = first + t
                    outs[o][at] = part if outs[o][at] is None else outs[o][at] + part
        for t in range(D // 128):
            lanes = slice(t * 128, (t + 1) * 128)
            dq_all[here, lanes] = (outs[0][t] * SCALE).astype(BF)
            dk_all[here, lanes] = (outs[1][t] * SCALE).astype(BF)
            dv_all[here, lanes] = outs[2][t].astype(BF)
        dq, dk, dv = dq_all[here, :], dk_all[here, :], dv_all[here, :]
        c = dot(dq, w_ref[0], NT) + dot(dk, w_ref[1], NT) + dot(dv, w_ref[2], NT)
        u, rstd = norm_stats(emb_ref[...])
        ge = ga_ref[...] + norm_back(c, vec_ref[0:1, :], u, rstd)
        high = ge.astype(BF)
        ig_ref[0] = high
        low = (ge - high.astype(F32)).astype(BF)
        target = crop_target(
            lax.broadcasted_iota(jnp.int32, (CELLS, 1), 0), height, breadth, top, left
        )
        cell = lax.broadcasted_iota(jnp.int32, (CELLS, CELLS), 1)
        onehot = jnp.where(cell == target, 1.0, 0.0).astype(BF)
        table_ref[...] += dot(onehot, high) + dot(onehot, low)
        for row, v in enumerate((dq.astype(F32), dv.astype(F32), c * u, c)):
            gs_ref[row : row + 1, :] += jnp.sum(v, axis=0, keepdims=True)

    @pl.when(i == grids)
    def _():
        for b, ref in enumerate((dq_all, dk_all, dv_all)):
            keep(core, b, dot(n1t_ref[...], ref[...]).astype(BF), mine_ref, other_ref)
        table_out[...] = table_ref[...]
        gs_out[...] = gs_ref[...]
        start = 3 * HALF
        table = table_ref[...].astype(BF).reshape(OWNERS, 2, 16, D)
        norm = jnp.concatenate([gs_ref[2:4, :], gn_ref[2:6, :]], axis=0).astype(BF)
        split = jnp.concatenate([gs_ref[0:2, :], gb_ref[0:4, :]], axis=0).astype(BF)
        wide, thin = D // OWNERS, D // (4 * OWNERS)
        side = D // 2

        def small(ref, half):
            ref[:, start : start + 16, :] = table[:, half]
            ref[:, start + 16 : start + 32, :] = jnp.zeros((OWNERS, 16, D), BF)
            for dp in range(OWNERS):
                for x in range(2):
                    lane = x * side
                    ref[dp, start + 16 : start + 22, lane : lane + wide] = norm[
                        :, dp * wide : (dp + 1) * wide
                    ]
                    at = (2 * x + half) * (D // 4) + dp * thin
                    ref[dp, start + 24 : start + 30, lane : lane + thin] = split[:, at : at + thin]

        @pl.when(core == 0)
        def _():
            small(mine_ref, 0)
            small(other_ref, 1)

        @pl.when(core != 0)
        def _():
            small(mine_ref, 1)
            small(other_ref, 0)


def sds(shape, dtype):
    return jax.ShapeDtypeStruct(shape, dtype)


TOKEN = sds((8, 128), F32)


def in_hbm(shape):
    return pltpu.HBM(shape.shape, shape.dtype)


def behind(value, token):
    return lax.optimization_barrier((value, token))


ANY = pl.BlockSpec(memory_space=pl.ANY)


def half_shape(blocks, extra=0):
    return sds((OWNERS, blocks * HALF + extra, D), BF)


def whole_block(shape, buffers=None):
    zeros = (0,) * len(shape)
    mode = None if buffers is None else pl.Buffered(buffers)
    return pl.BlockSpec(shape, lambda i, *_: zeros, pipeline_mode=mode)


def attention_forward(scal, crop, x, mine, other, grids, deps=()):
    tokens = grids * CELLS
    rows = pl.BlockSpec((CELLS, D), lambda i, *_: (i, 0))
    spec = pltpu.PrefetchScalarGridSpec(
        num_scalar_prefetch=2,
        grid=(grids,),
        in_specs=[
            pl.BlockSpec((1, CELLS, D), lambda i, s, c: (s[0] + i, 0, 0)),
            whole_block(mine.shape, 1),
            whole_block(mine.shape, 1),
        ] + [ANY] * len(deps),
        out_specs=[
            rows, rows, rows, rows, rows,
            pl.BlockSpec((1, HEADS, CELLS, CELLS), lambda i, *_: (i, 0, 0, 0)),
            rows, rows, rows,
            pl.BlockSpec(memory_space=pl.ANY),
            whole_block((16, D)),
            whole_block((8, 128)),
        ],
        scratch_shapes=[
            pltpu.VMEM((4, D, D), BF), pltpu.VMEM((CELLS, D), BF), pltpu.SemaphoreType.DMA,
        ],
    )
    low, full = pltpu.HBM((tokens, D), BF), pltpu.HBM((tokens, D), F32)
    return pl.pallas_call(
        ignoring(attention_forward_kernel, 5, len(deps)),
        grid_spec=spec,
        out_shape=[
            full, low, low, low, low, pltpu.HBM((grids, HEADS, CELLS, CELLS), BF), low, full,
            sds((tokens, D), BF), pltpu.HBM((4, D, D), BF), sds((16, D), F32), TOKEN,
        ],
        compiler_params=params(40 * MIB),
        cost_estimate=NO_COST,
        name="attention_forward",
    )(scal, crop, x, mine, other, *deps)


def up_forward(scal, n2, mine, other, vec, cotangent, grids, deps=()):
    tokens = grids * CELLS
    block = pl.BlockSpec((1, tokens, D), lambda j, *_: (j, 0, 0))
    half = pl.BlockSpec((OWNERS, HALF, D), lambda j, *_: (0, j, 0))
    spec = pltpu.PrefetchScalarGridSpec(
        num_scalar_prefetch=1,
        grid=(4,),
        in_specs=[
            whole_block((tokens, D), 1),
            whole_block((2 * D, D), 1),
            whole_block((2 * D, D), 1),
            whole_block((16, D)),
            pl.BlockSpec((grids, CELLS, D), lambda j, s: (s[2], 0, 0), pipeline_mode=pl.Buffered(1)),
        ] + [ANY] * len(deps),
        out_specs=[block, block, half, half, pl.BlockSpec(memory_space=pl.ANY), whole_block((8, 128))],
        scratch_shapes=[
            pltpu.VMEM((D, tokens), BF), pltpu.VMEM((4, D, D), BF), pltpu.SemaphoreType.DMA,
        ],
    )
    return pl.pallas_call(
        ignoring(up_kernel, 6, len(deps)),
        grid_spec=spec,
        out_shape=[
            sds((4, tokens, D), BF), pltpu.HBM((4, tokens, D), BF), half_shape(4), in_hbm(half_shape(4)),
            pltpu.HBM((4, D, D), BF), TOKEN,
        ],
        compiler_params=params(40 * MIB * tokens // 768),
        cost_estimate=NO_COST,
        name="up_forward",
    )(scal, n2, mine, other, vec, cotangent, *deps)


def down_forward(scal, hidden, mine, other, after, vec, grids, deps=()):
    tokens = grids * CELLS
    spec = pltpu.PrefetchScalarGridSpec(
        num_scalar_prefetch=1,
        grid=(grids,),
        in_specs=[
            pl.BlockSpec((4, CELLS, D), lambda i, *_: (0, i, 0)),
            whole_block((2 * D, D), 1),
            whole_block((2 * D, D), 1),
            pl.BlockSpec((CELLS, D), lambda i, *_: (i, 0)),
            whole_block((16, D)),
        ] + [ANY] * len(deps),
        out_specs=[
            pl.BlockSpec((1, CELLS, D), lambda i, *_: (i, 0, 0)),
            pl.BlockSpec(memory_space=pl.ANY),
            whole_block((8, 128)),
        ],
        scratch_shapes=[pltpu.VMEM((4, D, D), BF), pltpu.SemaphoreType.DMA],
    )
    return pl.pallas_call(
        ignoring(down_kernel, 6, len(deps)),
        grid_spec=spec,
        out_shape=[pltpu.HBM((grids, CELLS, D), BF), pltpu.HBM((4, D, D), BF), TOKEN],
        compiler_params=params(24 * MIB),
        cost_estimate=NO_COST,
        name="down_forward",
    )(scal, hidden, mine, other, after, vec, *deps)


def mlp_backward(scal, gp, down, up, n2, cotangent, after, vec, mixed, grids, deps=()):
    tokens = grids * CELLS
    last = lambda j: jnp.minimum(j, 3)
    block = pl.BlockSpec((1, tokens, D), lambda j, *_: (last(j), 0, 0))
    weight = pl.BlockSpec((1, D, D), lambda j, *_: (last(j), 0, 0))
    half = pl.BlockSpec((OWNERS, HALF, D), lambda j, *_: (0, j, 0))
    rows = whole_block((tokens, D))
    any_spec = pl.BlockSpec(memory_space=pl.ANY)
    spec = pltpu.PrefetchScalarGridSpec(
        num_scalar_prefetch=1,
        grid=(5,),
        in_specs=[
            block, weight, weight, whole_block((tokens, D), 1),
            pl.BlockSpec((grids, CELLS, D), lambda j, s: (s[2], 0, 0), pipeline_mode=pl.Buffered(1)),
            any_spec, whole_block((16, D)), any_spec,
        ] + [ANY] * len(deps),
        out_specs=[rows, rows, half, half, whole_block((8, D)), whole_block((8, D)), whole_block((8, 128))],
        scratch_shapes=[
            pltpu.VMEM((tokens, D), F32), pltpu.VMEM((D, tokens), BF), pltpu.VMEM((tokens, D), BF),
            pltpu.VMEM((tokens, D), F32), pltpu.VMEM((tokens, D), BF),
            pltpu.SemaphoreType.DMA((2,)),
        ],
    )
    return pl.pallas_call(
        ignoring(mlp_kernel, 9, len(deps)),
        grid_spec=spec,
        out_shape=[
            sds((tokens, D), F32), sds((tokens, D), BF),
            half_shape(5), in_hbm(half_shape(5)), sds((8, D), F32), sds((8, D), F32), TOKEN,
        ],
        compiler_params=params(40 * MIB * tokens // 768),
        cost_estimate=NO_COST,
        name="mlp_backward",
    )(scal, gp, down, up, n2, cotangent, after, vec, mixed, *deps)


def attention_backward(scal, crop, ga, galow, mixed, p, q, k, v, emb, n1, w, vec, gn, gb, grids, deps=()):
    tokens = grids * CELLS
    last = lambda i: jnp.minimum(i, grids - 1)
    rows = pl.BlockSpec((CELLS, D), lambda i, *_: (last(i), 0))
    half = half_shape(3, SMALL)
    few = whole_block((8, D))
    spec = pltpu.PrefetchScalarGridSpec(
        num_scalar_prefetch=2,
        grid=(grids + 1,),
        in_specs=[
            rows, rows, rows,
            pl.BlockSpec((1, HEADS, CELLS, CELLS), lambda i, *_: (last(i), 0, 0, 0)),
            rows, rows, rows, rows, rows,
            whole_block((4, D, D), 1),
            whole_block((16, D)), few, few,
        ] + [ANY] * len(deps),
        out_specs=[
            pl.BlockSpec((1, CELLS, D), lambda i, *_: (last(i), 0, 0)),
            whole_block((CELLS, D)),
            few,
            whole_block(half.shape, 1), whole_block(half.shape, 1),
            whole_block((8, 128)),
        ],
        scratch_shapes=[pltpu.VMEM((CELLS, D), BF), pltpu.VMEM((HEADS, CELLS, CELLS), BF)]
        + [pltpu.VMEM((tokens, D), BF)] * 3
        + [pltpu.VMEM((D, tokens), BF), pltpu.VMEM((CELLS, D), F32), pltpu.VMEM((8, D), F32)],
    )
    return pl.pallas_call(
        ignoring(attention_backward_kernel, 15, len(deps)),
        grid_spec=spec,
        out_shape=[
            pltpu.HBM((grids, CELLS, D), BF), sds((CELLS, D), F32), sds((8, D), F32), half, in_hbm(half), TOKEN,
        ],
        compiler_params=params(40 * MIB),
        cost_estimate=NO_COST,
        name="attention_backward",
    )(scal, crop, ga, galow, mixed, p, q, k, v, emb, n1, w, vec, gn, gb, *deps)


class Place:
    def __init__(self, dp_size, mp_size):
        self.z_size = dp_size // 2
        dp, mp = lax.axis_index("dp"), lax.axis_index("mp")
        self.dp, self.mp = dp, mp
        self.z, self.y = dp // 2, dp % 2
        self.x, self.c = mp // 2, mp % 2
        self.core_pairs = [(i, i ^ 1) for i in range(mp_size)]
        self.x_pairs = [(i, i ^ 2) for i in range(mp_size)]
        self.y_pairs = [(i, i ^ 1) for i in range(dp_size)]
        self.z_shift = [
            [(i, ((i // 2 + s) % self.z_size) * 2 + i % 2) for i in range(dp_size)]
            for s in range(self.z_size)
        ]

        self.corner_pairs = [
            (d * mp_size + m, (d ^ 1) * mp_size + (m ^ 2))
            for d in range(dp_size)
            for m in range(mp_size)
        ]

    def core(self, v):
        return lax.ppermute(v, "mp", self.core_pairs)

    def over_corner(self, v):
        return lax.ppermute(v, ("dp", "mp"), self.corner_pairs)

    def over_x(self, v):
        return lax.ppermute(v, "mp", self.x_pairs)

    def over_y(self, v):
        return lax.ppermute(v, "dp", self.y_pairs)

    def over_z(self, v, shift):
        return lax.ppermute(v, "dp", self.z_shift[shift])


def ignoring(kernel, at, count):
    return lambda *refs: kernel(*refs[:at], *refs[at + count :])


def assemble_kernel(rows, extra, depth, views, where, *refs):
    count = 1 + max(at for at, _ in views)
    out, token = refs[count:]
    token[...] = jnp.zeros_like(token)
    z, y, x = where[0], where[1], where[2]
    unit = rows + extra
    held = [(refs[at], row) for at, row in views]
    for s in range(depth):
        zs = lax.rem(z - s + depth, depth)
        for xr in range(2):
            for yr in range(2):
                xs = x if xr == 0 else 1 - x
                ys = y if yr == 0 else 1 - y
                dp = zs * 2 + ys
                lane = pl.ds(pl.multiple_of(xs * (D // 2), D // 2), D // 2)
                for b in range(2):
                    if xr and yr:
                        ref, first = held[3 + b]
                        first += s * unit
                    else:
                        ref, first = held[xr + 2 * yr]
                        first += (b * depth + s) * unit
                    row = pl.ds(pl.multiple_of(b * D + dp * rows, rows), rows)
                    out[row, lane] = ref[first : first + rows, :]
                    if extra:
                        at = 2 * D + b * depth * 2 * extra + dp * extra
                        row = pl.ds(pl.multiple_of(at, extra), extra)
                        out[row, lane] = ref[first + rows : first + unit, :]


def assemble(where, views, pieces, extra, dp_size, deps=()):
    kernel = functools.partial(assemble_kernel, D // dp_size, extra, dp_size // 2, views)
    shape = sds((2 * D + 2 * dp_size * extra, D), BF)
    return call(kernel, "assemble", where, pieces, [shape], deps)


def gather_z(place, u):
    return [u] + [place.over_z(u, s) for s in range(1, place.z_size)]


def call(kernel, name, where, ins, shapes, deps=(), limit=16):
    vmem = pl.BlockSpec(memory_space=pltpu.VMEM)
    return pl.pallas_call(
        ignoring(kernel, 1 + len(ins), len(deps)),
        in_specs=[pl.BlockSpec(memory_space=pltpu.SMEM)] + [vmem] * len(ins) + [ANY] * len(deps),
        out_specs=[vmem] * (len(shapes) + 1),
        out_shape=[*shapes, TOKEN],
        compiler_params=params(limit * MIB),
        cost_estimate=NO_COST,
        name=name,
    )(where, *ins, *deps)


def pack_kernel(count, has_next, unit_at, where, *refs):
    parts, refs = refs[:count], refs[count:]
    half, lows = 0, None
    if has_next:
        by_x, by_y, refs = refs[0], refs[1], refs[2:]
        half = has_next
    token = refs[-1]
    token[...] = jnp.zeros_like(token)
    outs = refs[:-1]
    if unit_at:
        units, outs = outs[0], outs[1:]
        outs[-1][...] = units[unit_at]
        outs = outs[:-1]
    if half:
        first_x, first_y = half[0], half[1]
        size = half[2]
        outs[-2][:size, :] = by_x[first_x : first_x + size, :]
        outs[-1][:size, :] = by_y[first_y : first_y + size, :]
    if count:
        unit = parts[0].shape[1]
        for b in range(2):
            for s in range(count):
                value = parts[s][b]
                at = (b * count + s) * unit
                outs[0][at : at + unit, :] = value
                if half:
                    outs[-2][size + at : size + at + unit, :] = value
                    outs[-1][size + at : size + at + unit, :] = value


def pack(where, parts, by_x, by_y, half, units=None, unit_at=0, deps=()):
    count = len(parts)
    shapes = []
    rows = 2 * count * parts[0].shape[1] if count else 0
    if count:
        shapes.append(sds((rows, D // 2), BF))
    ins = list(parts)
    if half:
        ins += [by_x, by_y]
        shapes += [sds((half[2] + rows, D // 2), BF)] * 2
    if unit_at:
        ins.append(units)
        shapes.append(sds(units.shape[1:], BF))
    kernel = functools.partial(pack_kernel, count, half, unit_at)
    return call(kernel, "pack", where, ins, shapes, deps)


def add(a, b):
    return a.astype(F32) + b.astype(F32)


def dp_of(z, y):
    return z * 2 + y


def split_y(y, value_at, depth, send, keep):
    for z in range(depth):
        send[z] = value_at(dp_of(z, 1 - y)).astype(BF)
        keep[z] = value_at(dp_of(z, y)).astype(BF)


def split_x(x, value, send, keep):
    side = D // 2
    left, right = value[:, :side].astype(BF), value[:, side:].astype(BF)

    @pl.when(x == 0)
    def _():
        send[...] = right
        keep[...] = left

    @pl.when(x != 0)
    def _():
        send[...] = left
        keep[...] = right


def first_y_kernel(where, mine, got, send, keep, token):
    token[...] = jnp.zeros_like(token)
    split_y(where[1], lambda dp: add(mine[dp], got[dp]), OWNERS // 2, send, keep)


def first_y(where, mine, got, deps=()):
    rows = mine.shape[1]
    shape = sds((OWNERS // 2, rows, D), BF)
    return call(first_y_kernel, "first_y", where, [mine, got], [shape, shape], deps)


def first_both_kernel(cut, where, mine, got, send_y, keep_y, send_x, keep_x, token):
    token[...] = jnp.zeros_like(token)
    depth = OWNERS // 2
    split_y(where[1], lambda dp: add(mine[dp, :cut], got[dp, :cut]), depth, send_y, keep_y)
    for dp in range(OWNERS):
        split_x(where[2], add(mine[dp, cut:], got[dp, cut:]), send_x.at[dp], keep_x.at[dp])


def first_both(where, mine, got, deps=()):
    rows = mine.shape[1]
    cut = (2 * rows // 3) // 16 * 16
    over_y = sds((OWNERS // 2, cut, D), BF)
    over_x = sds((OWNERS, rows - cut, D // 2), BF)
    kernel = functools.partial(first_both_kernel, cut)
    return call(kernel, "first_both", where, [mine, got], [over_y, over_y, over_x, over_x], deps)


def first_x_kernel(where, mine, got, send, keep, token):
    token[...] = jnp.zeros_like(token)
    for dp in range(OWNERS):
        split_x(where[2], add(mine[dp], got[dp]), send.at[dp], keep.at[dp])


def first_x(where, mine, got, deps=()):
    shape = sds((OWNERS, mine.shape[1], D // 2), BF)
    return call(first_x_kernel, "first_x", where, [mine, got], [shape, shape], deps)


def second_y_kernel(where, mine, got, send, keep, token):
    token[...] = jnp.zeros_like(token)
    split_y(where[1], lambda dp: add(mine[dp], got[dp]), OWNERS // 2, send, keep)


def second_y(where, mine, got, deps=()):
    shape = sds((OWNERS // 2,) + mine.shape[1:], BF)
    return call(second_y_kernel, "second_y", where, [mine, got], [shape, shape], deps)


def second_both_kernel(where, keep_y, got_y, keep_x, got_x, send_a, left_a, send_b, left_b, token):
    token[...] = jnp.zeros_like(token)
    depth = OWNERS // 2
    for z in range(depth):
        split_x(where[2], add(keep_y[z], got_y[z]), send_a.at[z], left_a.at[z])
    split_y(where[1], lambda dp: add(keep_x[dp], got_x[dp]), depth, send_b, left_b)


def second_both(where, keep_y, got_y, keep_x, got_x, deps=()):
    over_x = sds((OWNERS // 2, keep_y.shape[1], D // 2), BF)
    over_y = sds((OWNERS // 2, keep_x.shape[1], D // 2), BF)
    ins = [keep_y, got_y, keep_x, got_x]
    return call(second_both_kernel, "second_both", where, ins, [over_x, over_x, over_y, over_y], deps)


def split_z_kernel(pairs, where, *refs):
    ins, outs = refs[: 2 * pairs], refs[2 * pairs : -1]
    refs[-1][...] = jnp.zeros_like(refs[-1])
    depth = ins[0].shape[0]
    for s in range(depth):
        z = lax.rem(where[0] + s, depth)
        row = 0
        for i in range(pairs):
            value = add(ins[2 * i][z], ins[2 * i + 1][z]).astype(BF)
            outs[s][row : row + value.shape[0], :] = value
            row += value.shape[0]


def split_z(where, *ins, deps=()):
    depth, width = ins[0].shape[0], ins[0].shape[2]
    rows = sum(v.shape[1] for v in ins[::2])
    kernel = functools.partial(split_z_kernel, len(ins) // 2)
    return call(kernel, "split_z", where, list(ins), [sds((rows, width), BF)] * depth, deps)


def z_to_x_kernel(where, keep, *refs):
    got, (send, left, token) = refs[:-3], refs[-3:]
    token[...] = jnp.zeros_like(token)
    total = keep[...].astype(F32)
    for ref in got:
        total = total + ref[...].astype(F32)
    split_x(where[2], total, send, left)


def z_to_x(where, keep, got, deps=()):
    shape = sds((keep.shape[0], D // 2), BF)
    return call(z_to_x_kernel, "z_to_x", where, [keep, *got], [shape, shape], deps)


def pair_kernel(where, own, by_x, out, token):
    token[...] = jnp.zeros_like(token)
    out[0] = own[...]
    out[1] = by_x[...]


def collect_kernel(where, here, there, out, token):
    token[...] = jnp.zeros_like(token)
    x, c = where[2], where[3]
    grids = here.shape[1]
    for piece, core in ((here, c), (there, 1 - c)):
        for half in range(2):
            mp = 2 * (x if half == 0 else 1 - x) + core
            for n in range(grids):
                out[mp * grids + n] = piece[half, n]


def pair_grids(where, own, by_x, deps=()):
    return call(pair_kernel, "pair", where, [own, by_x], [sds((2,) + own.shape, own.dtype)], deps)


def finish_grids(where, here, there, deps=()):
    shape = sds((here.shape[0] * 2 * here.shape[1],) + here.shape[2:], here.dtype)
    return call(collect_kernel, "collect", where, [here, there], [shape], deps)


def plane_kernel(where, own, by_x, by_y, by_corner, out, token):
    token[...] = jnp.zeros_like(token)
    out[0:16, :] = own[0:16, :]
    out[16:32, :] = by_x[0:16, :]
    here = own[16:24, :] + by_x[16:24, :]
    out[32:40, :] = here + (by_y[...] + by_corner[...])


def sum_plane(place, where, packed, square):
    ins = [packed, place.over_x(packed), place.over_y(square), place.over_corner(square)]
    here, _ = call(plane_kernel, "plane", where, ins, [sds((40, D // 2), F32)])
    there = place.core(here)
    value = here[32:40, :128] + there[32:40, :128]
    return here, there, [value] + [place.over_z(value, s) for s in range(1, place.z_size)]


ROWS1, ROWS2, ROWS3 = 4 * HALF, 5 * HALF, 3 * HALF
ROWS = ROWS1 + ROWS2 + ROWS3


def sums_kernel(where, keep, *refs):
    got, (total, token) = refs[:-2], refs[-2:]
    token[...] = jnp.zeros_like(token)
    value = keep[...].astype(F32)
    for ref in got:
        value = value + ref[...].astype(F32)
    total[...] = value


def sums(where, keep, got, deps=()):
    return call(sums_kernel, "sums", where, [keep, *got], [sds(keep.shape, F32)], deps)


def totals_kernel(where, *refs):
    keep1, got1, total2, keep3, *got3 = refs[:-6]
    kept_ref, sent_ref, tail_ref, packed_ref, square_ref, token = refs[-6:]
    token[...] = jnp.zeros_like(token)
    x, c = where[2], where[3]
    whole3 = keep3[...].astype(F32)
    for ref in got3:
        whole3 = whole3 + ref[...].astype(F32)
    parts = (add(keep1[...], got1[...]), total2[...], whole3[:ROWS3])
    wide = D // 4
    row = 0
    square = jnp.zeros((1, D // 2), F32)
    for value in parts:
        rows = slice(row, row + value.shape[0])
        left, right = value[:, :wide], value[:, wide:]

        @pl.when(c == 0)
        def _():
            kept_ref[rows, :] = left
            sent_ref[rows, :] = right

        @pl.when(c != 0)
        def _():
            kept_ref[rows, :] = right
            sent_ref[rows, :] = left

        square = square + jnp.sum(value * value, axis=0, keepdims=True)
        row += value.shape[0]
    tail = whole3[ROWS3:]
    tail_ref[...] = tail
    lane = lax.broadcasted_iota(jnp.int32, (16, D // 2), 1)
    line = lax.broadcasted_iota(jnp.int32, (16, D // 2), 0)
    owner = jnp.where((x == 0) & (c == 0), 1.0, 0.0)
    codes = tail[16:32]
    small = jnp.where(line < 8, jnp.where(lane < D // OWNERS, codes * owner, 0.0), 0.0)
    small = jnp.where((line >= 8) & (lane < D // (4 * OWNERS)), codes, small)
    square = square + jnp.sum(tail[:16] * tail[:16] + small * small, axis=0, keepdims=True)
    square_ref[...] = jnp.full((8, D // 2), jnp.sum(square), F32)
    packed_ref[0:16, :] = tail[:16]
    packed_ref[16:24, :] = square_ref[...]


def totals(where, keep1, got1, total2, keep3, got3, deps=()):
    ins = [keep1, got1, total2, keep3, *got3]
    half = sds((ROWS, D // 4), F32)
    shapes = [half, half] + [sds((rows, D // 2), F32) for rows in (SMALL, 24, 8)]
    return call(totals_kernel, "totals", where, ins, shapes, deps)


def update_kernel(where, *refs):
    kept, got, tail, plane, other_plane = refs[:5]
    squares = refs[5:9]
    state, outs = refs[9:24], refs[24:]
    x, c = where[2], where[3]
    square = (squares[0][0:1, 0:1] + squares[2][0:1, 0:1]) + (
        squares[1][0:1, 0:1] + squares[3][0:1, 0:1]
    )
    norm = jnp.sqrt(square)
    factor = jnp.minimum(1.0, CLIP_LIMIT / (norm + 1e-06))
    outs[0][...] = norm

    def step(at, index, gradient, rate, decay):
        weight, first, second = (state[at + 5 * i][index] for i in range(3))
        new = adam_step(weight, gradient, first, second, rate, decay)
        for i in range(3):
            outs[1 + at + 5 * i][index] = new[i]

    def block(row):
        rows = slice(row, row + HALF)
        own, other = kept[rows, :], got[rows, :]
        top = jnp.where(c == 0, own, other)
        bottom = jnp.where(c == 0, other, own)
        return jnp.concatenate([top, bottom], axis=0) * factor

    front = [ROWS1 + ROWS2 + HALF * b for b in range(3)] + [ROWS1 + HALF * b for b in range(4)]
    for b, row in enumerate(front):
        step(0, b, block(row), RATE_MATRIX, DECAY_RATE)
    back = [ROWS1 + 4 * HALF] + [HALF * b for b in range(4)]
    for b, row in enumerate(back):
        step(1, b, block(row).T, RATE_MATRIX, DECAY_RATE)
    norm_grad = tail[16:22, : D // OWNERS] * factor
    outs[16][...] = norm_grad
    step(3, Ellipsis, norm_grad, RATE_VECTOR, 0.0)
    step(2, Ellipsis, tail[24:30, : D // (4 * OWNERS)] * factor, RATE_VECTOR, 0.0)
    own, by_x = plane[0:16, :], plane[16:32, :]
    by_core, by_both = other_plane[0:16, :], other_plane[16:32, :]
    here = jnp.concatenate(
        [jnp.where(c == 0, own, by_core), jnp.where(c == 0, by_core, own)], axis=0
    )
    there = jnp.concatenate(
        [jnp.where(c == 0, by_x, by_both), jnp.where(c == 0, by_both, by_x)], axis=0
    )
    side = D // 2
    for half in range(2):
        gradient = jnp.where(x == half, here, there) * factor
        lanes = (slice(None), slice(half * side, (half + 1) * side))
        step(4, lanes, gradient, RATE_TABLE, DECAY_RATE)


def update(where, kept, got, tail, here, there, squares, state, deps):
    vmem = pl.BlockSpec(memory_space=pltpu.VMEM)
    ins = [kept, got, tail, here, there, *squares, *state]
    shapes = [sds((1, 1), F32)] + [sds(v.shape, F32) for v in state] + [sds(state[3].shape, F32)]
    return pl.pallas_call(
        ignoring(update_kernel, 1 + len(ins), len(deps)),
        in_specs=[pl.BlockSpec(memory_space=pltpu.SMEM)] + [vmem] * len(ins) + [ANY] * len(deps),
        out_specs=[vmem] * len(shapes),
        out_shape=shapes,
        compiler_params=params(24 * MIB),
        cost_estimate=NO_COST,
        name="update",
    )(where, *ins, *deps)


def adam_step(weight, gradient, first, second, rate, decay):
    first_new = BETA_FIRST * first + (1.0 - BETA_FIRST) * gradient
    second_new = BETA_SECOND * second + (1.0 - BETA_SECOND) * gradient * gradient
    first_hat = first_new / (1.0 - BETA_FIRST**STEP)
    second_hat = second_new / (1.0 - BETA_SECOND**STEP)
    weight_new = weight - rate * (first_hat / (jnp.sqrt(second_hat) + ADAM_EPS) + decay * weight)
    return (weight_new, first_new, second_new)


def body(
    dp_size, mp_size,
    block_input, cotangent, crop_boxes, front_weights, back_weights, split_biases, norm_params,
    pos_table, front_first, back_weight_first_moment, split_first, norm_first, table_first,
    front_second, back_second, split_second, norm_second, table_second,
):
    place = Place(dp_size, mp_size)
    block_input = pltpu.with_memory_space_constraint(block_input, pltpu.HBM)
    direct = dp_size == 8 and mp_size == 4
    x, y, z, c = place.x, place.y, place.z, place.c
    grids = block_input.shape[0] // mp_size
    scal = jnp.stack([place.mp * grids, c, place.mp, place.dp]).astype(jnp.int32)
    where = jnp.stack([z, y, x, c]).astype(jnp.int32)
    turned = jnp.swapaxes(back_weights, 1, 2).astype(BF)
    low_front = front_weights.astype(BF)
    rows, lanes = low_front.shape[1], low_front.shape[2]

    if direct:
        shards = jnp.concatenate([low_front[:3], turned[:1], low_front[3:], turned[1:]])
        shards = shards.reshape(3, 2, 2, rows, lanes)
        mine = lax.dynamic_index_in_dim(shards, c, axis=1, keepdims=False)
        sent = lax.dynamic_index_in_dim(shards, 1 - c, axis=1, keepdims=False)
        got = place.core(sent)
        units = jnp.where(
            c == 0, jnp.concatenate([mine, got], -1), jnp.concatenate([got, mine], -1)
        )
        extra = pos_table.shape[0] // 2
        half = jnp.where(c == 0, pos_table[:extra], pos_table[extra:]).astype(BF)
        half = jnp.where(x == 0, half[:, : D // 2], half[:, D // 2 :])
        packed = jnp.zeros((extra, D // 2), BF)
        packed = lax.dynamic_update_slice(packed, norm_params.astype(BF), (0, 0))
        packed = lax.dynamic_update_slice(packed, split_biases.astype(BF), (0, 128))
        first_unit = jnp.concatenate([units[0], jnp.stack([half, packed])], axis=1)
        own1, unit2, _ = pack(where, gather_z(place, first_unit), None, None, None, units, 1)
        x1, y1 = place.over_x(own1), place.over_y(own1)
        size1, size2 = own1.shape[0] // 2, units.shape[1] * units.shape[2] * place.z_size // 2
        own2, sent_y, sent_x, unit3, _ = pack(
            where, gather_z(place, unit2), x1, y1, (0, size1, size1), units, 2
        )
        y2, x2 = place.over_y(sent_y), place.over_x(sent_x)
        own3, sent_y, sent_x, token3 = pack(
            where, gather_z(place, unit3), x2, y2, (size1, size1 + size2, size2)
        )
        y3, x3 = place.over_y(sent_y), place.over_x(sent_x)
        attn_mine, _ = assemble(
            where, ((0, 0), (1, 0), (2, 0), (4, 0), (3, 0)), (own1, x1, y1, x2, y2), extra, dp_size,
            (token3,),
        )
        attn_other = place.core(attn_mine)
        first_deps = (token3,)
    else:

        def halves(v):
            v = lax.all_gather(v, "dp", axis=1, tiled=True)
            v = lax.all_gather(v, "mp", axis=2, tiled=True).reshape(2, 2 * D, D)
            return jnp.where(c == 0, v[0], v[1]), jnp.where(c == 0, v[1], v[0])

        attn_mine, attn_other = halves(jnp.concatenate([low_front[:3], turned[:1]]))
        up_pair, down_pair = halves(low_front[3:]), halves(turned[1:])
        table = lax.all_gather(pos_table.astype(BF), "dp", axis=0, tiled=True)
        table = table.reshape(OWNERS, 2, CELLS // (2 * OWNERS), D)
        table = jnp.swapaxes(table, 0, 1).reshape(2, CELLS // 2, D)
        norms = lax.all_gather(norm_params.astype(BF), "dp", axis=1, tiled=True)
        splits = lax.all_gather(split_biases.astype(BF), ("mp", "dp"), axis=1, tiled=True)
        norms = jnp.swapaxes(norms.reshape(6, OWNERS, D // OWNERS), 0, 1)
        splits = jnp.transpose(splits.reshape(6, 2, 2, OWNERS, -1), (2, 3, 0, 1, 4))
        codes = jnp.zeros((2, OWNERS, CELLS // (2 * OWNERS), D), BF)
        codes = codes.at[:, :, 0:6, : norms.shape[2]].set(norms)
        for side in range(2):
            lane = side * (D // 2) + 128
            codes = codes.at[:, :, 0:6, lane : lane + splits.shape[4]].set(splits[:, :, :, side])
        table = jnp.concatenate([table, codes.reshape(2, -1, D)], axis=1)
        attn_mine = jnp.concatenate([attn_mine, jnp.where(c == 0, table[0], table[1])])
        attn_other = jnp.concatenate([attn_other, jnp.where(c == 0, table[1], table[0])])
        first_deps = ()

    emb, normed1, q, k, v, p, mixed, after, normed2, w_attn, vec, token = attention_forward(
        scal, crop_boxes, block_input, attn_mine, attn_other, grids, first_deps
    )
    deps = ()
    if direct:
        sent_y, sent_x, token4 = pack(where, [], x3, y3, (size2, 2 * size2, size2), deps=(token,))
        y4, x4 = place.over_y(sent_y), place.over_x(sent_x)
        half, _ = assemble(
            where, ((0, 0), (1, size1), (2, size1), (4, 0), (3, 0)), (own2, x2, y2, x3, y3), 0, dp_size,
            (token4,),
        )
        up_pair = half, place.core(half)
        deps = (token4,)
    hidden, gp, down_mine, down_other, w_up, token = up_forward(
        scal, normed2, *up_pair, vec, cotangent, grids, deps
    )
    if direct:
        half, token = assemble(
            where, ((0, 0), (1, size2), (2, size2), (4, 0), (3, 0)), (own3, x3, y3, x4, y4), 0, dp_size,
            (token,),
        )
        down_pair = half, place.core(half)
        down_other, token = behind(down_other, token)
        sent, keep1, token = first_y(where, down_mine, place.core(down_other))
        got1 = place.over_y(sent)
        deps = (token,)
    out, w_down, token = down_forward(scal, hidden, *down_pair, after, vec, grids, deps)
    if direct:
        out_x = place.over_x(out)
        deps = (token,)
    ga, galow, up_mine, up_other, gb, gn, token = mlp_backward(
        scal, gp, w_down, w_up, normed2, cotangent, after, vec, mixed, grids, deps
    )
    if direct:
        out_pair, token = pair_grids(where, out, out_x, (token,))
        keep1, *sent, token1 = split_z(where, keep1, got1, deps=(token,))
        got1 = [place.over_z(sent[s - 1], s) for s in range(1, place.z_size)]
        up_other, token1 = behind(up_other, token1)
        sent_x, keep2, token2 = first_x(where, up_mine, place.core(up_other), (token1,))
        got2 = place.over_x(sent_x)
        out_far = place.core(out_pair)
        deps = (token1, token2)
    ig, dtable, gs, mine3, other3, token = attention_backward(
        scal, crop_boxes, ga, galow, mixed, p, q, k, v, emb, normed1, w_attn, vec, gn, gb, grids, deps
    )
    cells_here, norm_here = pos_table.shape[0], norm_params.shape[1]
    split_here = split_biases.shape[1]
    if direct:
        sent1, keep1, token1 = z_to_x(where, keep1, got1, (token,))
        got1 = place.over_x(sent1)
        sent_y, keep2, token2 = second_y(where, keep2, got2, (token1,))
        got2 = place.over_y(sent_y)
        ig_x = place.over_x(ig)
        other3, token2 = behind(other3, token2)
        sent_y, keep3a, sent_x, keep3b, token3 = first_both(
            where, mine3, place.core(other3), (token1, token2)
        )
        got3a, got3b = place.over_y(sent_y), place.over_x(sent_x)
        block_output, token3 = finish_grids(where, out_pair, out_far, (token3,))
        keep2, *sent, token = split_z(where, keep2, got2, deps=(token3,))
        got2 = [place.over_z(sent[s - 1], s) for s in range(1, place.z_size)]
        total2, token = sums(where, keep2, got2, (token,))
        sent_x, keep3a, sent_y, keep3b, token = second_both(
            where, keep3a, got3a, keep3b, got3b, (token,)
        )
        got3a, got3b = place.over_x(sent_x), place.over_y(sent_y)
        ig_pair, token = pair_grids(where, ig, ig_x, (token,))
        keep3, *sent, token = split_z(where, keep3a, got3a, keep3b, got3b, deps=(token,))
        got3 = [place.over_z(sent[s - 1], s) for s in range(1, place.z_size)]
        input_grad, token = finish_grids(where, ig_pair, place.core(ig_pair), (token,))
        kept, sent, tail, packed, square, _ = totals(
            where, keep1, got1, total2, keep3, got3, (token,)
        )
        got = place.core(sent)
        here, there, squares = sum_plane(place, where, packed, square)
        state = (
            front_weights, back_weights, split_biases, norm_params, pos_table,
            front_first, back_weight_first_moment, split_first, norm_first, table_first,
            front_second, back_second, split_second, norm_second, table_second,
        )
        state = [pltpu.with_memory_space_constraint(v, pltpu.HBM) for v in state]
        new = update(where, kept, got, tail, here, there, squares, state, ())
        return (block_output, input_grad, new[0][0, 0], *new[1:])
    else:

        def share(mine, other, blocks):
            low, high = jnp.where(c == 0, mine, other), jnp.where(c == 0, other, mine)
            full = jnp.stack([low, high], 1)[:, :, : blocks * HALF].astype(F32)
            full = full.reshape(OWNERS, 2, blocks, HALF, D)
            full = jnp.transpose(full, (2, 0, 1, 3, 4)).reshape(blocks, D, D)
            full = lax.psum_scatter(full, "dp", scatter_dimension=1, tiled=True)
            return lax.psum_scatter(full, "mp", scatter_dimension=2, tiled=True)

        down_share = share(down_mine, down_other, 4)
        up_share = share(up_mine, up_other, 5)
        out_share, up_share = up_share[4:], up_share[:4]
        qkv_share = share(mine3, other3, 3)
        block_output = lax.all_gather(out, "mp", axis=0, tiled=True)
        input_grad = lax.all_gather(ig, "mp", axis=0, tiled=True)
        norm_grad = jnp.concatenate([gs[2:4], gn[2:6]])
        split_grad = jnp.concatenate([gs[0:2], gb[0:4]])
        dtable = lax.psum(dtable, ("dp", "mp"))
        norm_grad = lax.psum(norm_grad, ("dp", "mp"))
        split_grad = lax.psum(split_grad, ("dp", "mp"))
        table_share = lax.dynamic_slice(dtable, (place.dp * cells_here, 0), (cells_here, D))
        norm_share = lax.dynamic_slice(norm_grad, (0, place.dp * norm_here), (6, norm_here))
        split_share = lax.dynamic_slice(
            split_grad, (0, (place.mp * dp_size + place.dp) * split_here), (6, split_here)
        )
        table_square = jnp.sum(table_share * table_share) / mp_size
    front_share = jnp.concatenate([qkv_share, up_share])
    back_share = jnp.concatenate([out_share, down_share])
    owner = (place.mp == 0).astype(F32)
    square = (
        jnp.sum(qkv_share * qkv_share)
        + jnp.sum(out_share * out_share)
        + jnp.sum(up_share * up_share)
        + jnp.sum(down_share * down_share)
        + jnp.sum(split_share * split_share)
        + owner * jnp.sum(norm_share * norm_share)
        + table_square
    )
    clip_norm = jnp.sqrt(lax.psum(square, ("dp", "mp")))
    factor = jnp.minimum(1.0, CLIP_LIMIT / (clip_norm + 1e-06))
    norm_clipped = norm_share * factor
    new_front, front_first_new, front_second_new = adam_step(
        front_weights, front_share * factor, front_first, front_second, RATE_MATRIX, DECAY_RATE
    )
    new_back, back_first_new, back_second_new = adam_step(
        back_weights,
        jnp.swapaxes(back_share, 1, 2) * factor,
        back_weight_first_moment,
        back_second,
        RATE_MATRIX,
        DECAY_RATE,
    )
    new_split, split_first_new, split_second_new = adam_step(
        split_biases, split_share * factor, split_first, split_second, RATE_VECTOR, 0.0
    )
    new_norm, norm_first_new, norm_second_new = adam_step(
        norm_params, norm_clipped, norm_first, norm_second, RATE_VECTOR, 0.0
    )
    new_table, table_first_new, table_second_new = adam_step(
        pos_table, table_share * factor, table_first, table_second, RATE_TABLE, DECAY_RATE
    )
    return (
        block_output, input_grad, clip_norm,
        new_front, new_back, new_split, new_norm, new_table,
        front_first_new, back_first_new, split_first_new, norm_first_new, table_first_new,
        front_second_new, back_second_new, split_second_new, norm_second_new, table_second_new,
        norm_clipped,
    )


def solution(mesh):
    front, back = P(None, "dp", "mp"), P(None, "mp", "dp")
    split, norm, table = P(None, ("mp", "dp")), P(None, "dp"), P("dp", None)
    state = (front, back, split, norm, table)
    rows = P("dp", None, None)
    return jax.shard_map(
        functools.partial(body, mesh.shape["dp"], mesh.shape["mp"]),
        mesh=mesh,
        in_specs=(rows, rows, P("dp", None)) + state * 3,
        out_specs=(rows, rows, P()) + state * 3 + (norm,),
        check_vma=False,
    )
```

```python
import functools

import jax
import jax.numpy as jnp
from jax import lax
from jax.experimental import pallas as pl
from jax.experimental.pallas import tpu as pltpu
from jax.sharding import PartitionSpec as P

D = 768
HEADS = 16
HEAD = D // HEADS
SIDE = 16
CELLS = 256
STEP = 5
CORES = 2

NORM_EPS = 1e-05
BETA_FIRST = 0.9
BETA_SECOND = 0.95
ADAM_EPS = 1e-08
RATE_MATRIX = 0.05
RATE_TABLE = 0.2
RATE_VECTOR = 0.5
DECAY_RATE = 0.1
CLIP_LIMIT = 0.01
MASK_FILL = -1e30
SCALE = HEAD ** (-0.5)
LOG2E = 1.4426950408889634
INV_SQRT_2PI = 0.3989422804014327

OWNERS = 8
HALF = D // (2 * OWNERS)
SMALL = 32

BF = jnp.bfloat16
F32 = jnp.float32
MIB = 1024 * 1024
NN = (((1,), (0,)), ((), ()))
NT = (((1,), (1,)), ((), ()))
TN = (((0,), (0,)), ((), ()))


NO_COST = pl.CostEstimate(flops=0, bytes_accessed=0, transcendentals=0)


def dot(a, b, dims=NN):
    return lax.dot_general(a, b, dims, preferred_element_type=F32)


def params(limit):
    return pltpu.CompilerParams(vmem_limit_bytes=limit)


def norm_stats(v):
    mean = jnp.mean(v, axis=-1, keepdims=True)
    centred = v - mean
    spread = jnp.mean(centred * centred, axis=-1, keepdims=True)
    rstd = lax.rsqrt(spread + NORM_EPS)
    return centred * rstd, rstd


def norm_back(c, gain, u, rstd):
    cg = c * gain
    mean_cg = jnp.mean(cg, axis=-1, keepdims=True)
    mean_cgu = jnp.mean(cg * u, axis=-1, keepdims=True)
    return rstd * (cg - mean_cg - u * mean_cgu)


def head_window(h):
    low = h * HEAD
    first = low // 128
    last = (low + HEAD - 1) // 128
    return first, last + 1 - first


def head_mask(h):
    first, tiles = head_window(h)
    lane = lax.broadcasted_iota(jnp.int32, (1, tiles * 128), 1) + first * 128
    return (lane >= h * HEAD) & (lane < (h + 1) * HEAD)


def crop_target(position, height, breadth, top, left):
    row = (position >> 4) - top
    col = (position & (SIDE - 1)) - left
    inside = (row >= 0) & (row < height) & (col >= 0) & (col < breadth)
    return jnp.where(inside, row * breadth + col, -1)


def load_weights(core, mine_ref, other_ref, w_ref, copy_ref, sem, token_ref):
    copy = pltpu.make_async_copy(w_ref, copy_ref, sem)

    @pl.when(pl.program_id(0) == 0)
    def _():
        token_ref[...] = jnp.zeros_like(token_ref)

        def fill(low, high):
            for b in range(2):
                rows = slice(b * D, (b + 1) * D)
                w_ref[b] = low[rows, :]
                w_ref[2 + b] = high[rows, :]

        @pl.when(core == 0)
        def _():
            fill(mine_ref, other_ref)

        @pl.when(core != 0)
        def _():
            fill(other_ref, mine_ref)

        copy.start()

    @pl.when(pl.program_id(0) == pl.num_programs(0) - 1)
    def _():
        copy.wait()


def attention_forward_kernel(
    scal, crop, x_ref, mine_ref, other_ref,
    emb_ref, n1_ref, q_ref, k_ref, v_ref, p_ref, mixed_ref, after_ref, n2_ref, wcopy_ref, vec_ref, token_ref,
    w_ref, table_ref, sem,
):
    load_weights(scal[1], mine_ref, other_ref, w_ref, wcopy_ref, sem, token_ref)
    part = CELLS // (2 * OWNERS)

    @pl.when(pl.program_id(0) == 0)
    def _():
        for at, ref in ((scal[1], mine_ref), (1 - scal[1], other_ref)):
            for dp in range(OWNERS):
                row = pl.ds(pl.multiple_of((2 * dp + at) * part, part), part)
                table_ref[row, :] = ref[2 * D + dp * part : 2 * D + (dp + 1) * part, :]
        vec_ref[...] = jnp.zeros_like(vec_ref)
        wide, thin = D // OWNERS, D // (4 * OWNERS)
        first = 2 * D + CELLS // 2

        def unpack(ref, core):
            for dp in range(OWNERS):
                rows = slice(first + dp * part, first + dp * part + 6)
                if core == 0:
                    vec_ref[0:6, dp * wide : (dp + 1) * wide] = ref[rows, 0:wide].astype(F32)
                for x in range(2):
                    lane = x * (D // 2) + 128
                    at = (2 * x + core) * (D // 4) + dp * thin
                    vec_ref[8:14, at : at + thin] = ref[rows, lane : lane + thin].astype(F32)

        @pl.when(scal[1] == 0)
        def _():
            unpack(mine_ref, 0)
            unpack(other_ref, 1)

        @pl.when(scal[1] != 0)
        def _():
            unpack(other_ref, 0)
            unpack(mine_ref, 1)

    grid = scal[0] + pl.program_id(0)
    height, breadth, top, left = crop[grid, 0], crop[grid, 1], crop[grid, 2], crop[grid, 3]
    target = crop_target(
        lax.broadcasted_iota(jnp.int32, (1, CELLS), 1), height, breadth, top, left
    )
    cell = lax.broadcasted_iota(jnp.int32, (CELLS, CELLS), 0)
    onehot = jnp.where(cell == target, 1.0, 0.0).astype(BF)
    emb = x_ref[0].astype(F32) + dot(onehot, table_ref[...])
    emb_ref[...] = emb
    u, _ = norm_stats(emb)
    n1 = (u * vec_ref[0:1, :] + vec_ref[1:2, :]).astype(BF)
    n1_ref[...] = n1
    q_ref[...] = (dot(n1, w_ref[0]) + vec_ref[8:9, :]).astype(BF)
    k_ref[...] = dot(n1, w_ref[1]).astype(BF)
    v_ref[...] = (dot(n1, w_ref[2]) + vec_ref[9:10, :]).astype(BF)
    valid = lax.broadcasted_iota(jnp.int32, (1, CELLS), 1) < height * breadth
    tiles_out = [None] * (D // 128)
    for h in range(HEADS):
        first, tiles = head_window(h)
        lanes = slice(first * 128, (first + tiles) * 128)
        mask = head_mask(h)
        qh = jnp.where(mask, q_ref[:, lanes], 0).astype(BF)
        s = jnp.where(valid, dot(qh, k_ref[:, lanes], NT), MASK_FILL)
        top_score = jnp.max(s, axis=-1, keepdims=True)
        e = jnp.exp2((s - top_score) * (SCALE * LOG2E))
        p_ref[0, h] = (e * (1.0 / jnp.sum(e, axis=-1, keepdims=True))).astype(BF)
    for h in range(HEADS):
        first, tiles = head_window(h)
        lanes = slice(first * 128, (first + tiles) * 128)
        mask = head_mask(h)
        vh = jnp.where(mask, v_ref[:, lanes], 0).astype(BF)
        o = dot(p_ref[0, h], vh)
        for t in range(tiles):
            part = o[:, t * 128 : (t + 1) * 128]
            at = first + t
            tiles_out[at] = part if tiles_out[at] is None else tiles_out[at] + part
    for t in range(D // 128):
        mixed_ref[:, t * 128 : (t + 1) * 128] = tiles_out[t].astype(BF)
    attention = dot(mixed_ref[...], w_ref[3], NT)
    after = emb_ref[...] + attention + vec_ref[2:3, :]
    after_ref[...] = after
    u2, _ = norm_stats(after)
    n2_ref[...] = (u2 * vec_ref[3:4, :] + vec_ref[4:5, :]).astype(BF)


def up_kernel(
    scal, n2_ref, low_ref, high_ref, vec_ref, g_ref,
    hidden_ref, gp_ref, mine_ref, other_ref, wcopy_ref, token_ref, gt_ref, w_ref, sem,
):
    j = pl.program_id(0)
    load_weights(scal[1], low_ref, high_ref, w_ref, wcopy_ref, sem, token_ref)
    grids = g_ref.shape[0]

    @pl.when(j == 0)
    def _():
        for n in range(grids):
            gt_ref[:, n * CELLS : (n + 1) * CELLS] = g_ref[n].T

    bias = vec_ref[pl.ds(10 + j, 1), :]
    for n in range(grids):
        rows = slice(n * CELLS, (n + 1) * CELLS)
        pre = dot(n2_ref[rows, :], w_ref[j]) + bias
        phi = 0.5 + 0.5 * lax.erf(pre * (0.5**0.5))
        density = jnp.exp2(pre * pre * (-0.5 * LOG2E)) * INV_SQRT_2PI
        hidden_ref[0, rows, :] = (pre * phi).astype(BF)
        gp_ref[0, rows, :] = (phi + pre * density).astype(BF)
    grad = dot(gt_ref[...], hidden_ref[0]).astype(BF)
    keep(scal[1], 0, grad, mine_ref, other_ref)


def keep(core, at, grad, mine_ref, other_ref):
    parts = grad.reshape(OWNERS, 2, HALF, D)
    rows = slice(at * HALF, (at + 1) * HALF)

    @pl.when(core == 0)
    def _():
        mine_ref[:, rows, :] = parts[:, 0]
        other_ref[:, rows, :] = parts[:, 1]

    @pl.when(core != 0)
    def _():
        mine_ref[:, rows, :] = parts[:, 1]
        other_ref[:, rows, :] = parts[:, 0]


def down_kernel(
    scal, hidden_ref, low_ref, high_ref, after_ref, vec_ref, out_ref, wcopy_ref, token_ref, down_ref, sem
):
    load_weights(scal[1], low_ref, high_ref, down_ref, wcopy_ref, sem, token_ref)
    total = dot(hidden_ref[0], down_ref[0], NT)
    for j in range(1, 4):
        total = total + dot(hidden_ref[j], down_ref[j], NT)
    out_ref[0] = (after_ref[...] + total + vec_ref[5:6, :]).astype(BF)


def mlp_kernel(
    scal, gp_ref, down_ref, up_ref, n2_ref, g_ref, after_any, vec_ref, mixed_any,
    ga_ref, galow_ref, mine_ref, other_ref, gb_ref, gn_ref, token_ref,
    dn2_acc, n2t_ref, gpre_ref, after_ref, mixed_ref, sem,
):
    j = pl.program_id(0)
    grids = g_ref.shape[0]
    core = scal[1]
    late = (
        pltpu.make_async_copy(after_any, after_ref, sem.at[0]),
        pltpu.make_async_copy(mixed_any, mixed_ref, sem.at[1]),
    )

    @pl.when(j == 0)
    def _():
        for copy in late:
            copy.start()
        for n in range(grids):
            rows = slice(n * CELLS, (n + 1) * CELLS)
            n2t_ref[:, rows] = n2_ref[rows, :].T
        dn2_acc[...] = jnp.zeros_like(dn2_acc)
        gb_ref[...] = jnp.zeros_like(gb_ref)
        gn_ref[...] = jnp.zeros_like(gn_ref)
        token_ref[...] = jnp.zeros_like(token_ref)

    @pl.when(j < 4)
    def _():
        colsum = jnp.zeros((1, D), F32)
        for n in range(grids):
            rows = slice(n * CELLS, (n + 1) * CELLS)
            gh = dot(g_ref[n], down_ref[0])
            gpre = (gh * gp_ref[0, rows, :].astype(F32)).astype(BF)
            gpre_ref[rows, :] = gpre
            colsum = colsum + jnp.sum(gpre.astype(F32), axis=0, keepdims=True)
        for n in range(grids):
            rows = slice(n * CELLS, (n + 1) * CELLS)
            dn2_acc[rows, :] += dot(gpre_ref[rows, :], up_ref[0], NT)
        gb_ref[pl.ds(j, 1), :] = colsum
        keep(core, 0, dot(n2t_ref[...], gpre_ref[...]).astype(BF), mine_ref, other_ref)

    @pl.when(j == 4)
    def _():
        for copy in late:
            copy.wait()
        sums = [jnp.zeros((1, D), F32)] * 4
        for n in range(grids):
            rows = slice(n * CELLS, (n + 1) * CELLS)
            u, rstd = norm_stats(after_ref[rows, :])
            c = dn2_acc[rows, :]
            g = g_ref[n].astype(F32)
            ga = g + norm_back(c, vec_ref[3:4, :], u, rstd)
            ga_ref[rows, :] = ga
            galow = ga.astype(BF)
            galow_ref[rows, :] = galow
            n2t_ref[:, rows] = galow.T
            parts = (ga, c * u, c, g)
            sums = [s + jnp.sum(v, axis=0, keepdims=True) for s, v in zip(sums, parts)]
        for i in range(4):
            gn_ref[2 + i : 3 + i, :] = sums[i]
        keep(core, 0, dot(n2t_ref[...], mixed_ref[...]).astype(BF), mine_ref, other_ref)


def attention_backward_kernel(
    scal, crop, ga_ref, galow_ref, mixed_ref, p_ref, q_ref, k_ref, v_ref, emb_ref, n1_ref,
    w_ref, vec_ref, gn_ref, gb_ref,
    ig_ref, table_out, gs_out, mine_ref, other_ref, token_ref,
    dm_ref, ds_ref, dq_all, dk_all, dv_all, n1t_ref, table_ref, gs_ref,
):
    i = pl.program_id(0)
    grids = pl.num_programs(0) - 1
    core = scal[1]

    @pl.when(i == 0)
    def _():
        table_ref[...] = jnp.zeros_like(table_ref)
        gs_ref[...] = jnp.zeros_like(gs_ref)
        token_ref[...] = jnp.zeros_like(token_ref)

    @pl.when(i < grids)
    def _():
        grid = scal[0] + i
        height, breadth, top, left = crop[grid, 0], crop[grid, 1], crop[grid, 2], crop[grid, 3]
        here = pl.ds(pl.multiple_of(i * CELLS, CELLS), CELLS)
        n1t_ref[:, here] = n1_ref[...].T
        dm_ref[...] = dot(galow_ref[...], w_ref[3]).astype(BF)
        outs = [[None] * (D // 128) for _ in range(3)]
        for h in range(HEADS):
            first, tiles = head_window(h)
            lanes = slice(first * 128, (first + tiles) * 128)
            mask = head_mask(h)
            dmh = jnp.where(mask, dm_ref[:, lanes], 0).astype(BF)
            dp = dot(dmh, v_ref[:, lanes], NT)
            delta = jnp.sum(
                dmh.astype(F32) * mixed_ref[:, lanes].astype(F32), axis=-1, keepdims=True
            )
            ds_ref[h] = (p_ref[0, h].astype(F32) * (dp - delta)).astype(BF)
        for h in range(HEADS):
            first, tiles = head_window(h)
            lanes = slice(first * 128, (first + tiles) * 128)
            mask = head_mask(h)
            qh = jnp.where(mask, q_ref[:, lanes], 0).astype(BF)
            kh = jnp.where(mask, k_ref[:, lanes], 0).astype(BF)
            dmh = jnp.where(mask, dm_ref[:, lanes], 0).astype(BF)
            ds = ds_ref[h]
            got = (dot(ds, kh), dot(ds, qh, TN), dot(p_ref[0, h], dmh, TN))
            for o in range(3):
                for t in range(tiles):
                    part = got[o][:, t * 128 : (t + 1) * 128]
                    at = first + t
                    outs[o][at] = part if outs[o][at] is None else outs[o][at] + part
        for t in range(D // 128):
            lanes = slice(t * 128, (t + 1) * 128)
            dq_all[here, lanes] = (outs[0][t] * SCALE).astype(BF)
            dk_all[here, lanes] = (outs[1][t] * SCALE).astype(BF)
            dv_all[here, lanes] = outs[2][t].astype(BF)
        dq, dk, dv = dq_all[here, :], dk_all[here, :], dv_all[here, :]
        c = dot(dq, w_ref[0], NT) + dot(dk, w_ref[1], NT) + dot(dv, w_ref[2], NT)
        u, rstd = norm_stats(emb_ref[...])
        ge = ga_ref[...] + norm_back(c, vec_ref[0:1, :], u, rstd)
        high = ge.astype(BF)
        ig_ref[0] = high
        low = (ge - high.astype(F32)).astype(BF)
        target = crop_target(
            lax.broadcasted_iota(jnp.int32, (CELLS, 1), 0), height, breadth, top, left
        )
        cell = lax.broadcasted_iota(jnp.int32, (CELLS, CELLS), 1)
        onehot = jnp.where(cell == target, 1.0, 0.0).astype(BF)
        table_ref[...] += dot(onehot, high) + dot(onehot, low)
        for row, v in enumerate((dq.astype(F32), dv.astype(F32), c * u, c)):
            gs_ref[row : row + 1, :] += jnp.sum(v, axis=0, keepdims=True)

    @pl.when(i == grids)
    def _():
        for b, ref in enumerate((dq_all, dk_all, dv_all)):
            keep(core, b, dot(n1t_ref[...], ref[...]).astype(BF), mine_ref, other_ref)
        table_out[...] = table_ref[...]
        gs_out[...] = gs_ref[...]
        start = 3 * HALF
        table = table_ref[...].astype(BF).reshape(OWNERS, 2, 16, D)
        norm = jnp.concatenate([gs_ref[2:4, :], gn_ref[2:6, :]], axis=0).astype(BF)
        split = jnp.concatenate([gs_ref[0:2, :], gb_ref[0:4, :]], axis=0).astype(BF)
        wide, thin = D // OWNERS, D // (4 * OWNERS)
        side = D // 2

        def small(ref, half):
            ref[:, start : start + 16, :] = table[:, half]
            ref[:, start + 16 : start + 32, :] = jnp.zeros((OWNERS, 16, D), BF)
            for dp in range(OWNERS):
                for x in range(2):
                    lane = x * side
                    ref[dp, start + 16 : start + 22, lane : lane + wide] = norm[
                        :, dp * wide : (dp + 1) * wide
                    ]
                    at = (2 * x + half) * (D // 4) + dp * thin
                    ref[dp, start + 24 : start + 30, lane : lane + thin] = split[:, at : at + thin]

        @pl.when(core == 0)
        def _():
            small(mine_ref, 0)
            small(other_ref, 1)

        @pl.when(core != 0)
        def _():
            small(mine_ref, 1)
            small(other_ref, 0)


def sds(shape, dtype):
    return jax.ShapeDtypeStruct(shape, dtype)


TOKEN = sds((8, 128), F32)


def in_hbm(shape):
    return pltpu.HBM(shape.shape, shape.dtype)


def behind(value, token):
    return lax.optimization_barrier((value, token))


ANY = pl.BlockSpec(memory_space=pl.ANY)


def half_shape(blocks, extra=0):
    return sds((OWNERS, blocks * HALF + extra, D), BF)


def whole_block(shape, buffers=None):
    zeros = (0,) * len(shape)
    mode = None if buffers is None else pl.Buffered(buffers)
    return pl.BlockSpec(shape, lambda i, *_: zeros, pipeline_mode=mode)


def attention_forward(scal, crop, x, mine, other, grids, deps=()):
    tokens = grids * CELLS
    rows = pl.BlockSpec((CELLS, D), lambda i, *_: (i, 0))
    spec = pltpu.PrefetchScalarGridSpec(
        num_scalar_prefetch=2,
        grid=(grids,),
        in_specs=[
            pl.BlockSpec((1, CELLS, D), lambda i, s, c: (s[0] + i, 0, 0)),
            whole_block(mine.shape, 1),
            whole_block(mine.shape, 1),
        ] + [ANY] * len(deps),
        out_specs=[
            rows, rows, rows, rows, rows,
            pl.BlockSpec((1, HEADS, CELLS, CELLS), lambda i, *_: (i, 0, 0, 0)),
            rows, rows, rows,
            pl.BlockSpec(memory_space=pl.ANY),
            whole_block((16, D)),
            whole_block((8, 128)),
        ],
        scratch_shapes=[
            pltpu.VMEM((4, D, D), BF), pltpu.VMEM((CELLS, D), BF), pltpu.SemaphoreType.DMA,
        ],
    )
    low, full = pltpu.HBM((tokens, D), BF), pltpu.HBM((tokens, D), F32)
    return pl.pallas_call(
        ignoring(attention_forward_kernel, 5, len(deps)),
        grid_spec=spec,
        out_shape=[
            full, low, low, low, low, pltpu.HBM((grids, HEADS, CELLS, CELLS), BF), low, full,
            sds((tokens, D), BF), pltpu.HBM((4, D, D), BF), sds((16, D), F32), TOKEN,
        ],
        compiler_params=params(40 * MIB),
        cost_estimate=NO_COST,
        name="attention_forward",
    )(scal, crop, x, mine, other, *deps)


def up_forward(scal, n2, mine, other, vec, cotangent, grids, deps=()):
    tokens = grids * CELLS
    block = pl.BlockSpec((1, tokens, D), lambda j, *_: (j, 0, 0))
    half = pl.BlockSpec((OWNERS, HALF, D), lambda j, *_: (0, j, 0))
    spec = pltpu.PrefetchScalarGridSpec(
        num_scalar_prefetch=1,
        grid=(4,),
        in_specs=[
            whole_block((tokens, D), 1),
            whole_block((2 * D, D), 1),
            whole_block((2 * D, D), 1),
            whole_block((16, D)),
            pl.BlockSpec((grids, CELLS, D), lambda j, s: (s[2], 0, 0), pipeline_mode=pl.Buffered(1)),
        ] + [ANY] * len(deps),
        out_specs=[block, block, half, half, pl.BlockSpec(memory_space=pl.ANY), whole_block((8, 128))],
        scratch_shapes=[
            pltpu.VMEM((D, tokens), BF), pltpu.VMEM((4, D, D), BF), pltpu.SemaphoreType.DMA,
        ],
    )
    return pl.pallas_call(
        ignoring(up_kernel, 6, len(deps)),
        grid_spec=spec,
        out_shape=[
            sds((4, tokens, D), BF), pltpu.HBM((4, tokens, D), BF), half_shape(4), in_hbm(half_shape(4)),
            pltpu.HBM((4, D, D), BF), TOKEN,
        ],
        compiler_params=params(40 * MIB * tokens // 768),
        cost_estimate=NO_COST,
        name="up_forward",
    )(scal, n2, mine, other, vec, cotangent, *deps)


def down_forward(scal, hidden, mine, other, after, vec, grids, deps=()):
    tokens = grids * CELLS
    spec = pltpu.PrefetchScalarGridSpec(
        num_scalar_prefetch=1,
        grid=(grids,),
        in_specs=[
            pl.BlockSpec((4, CELLS, D), lambda i, *_: (0, i, 0)),
            whole_block((2 * D, D), 1),
            whole_block((2 * D, D), 1),
            pl.BlockSpec((CELLS, D), lambda i, *_: (i, 0)),
            whole_block((16, D)),
        ] + [ANY] * len(deps),
        out_specs=[
            pl.BlockSpec((1, CELLS, D), lambda i, *_: (i, 0, 0)),
            pl.BlockSpec(memory_space=pl.ANY),
            whole_block((8, 128)),
        ],
        scratch_shapes=[pltpu.VMEM((4, D, D), BF), pltpu.SemaphoreType.DMA],
    )
    return pl.pallas_call(
        ignoring(down_kernel, 6, len(deps)),
        grid_spec=spec,
        out_shape=[pltpu.HBM((grids, CELLS, D), BF), pltpu.HBM((4, D, D), BF), TOKEN],
        compiler_params=params(24 * MIB),
        cost_estimate=NO_COST,
        name="down_forward",
    )(scal, hidden, mine, other, after, vec, *deps)


def mlp_backward(scal, gp, down, up, n2, cotangent, after, vec, mixed, grids, deps=()):
    tokens = grids * CELLS
    last = lambda j: jnp.minimum(j, 3)
    block = pl.BlockSpec((1, tokens, D), lambda j, *_: (last(j), 0, 0))
    weight = pl.BlockSpec((1, D, D), lambda j, *_: (last(j), 0, 0))
    half = pl.BlockSpec((OWNERS, HALF, D), lambda j, *_: (0, j, 0))
    rows = whole_block((tokens, D))
    any_spec = pl.BlockSpec(memory_space=pl.ANY)
    spec = pltpu.PrefetchScalarGridSpec(
        num_scalar_prefetch=1,
        grid=(5,),
        in_specs=[
            block, weight, weight, whole_block((tokens, D), 1),
            pl.BlockSpec((grids, CELLS, D), lambda j, s: (s[2], 0, 0), pipeline_mode=pl.Buffered(1)),
            any_spec, whole_block((16, D)), any_spec,
        ] + [ANY] * len(deps),
        out_specs=[rows, rows, half, half, whole_block((8, D)), whole_block((8, D)), whole_block((8, 128))],
        scratch_shapes=[
            pltpu.VMEM((tokens, D), F32), pltpu.VMEM((D, tokens), BF), pltpu.VMEM((tokens, D), BF),
            pltpu.VMEM((tokens, D), F32), pltpu.VMEM((tokens, D), BF),
            pltpu.SemaphoreType.DMA((2,)),
        ],
    )
    return pl.pallas_call(
        ignoring(mlp_kernel, 9, len(deps)),
        grid_spec=spec,
        out_shape=[
            sds((tokens, D), F32), sds((tokens, D), BF),
            half_shape(5), in_hbm(half_shape(5)), sds((8, D), F32), sds((8, D), F32), TOKEN,
        ],
        compiler_params=params(40 * MIB * tokens // 768),
        cost_estimate=NO_COST,
        name="mlp_backward",
    )(scal, gp, down, up, n2, cotangent, after, vec, mixed, *deps)


def attention_backward(scal, crop, ga, galow, mixed, p, q, k, v, emb, n1, w, vec, gn, gb, grids, deps=()):
    tokens = grids * CELLS
    last = lambda i: jnp.minimum(i, grids - 1)
    rows = pl.BlockSpec((CELLS, D), lambda i, *_: (last(i), 0))
    half = half_shape(3, SMALL)
    few = whole_block((8, D))
    spec = pltpu.PrefetchScalarGridSpec(
        num_scalar_prefetch=2,
        grid=(grids + 1,),
        in_specs=[
            rows, rows, rows,
            pl.BlockSpec((1, HEADS, CELLS, CELLS), lambda i, *_: (last(i), 0, 0, 0)),
            rows, rows, rows, rows, rows,
            whole_block((4, D, D), 1),
            whole_block((16, D)), few, few,
        ] + [ANY] * len(deps),
        out_specs=[
            pl.BlockSpec((1, CELLS, D), lambda i, *_: (last(i), 0, 0)),
            whole_block((CELLS, D)),
            few,
            whole_block(half.shape, 1), whole_block(half.shape, 1),
            whole_block((8, 128)),
        ],
        scratch_shapes=[pltpu.VMEM((CELLS, D), BF), pltpu.VMEM((HEADS, CELLS, CELLS), BF)]
        + [pltpu.VMEM((tokens, D), BF)] * 3
        + [pltpu.VMEM((D, tokens), BF), pltpu.VMEM((CELLS, D), F32), pltpu.VMEM((8, D), F32)],
    )
    return pl.pallas_call(
        ignoring(attention_backward_kernel, 15, len(deps)),
        grid_spec=spec,
        out_shape=[
            pltpu.HBM((grids, CELLS, D), BF), sds((CELLS, D), F32), sds((8, D), F32), half, in_hbm(half), TOKEN,
        ],
        compiler_params=params(40 * MIB),
        cost_estimate=NO_COST,
        name="attention_backward",
    )(scal, crop, ga, galow, mixed, p, q, k, v, emb, n1, w, vec, gn, gb, *deps)


class Place:
    def __init__(self, dp_size, mp_size):
        self.z_size = dp_size // 2
        dp, mp = lax.axis_index("dp"), lax.axis_index("mp")
        self.dp, self.mp = dp, mp
        self.z, self.y = dp // 2, dp % 2
        self.x, self.c = mp // 2, mp % 2
        self.core_pairs = [(i, i ^ 1) for i in range(mp_size)]
        self.x_pairs = [(i, i ^ 2) for i in range(mp_size)]
        self.y_pairs = [(i, i ^ 1) for i in range(dp_size)]
        self.z_shift = [
            [(i, ((i // 2 + s) % self.z_size) * 2 + i % 2) for i in range(dp_size)]
            for s in range(self.z_size)
        ]

        self.corner_pairs = [
            (d * mp_size + m, (d ^ 1) * mp_size + (m ^ 2))
            for d in range(dp_size)
            for m in range(mp_size)
        ]

    def core(self, v):
        return lax.ppermute(v, "mp", self.core_pairs)

    def over_corner(self, v):
        return lax.ppermute(v, ("dp", "mp"), self.corner_pairs)

    def over_x(self, v):
        return lax.ppermute(v, "mp", self.x_pairs)

    def over_y(self, v):
        return lax.ppermute(v, "dp", self.y_pairs)

    def over_z(self, v, shift):
        return lax.ppermute(v, "dp", self.z_shift[shift])


def ignoring(kernel, at, count):
    return lambda *refs: kernel(*refs[:at], *refs[at + count :])


def assemble_kernel(rows, extra, depth, views, where, *refs):
    count = 1 + max(at for at, _ in views)
    out, token = refs[count:]
    token[...] = jnp.zeros_like(token)
    z, y, x = where[0], where[1], where[2]
    unit = rows + extra
    held = [(refs[at], row) for at, row in views]
    for s in range(depth):
        zs = lax.rem(z - s + depth, depth)
        for xr in range(2):
            for yr in range(2):
                xs = x if xr == 0 else 1 - x
                ys = y if yr == 0 else 1 - y
                dp = zs * 2 + ys
                lane = pl.ds(pl.multiple_of(xs * (D // 2), D // 2), D // 2)
                for b in range(2):
                    if xr and yr:
                        ref, first = held[3 + b]
                        first += s * unit
                    else:
                        ref, first = held[xr + 2 * yr]
                        first += (b * depth + s) * unit
                    row = pl.ds(pl.multiple_of(b * D + dp * rows, rows), rows)
                    out[row, lane] = ref[first : first + rows, :]
                    if extra:
                        at = 2 * D + b * depth * 2 * extra + dp * extra
                        row = pl.ds(pl.multiple_of(at, extra), extra)
                        out[row, lane] = ref[first + rows : first + unit, :]


def assemble(where, views, pieces, extra, dp_size, deps=()):
    kernel = functools.partial(assemble_kernel, D // dp_size, extra, dp_size // 2, views)
    shape = sds((2 * D + 2 * dp_size * extra, D), BF)
    return call(kernel, "assemble", where, pieces, [shape], deps)


def gather_z(place, u):
    return [u] + [place.over_z(u, s) for s in range(1, place.z_size)]


def call(kernel, name, where, ins, shapes, deps=(), limit=16):
    vmem = pl.BlockSpec(memory_space=pltpu.VMEM)
    return pl.pallas_call(
        ignoring(kernel, 1 + len(ins), len(deps)),
        in_specs=[pl.BlockSpec(memory_space=pltpu.SMEM)] + [vmem] * len(ins) + [ANY] * len(deps),
        out_specs=[vmem] * (len(shapes) + 1),
        out_shape=[*shapes, TOKEN],
        compiler_params=params(limit * MIB),
        cost_estimate=NO_COST,
        name=name,
    )(where, *ins, *deps)


def pack_kernel(count, has_next, unit_at, where, *refs):
    parts, refs = refs[:count], refs[count:]
    half, lows = 0, None
    if has_next:
        by_x, by_y, refs = refs[0], refs[1], refs[2:]
        half = has_next
    token = refs[-1]
    token[...] = jnp.zeros_like(token)
    outs = refs[:-1]
    if unit_at:
        units, outs = outs[0], outs[1:]
        outs[-1][...] = units[unit_at]
        outs = outs[:-1]
    if half:
        first_x, first_y = half[0], half[1]
        size = half[2]
        outs[-2][:size, :] = by_x[first_x : first_x + size, :]
        outs[-1][:size, :] = by_y[first_y : first_y + size, :]
    if count:
        unit = parts[0].shape[1]
        for b in range(2):
            for s in range(count):
                value = parts[s][b]
                at = (b * count + s) * unit
                outs[0][at : at + unit, :] = value
                if half:
                    outs[-2][size + at : size + at + unit, :] = value
                    outs[-1][size + at : size + at + unit, :] = value


def pack(where, parts, by_x, by_y, half, units=None, unit_at=0, deps=()):
    count = len(parts)
    shapes = []
    rows = 2 * count * parts[0].shape[1] if count else 0
    if count:
        shapes.append(sds((rows, D // 2), BF))
    ins = list(parts)
    if half:
        ins += [by_x, by_y]
        shapes += [sds((half[2] + rows, D // 2), BF)] * 2
    if unit_at:
        ins.append(units)
        shapes.append(sds(units.shape[1:], BF))
    kernel = functools.partial(pack_kernel, count, half, unit_at)
    return call(kernel, "pack", where, ins, shapes, deps)


def add(a, b):
    return a.astype(F32) + b.astype(F32)


def dp_of(z, y):
    return z * 2 + y


def split_y(y, value_at, depth, send, keep):
    for z in range(depth):
        send[z] = value_at(dp_of(z, 1 - y)).astype(BF)
        keep[z] = value_at(dp_of(z, y)).astype(BF)


def split_x(x, value, send, keep):
    side = D // 2
    left, right = value[:, :side].astype(BF), value[:, side:].astype(BF)

    @pl.when(x == 0)
    def _():
        send[...] = right
        keep[...] = left

    @pl.when(x != 0)
    def _():
        send[...] = left
        keep[...] = right


def first_y_kernel(where, mine, got, send, keep, token):
    token[...] = jnp.zeros_like(token)
    split_y(where[1], lambda dp: add(mine[dp], got[dp]), OWNERS // 2, send, keep)


def first_y(where, mine, got, deps=()):
    rows = mine.shape[1]
    shape = sds((OWNERS // 2, rows, D), BF)
    return call(first_y_kernel, "first_y", where, [mine, got], [shape, shape], deps)


def first_both_kernel(cut, where, mine, got, send_y, keep_y, send_x, keep_x, token):
    token[...] = jnp.zeros_like(token)
    depth = OWNERS // 2
    split_y(where[1], lambda dp: add(mine[dp, :cut], got[dp, :cut]), depth, send_y, keep_y)
    for dp in range(OWNERS):
        split_x(where[2], add(mine[dp, cut:], got[dp, cut:]), send_x.at[dp], keep_x.at[dp])


def first_both(where, mine, got, deps=()):
    rows = mine.shape[1]
    cut = (2 * rows // 3) // 16 * 16
    over_y = sds((OWNERS // 2, cut, D), BF)
    over_x = sds((OWNERS, rows - cut, D // 2), BF)
    kernel = functools.partial(first_both_kernel, cut)
    return call(kernel, "first_both", where, [mine, got], [over_y, over_y, over_x, over_x], deps)


def first_x_kernel(where, mine, got, send, keep, token):
    token[...] = jnp.zeros_like(token)
    for dp in range(OWNERS):
        split_x(where[2], add(mine[dp], got[dp]), send.at[dp], keep.at[dp])


def first_x(where, mine, got, deps=()):
    shape = sds((OWNERS, mine.shape[1], D // 2), BF)
    return call(first_x_kernel, "first_x", where, [mine, got], [shape, shape], deps)


def second_y_kernel(where, mine, got, send, keep, token):
    token[...] = jnp.zeros_like(token)
    split_y(where[1], lambda dp: add(mine[dp], got[dp]), OWNERS // 2, send, keep)


def second_y(where, mine, got, deps=()):
    shape = sds((OWNERS // 2,) + mine.shape[1:], BF)
    return call(second_y_kernel, "second_y", where, [mine, got], [shape, shape], deps)


def second_both_kernel(where, keep_y, got_y, keep_x, got_x, send_a, left_a, send_b, left_b, token):
    token[...] = jnp.zeros_like(token)
    depth = OWNERS // 2
    for z in range(depth):
        split_x(where[2], add(keep_y[z], got_y[z]), send_a.at[z], left_a.at[z])
    split_y(where[1], lambda dp: add(keep_x[dp], got_x[dp]), depth, send_b, left_b)


def second_both(where, keep_y, got_y, keep_x, got_x, deps=()):
    over_x = sds((OWNERS // 2, keep_y.shape[1], D // 2), BF)
    over_y = sds((OWNERS // 2, keep_x.shape[1], D // 2), BF)
    ins = [keep_y, got_y, keep_x, got_x]
    return call(second_both_kernel, "second_both", where, ins, [over_x, over_x, over_y, over_y], deps)


def split_z_kernel(pairs, where, *refs):
    ins, outs = refs[: 2 * pairs], refs[2 * pairs : -1]
    refs[-1][...] = jnp.zeros_like(refs[-1])
    depth = ins[0].shape[0]
    for s in range(depth):
        z = lax.rem(where[0] + s, depth)
        row = 0
        for i in range(pairs):
            value = add(ins[2 * i][z], ins[2 * i + 1][z]).astype(BF)
            outs[s][row : row + value.shape[0], :] = value
            row += value.shape[0]


def split_z(where, *ins, deps=()):
    depth, width = ins[0].shape[0], ins[0].shape[2]
    rows = sum(v.shape[1] for v in ins[::2])
    kernel = functools.partial(split_z_kernel, len(ins) // 2)
    return call(kernel, "split_z", where, list(ins), [sds((rows, width), BF)] * depth, deps)


def z_to_x_kernel(where, keep, *refs):
    got, (send, left, token) = refs[:-3], refs[-3:]
    token[...] = jnp.zeros_like(token)
    total = keep[...].astype(F32)
    for ref in got:
        total = total + ref[...].astype(F32)
    split_x(where[2], total, send, left)


def z_to_x(where, keep, got, deps=()):
    shape = sds((keep.shape[0], D // 2), BF)
    return call(z_to_x_kernel, "z_to_x", where, [keep, *got], [shape, shape], deps)


def pair_kernel(where, own, by_x, out, token):
    token[...] = jnp.zeros_like(token)
    out[0] = own[...]
    out[1] = by_x[...]


def collect_kernel(where, here, there, out, token):
    token[...] = jnp.zeros_like(token)
    x, c = where[2], where[3]
    grids = here.shape[1]
    for piece, core in ((here, c), (there, 1 - c)):
        for half in range(2):
            mp = 2 * (x if half == 0 else 1 - x) + core
            for n in range(grids):
                out[mp * grids + n] = piece[half, n]


def pair_grids(where, own, by_x, deps=()):
    return call(pair_kernel, "pair", where, [own, by_x], [sds((2,) + own.shape, own.dtype)], deps)


def finish_grids(where, here, there, deps=()):
    shape = sds((here.shape[0] * 2 * here.shape[1],) + here.shape[2:], here.dtype)
    return call(collect_kernel, "collect", where, [here, there], [shape], deps)


def plane_kernel(where, own, by_x, by_y, by_corner, out, token):
    token[...] = jnp.zeros_like(token)
    out[0:16, :] = own[0:16, :]
    out[16:32, :] = by_x[0:16, :]
    here = own[16:24, :] + by_x[16:24, :]
    out[32:40, :] = here + (by_y[...] + by_corner[...])


def sum_plane(place, where, packed, square):
    ins = [packed, place.over_x(packed), place.over_y(square), place.over_corner(square)]
    here, _ = call(plane_kernel, "plane", where, ins, [sds((40, D // 2), F32)])
    there = place.core(here)
    value = here[32:40, :128] + there[32:40, :128]
    return here, there, [value] + [place.over_z(value, s) for s in range(1, place.z_size)]


ROWS1, ROWS2, ROWS3 = 4 * HALF, 5 * HALF, 3 * HALF
ROWS = ROWS1 + ROWS2 + ROWS3


def sums_kernel(where, keep, *refs):
    got, (total, token) = refs[:-2], refs[-2:]
    token[...] = jnp.zeros_like(token)
    value = keep[...].astype(F32)
    for ref in got:
        value = value + ref[...].astype(F32)
    total[...] = value


def sums(where, keep, got, deps=()):
    return call(sums_kernel, "sums", where, [keep, *got], [sds(keep.shape, F32)], deps)


def totals_kernel(where, *refs):
    keep1, got1, total2, keep3, *got3 = refs[:-6]
    kept_ref, sent_ref, tail_ref, packed_ref, square_ref, token = refs[-6:]
    token[...] = jnp.zeros_like(token)
    x, c = where[2], where[3]
    whole3 = keep3[...].astype(F32)
    for ref in got3:
        whole3 = whole3 + ref[...].astype(F32)
    parts = (add(keep1[...], got1[...]), total2[...], whole3[:ROWS3])
    wide = D // 4
    row = 0
    square = jnp.zeros((1, D // 2), F32)
    for value in parts:
        rows = slice(row, row + value.shape[0])
        left, right = value[:, :wide], value[:, wide:]

        @pl.when(c == 0)
        def _():
            kept_ref[rows, :] = left
            sent_ref[rows, :] = right

        @pl.when(c != 0)
        def _():
            kept_ref[rows, :] = right
            sent_ref[rows, :] = left

        square = square + jnp.sum(value * value, axis=0, keepdims=True)
        row += value.shape[0]
    tail = whole3[ROWS3:]
    tail_ref[...] = tail
    lane = lax.broadcasted_iota(jnp.int32, (16, D // 2), 1)
    line = lax.broadcasted_iota(jnp.int32, (16, D // 2), 0)
    owner = jnp.where((x == 0) & (c == 0), 1.0, 0.0)
    codes = tail[16:32]
    small = jnp.where(line < 8, jnp.where(lane < D // OWNERS, codes * owner, 0.0), 0.0)
    small = jnp.where((line >= 8) & (lane < D // (4 * OWNERS)), codes, small)
    square = square + jnp.sum(tail[:16] * tail[:16] + small * small, axis=0, keepdims=True)
    square_ref[...] = jnp.full((8, D // 2), jnp.sum(square), F32)
    packed_ref[0:16, :] = tail[:16]
    packed_ref[16:24, :] = square_ref[...]


def totals(where, keep1, got1, total2, keep3, got3, deps=()):
    ins = [keep1, got1, total2, keep3, *got3]
    half = sds((ROWS, D // 4), F32)
    shapes = [half, half] + [sds((rows, D // 2), F32) for rows in (SMALL, 24, 8)]
    return call(totals_kernel, "totals", where, ins, shapes, deps)


def update_kernel(where, *refs):
    kept, got, tail, plane, other_plane = refs[:5]
    squares = refs[5:9]
    state, outs = refs[9:24], refs[24:]
    x, c = where[2], where[3]
    square = (squares[0][0:1, 0:1] + squares[2][0:1, 0:1]) + (
        squares[1][0:1, 0:1] + squares[3][0:1, 0:1]
    )
    norm = jnp.sqrt(square)
    factor = jnp.minimum(1.0, CLIP_LIMIT / (norm + 1e-06))
    outs[0][...] = norm

    def step(at, index, gradient, rate, decay):
        weight, first, second = (state[at + 5 * i][index] for i in range(3))
        new = adam_step(weight, gradient, first, second, rate, decay)
        for i in range(3):
            outs[1 + at + 5 * i][index] = new[i]

    def block(row):
        rows = slice(row, row + HALF)
        own, other = kept[rows, :], got[rows, :]
        top = jnp.where(c == 0, own, other)
        bottom = jnp.where(c == 0, other, own)
        return jnp.concatenate([top, bottom], axis=0) * factor

    front = [ROWS1 + ROWS2 + HALF * b for b in range(3)] + [ROWS1 + HALF * b for b in range(4)]
    for b, row in enumerate(front):
        step(0, b, block(row), RATE_MATRIX, DECAY_RATE)
    back = [ROWS1 + 4 * HALF] + [HALF * b for b in range(4)]
    for b, row in enumerate(back):
        step(1, b, block(row).T, RATE_MATRIX, DECAY_RATE)
    norm_grad = tail[16:22, : D // OWNERS] * factor
    outs[16][...] = norm_grad
    step(3, Ellipsis, norm_grad, RATE_VECTOR, 0.0)
    step(2, Ellipsis, tail[24:30, : D // (4 * OWNERS)] * factor, RATE_VECTOR, 0.0)
    own, by_x = plane[0:16, :], plane[16:32, :]
    by_core, by_both = other_plane[0:16, :], other_plane[16:32, :]
    here = jnp.concatenate(
        [jnp.where(c == 0, own, by_core), jnp.where(c == 0, by_core, own)], axis=0
    )
    there = jnp.concatenate(
        [jnp.where(c == 0, by_x, by_both), jnp.where(c == 0, by_both, by_x)], axis=0
    )
    side = D // 2
    for half in range(2):
        gradient = jnp.where(x == half, here, there) * factor
        lanes = (slice(None), slice(half * side, (half + 1) * side))
        step(4, lanes, gradient, RATE_TABLE, DECAY_RATE)


def update(where, kept, got, tail, here, there, squares, state, deps):
    vmem = pl.BlockSpec(memory_space=pltpu.VMEM)
    ins = [kept, got, tail, here, there, *squares, *state]
    shapes = [sds((1, 1), F32)] + [sds(v.shape, F32) for v in state] + [sds(state[3].shape, F32)]
    return pl.pallas_call(
        ignoring(update_kernel, 1 + len(ins), len(deps)),
        in_specs=[pl.BlockSpec(memory_space=pltpu.SMEM)] + [vmem] * len(ins) + [ANY] * len(deps),
        out_specs=[vmem] * len(shapes),
        out_shape=shapes,
        compiler_params=params(24 * MIB),
        cost_estimate=NO_COST,
        name="update",
    )(where, *ins, *deps)


def adam_step(weight, gradient, first, second, rate, decay):
    first_new = BETA_FIRST * first + (1.0 - BETA_FIRST) * gradient
    second_new = BETA_SECOND * second + (1.0 - BETA_SECOND) * gradient * gradient
    first_hat = first_new / (1.0 - BETA_FIRST**STEP)
    second_hat = second_new / (1.0 - BETA_SECOND**STEP)
    weight_new = weight - rate * (first_hat / (jnp.sqrt(second_hat) + ADAM_EPS) + decay * weight)
    return (weight_new, first_new, second_new)


def body(
    dp_size, mp_size,
    block_input, cotangent, crop_boxes, front_weights, back_weights, split_biases, norm_params,
    pos_table, front_first, back_weight_first_moment, split_first, norm_first, table_first,
    front_second, back_second, split_second, norm_second, table_second,
):
    place = Place(dp_size, mp_size)
    block_input = pltpu.with_memory_space_constraint(block_input, pltpu.HBM)
    direct = dp_size == 8 and mp_size == 4
    x, y, z, c = place.x, place.y, place.z, place.c
    grids = block_input.shape[0] // mp_size
    scal = jnp.stack([place.mp * grids, c, place.mp, place.dp]).astype(jnp.int32)
    where = jnp.stack([z, y, x, c]).astype(jnp.int32)
    turned = jnp.swapaxes(back_weights, 1, 2).astype(BF)
    low_front = front_weights.astype(BF)
    rows, lanes = low_front.shape[1], low_front.shape[2]

    if direct:
        shards = jnp.concatenate([low_front[:3], turned[:1], low_front[3:], turned[1:]])
        shards = shards.reshape(3, 2, 2, rows, lanes)
        mine = lax.dynamic_index_in_dim(shards, c, axis=1, keepdims=False)
        sent = lax.dynamic_index_in_dim(shards, 1 - c, axis=1, keepdims=False)
        got = place.core(sent)
        units = jnp.where(
            c == 0, jnp.concatenate([mine, got], -1), jnp.concatenate([got, mine], -1)
        )
        extra = pos_table.shape[0] // 2
        half = jnp.where(c == 0, pos_table[:extra], pos_table[extra:]).astype(BF)
        half = jnp.where(x == 0, half[:, : D // 2], half[:, D // 2 :])
        packed = jnp.zeros((extra, D // 2), BF)
        packed = lax.dynamic_update_slice(packed, norm_params.astype(BF), (0, 0))
        packed = lax.dynamic_update_slice(packed, split_biases.astype(BF), (0, 128))
        first_unit = jnp.concatenate([units[0], jnp.stack([half, packed])], axis=1)
        own1, unit2, _ = pack(where, gather_z(place, first_unit), None, None, None, units, 1)
        x1, y1 = place.over_x(own1), place.over_y(own1)
        size1, size2 = own1.shape[0] // 2, units.shape[1] * units.shape[2] * place.z_size // 2
        own2, sent_y, sent_x, unit3, _ = pack(
            where, gather_z(place, unit2), x1, y1, (0, size1, size1), units, 2
        )
        y2, x2 = place.over_y(sent_y), place.over_x(sent_x)
        parts3 = gather_z(place, unit3)
        attn_mine, token = assemble(
            where, ((0, 0), (1, 0), (2, 0), (4, 0), (3, 0)), (own1, x1, y1, x2, y2), extra, dp_size,
            tuple(parts3[1:]),
        )
        attn_other = place.core(attn_mine)
        own3, sent_y, sent_x, token3 = pack(
            where, parts3, x2, y2, (size1, size1 + size2, size2), deps=(token,)
        )
        y3, x3 = place.over_y(sent_y), place.over_x(sent_x)
        first_deps = (token3,)
    else:

        def halves(v):
            v = lax.all_gather(v, "dp", axis=1, tiled=True)
            v = lax.all_gather(v, "mp", axis=2, tiled=True).reshape(2, 2 * D, D)
            return jnp.where(c == 0, v[0], v[1]), jnp.where(c == 0, v[1], v[0])

        attn_mine, attn_other = halves(jnp.concatenate([low_front[:3], turned[:1]]))
        up_pair, down_pair = halves(low_front[3:]), halves(turned[1:])
        table = lax.all_gather(pos_table.astype(BF), "dp", axis=0, tiled=True)
        table = table.reshape(OWNERS, 2, CELLS // (2 * OWNERS), D)
        table = jnp.swapaxes(table, 0, 1).reshape(2, CELLS // 2, D)
        norms = lax.all_gather(norm_params.astype(BF), "dp", axis=1, tiled=True)
        splits = lax.all_gather(split_biases.astype(BF), ("mp", "dp"), axis=1, tiled=True)
        norms = jnp.swapaxes(norms.reshape(6, OWNERS, D // OWNERS), 0, 1)
        splits = jnp.transpose(splits.reshape(6, 2, 2, OWNERS, -1), (2, 3, 0, 1, 4))
        codes = jnp.zeros((2, OWNERS, CELLS // (2 * OWNERS), D), BF)
        codes = codes.at[:, :, 0:6, : norms.shape[2]].set(norms)
        for side in range(2):
            lane = side * (D // 2) + 128
            codes = codes.at[:, :, 0:6, lane : lane + splits.shape[4]].set(splits[:, :, :, side])
        table = jnp.concatenate([table, codes.reshape(2, -1, D)], axis=1)
        attn_mine = jnp.concatenate([attn_mine, jnp.where(c == 0, table[0], table[1])])
        attn_other = jnp.concatenate([attn_other, jnp.where(c == 0, table[1], table[0])])
        first_deps = ()

    emb, normed1, q, k, v, p, mixed, after, normed2, w_attn, vec, token = attention_forward(
        scal, crop_boxes, block_input, attn_mine, attn_other, grids, first_deps
    )
    deps = ()
    if direct:
        half, token = assemble(
            where, ((0, 0), (1, size1), (2, size1), (4, 0), (3, 0)), (own2, x2, y2, x3, y3), 0, dp_size,
            (token,),
        )
        up_pair = half, place.core(half)
        sent_y, sent_x, token4 = pack(where, [], x3, y3, (size2, 2 * size2, size2), deps=(token,))
        y4, x4 = place.over_y(sent_y), place.over_x(sent_x)
        deps = (token4,)
    hidden, gp, down_mine, down_other, w_up, token = up_forward(
        scal, normed2, *up_pair, vec, cotangent, grids, deps
    )
    if direct:
        half, token = assemble(
            where, ((0, 0), (1, size2), (2, size2), (4, 0), (3, 0)), (own3, x3, y3, x4, y4), 0, dp_size,
            (token,),
        )
        down_pair = half, place.core(half)
        down_other, token = behind(down_other, token)
        sent, keep1, token = first_y(where, down_mine, place.core(down_other))
        got1 = place.over_y(sent)
        deps = (token,)
    out, w_down, token = down_forward(scal, hidden, *down_pair, after, vec, grids, deps)
    if direct:
        out_x = place.over_x(out)
        deps = (token,)
    ga, galow, up_mine, up_other, gb, gn, token = mlp_backward(
        scal, gp, w_down, w_up, normed2, cotangent, after, vec, mixed, grids, deps
    )
    if direct:
        out_pair, token = pair_grids(where, out, out_x, (token,))
        keep1, *sent, token1 = split_z(where, keep1, got1, deps=(token,))
        got1 = [place.over_z(sent[s - 1], s) for s in range(1, place.z_size)]
        up_other, token1 = behind(up_other, token1)
        sent_x, keep2, token2 = first_x(where, up_mine, place.core(up_other), (token1,))
        got2 = place.over_x(sent_x)
        out_far = place.core(out_pair)
        deps = (token1, token2)
    ig, dtable, gs, mine3, other3, token = attention_backward(
        scal, crop_boxes, ga, galow, mixed, p, q, k, v, emb, normed1, w_attn, vec, gn, gb, grids, deps
    )
    cells_here, norm_here = pos_table.shape[0], norm_params.shape[1]
    split_here = split_biases.shape[1]
    if direct:
        sent1, keep1, token1 = z_to_x(where, keep1, got1, (token,))
        got1 = place.over_x(sent1)
        sent_y, keep2, token2 = second_y(where, keep2, got2, (token1,))
        got2 = place.over_y(sent_y)
        ig_x = place.over_x(ig)
        other3, token2 = behind(other3, token2)
        sent_y, keep3a, sent_x, keep3b, token3 = first_both(
            where, mine3, place.core(other3), (token1, token2)
        )
        got3a, got3b = place.over_y(sent_y), place.over_x(sent_x)
        block_output, token3 = finish_grids(where, out_pair, out_far, (token3,))
        keep2, *sent, token = split_z(where, keep2, got2, deps=(token3,))
        got2 = [place.over_z(sent[s - 1], s) for s in range(1, place.z_size)]
        total2, token = sums(where, keep2, got2, (token,))
        sent_x, keep3a, sent_y, keep3b, token = second_both(
            where, keep3a, got3a, keep3b, got3b, (token,)
        )
        got3a, got3b = place.over_x(sent_x), place.over_y(sent_y)
        ig_pair, token = pair_grids(where, ig, ig_x, (token,))
        keep3, *sent, token = split_z(where, keep3a, got3a, keep3b, got3b, deps=(token,))
        got3 = [place.over_z(sent[s - 1], s) for s in range(1, place.z_size)]
        input_grad, token = finish_grids(where, ig_pair, place.core(ig_pair), (token,))
        kept, sent, tail, packed, square, _ = totals(
            where, keep1, got1, total2, keep3, got3, (token,)
        )
        got = place.core(sent)
        here, there, squares = sum_plane(place, where, packed, square)
        state = (
            front_weights, back_weights, split_biases, norm_params, pos_table,
            front_first, back_weight_first_moment, split_first, norm_first, table_first,
            front_second, back_second, split_second, norm_second, table_second,
        )
        state = [pltpu.with_memory_space_constraint(v, pltpu.HBM) for v in state]
        new = update(where, kept, got, tail, here, there, squares, state, ())
        return (block_output, input_grad, new[0][0, 0], *new[1:])
    else:

        def share(mine, other, blocks):
            low, high = jnp.where(c == 0, mine, other), jnp.where(c == 0, other, mine)
            full = jnp.stack([low, high], 1)[:, :, : blocks * HALF].astype(F32)
            full = full.reshape(OWNERS, 2, blocks, HALF, D)
            full = jnp.transpose(full, (2, 0, 1, 3, 4)).reshape(blocks, D, D)
            full = lax.psum_scatter(full, "dp", scatter_dimension=1, tiled=True)
            return lax.psum_scatter(full, "mp", scatter_dimension=2, tiled=True)

        down_share = share(down_mine, down_other, 4)
        up_share = share(up_mine, up_other, 5)
        out_share, up_share = up_share[4:], up_share[:4]
        qkv_share = share(mine3, other3, 3)
        block_output = lax.all_gather(out, "mp", axis=0, tiled=True)
        input_grad = lax.all_gather(ig, "mp", axis=0, tiled=True)
        norm_grad = jnp.concatenate([gs[2:4], gn[2:6]])
        split_grad = jnp.concatenate([gs[0:2], gb[0:4]])
        dtable = lax.psum(dtable, ("dp", "mp"))
        norm_grad = lax.psum(norm_grad, ("dp", "mp"))
        split_grad = lax.psum(split_grad, ("dp", "mp"))
        table_share = lax.dynamic_slice(dtable, (place.dp * cells_here, 0), (cells_here, D))
        norm_share = lax.dynamic_slice(norm_grad, (0, place.dp * norm_here), (6, norm_here))
        split_share = lax.dynamic_slice(
            split_grad, (0, (place.mp * dp_size + place.dp) * split_here), (6, split_here)
        )
        table_square = jnp.sum(table_share * table_share) / mp_size
    front_share = jnp.concatenate([qkv_share, up_share])
    back_share = jnp.concatenate([out_share, down_share])
    owner = (place.mp == 0).astype(F32)
    square = (
        jnp.sum(qkv_share * qkv_share)
        + jnp.sum(out_share * out_share)
        + jnp.sum(up_share * up_share)
        + jnp.sum(down_share * down_share)
        + jnp.sum(split_share * split_share)
        + owner * jnp.sum(norm_share * norm_share)
        + table_square
    )
    clip_norm = jnp.sqrt(lax.psum(square, ("dp", "mp")))
    factor = jnp.minimum(1.0, CLIP_LIMIT / (clip_norm + 1e-06))
    norm_clipped = norm_share * factor
    new_front, front_first_new, front_second_new = adam_step(
        front_weights, front_share * factor, front_first, front_second, RATE_MATRIX, DECAY_RATE
    )
    new_back, back_first_new, back_second_new = adam_step(
        back_weights,
        jnp.swapaxes(back_share, 1, 2) * factor,
        back_weight_first_moment,
        back_second,
        RATE_MATRIX,
        DECAY_RATE,
    )
    new_split, split_first_new, split_second_new = adam_step(
        split_biases, split_share * factor, split_first, split_second, RATE_VECTOR, 0.0
    )
    new_norm, norm_first_new, norm_second_new = adam_step(
        norm_params, norm_clipped, norm_first, norm_second, RATE_VECTOR, 0.0
    )
    new_table, table_first_new, table_second_new = adam_step(
        pos_table, table_share * factor, table_first, table_second, RATE_TABLE, DECAY_RATE
    )
    return (
        block_output, input_grad, clip_norm,
        new_front, new_back, new_split, new_norm, new_table,
        front_first_new, back_first_new, split_first_new, norm_first_new, table_first_new,
        front_second_new, back_second_new, split_second_new, norm_second_new, table_second_new,
        norm_clipped,
    )


def solution(mesh):
    front, back = P(None, "dp", "mp"), P(None, "mp", "dp")
    split, norm, table = P(None, ("mp", "dp")), P(None, "dp"), P("dp", None)
    state = (front, back, split, norm, table)
    rows = P("dp", None, None)
    return jax.shard_map(
        functools.partial(body, mesh.shape["dp"], mesh.shape["mp"]),
        mesh=mesh,
        in_specs=(rows, rows, P("dp", None)) + state * 3,
        out_specs=(rows, rows, P()) + state * 3 + (norm,),
        check_vma=False,
    )
```

```python
import functools

import jax
import jax.numpy as jnp
from jax import lax
from jax.experimental import pallas as pl
from jax.experimental.pallas import tpu as pltpu
from jax.sharding import PartitionSpec as P

D = 768
HEADS = 16
HEAD = D // HEADS
SIDE = 16
CELLS = 256
STEP = 5
CORES = 2

NORM_EPS = 1e-05
BETA_FIRST = 0.9
BETA_SECOND = 0.95
ADAM_EPS = 1e-08
RATE_MATRIX = 0.05
RATE_TABLE = 0.2
RATE_VECTOR = 0.5
DECAY_RATE = 0.1
CLIP_LIMIT = 0.01
MASK_FILL = -1e30
SCALE = HEAD ** (-0.5)
LOG2E = 1.4426950408889634
INV_SQRT_2PI = 0.3989422804014327

OWNERS = 8
HALF = D // (2 * OWNERS)
SMALL = 32

BF = jnp.bfloat16
F32 = jnp.float32
MIB = 1024 * 1024
NN = (((1,), (0,)), ((), ()))
NT = (((1,), (1,)), ((), ()))
TN = (((0,), (0,)), ((), ()))


NO_COST = pl.CostEstimate(flops=0, bytes_accessed=0, transcendentals=0)


def dot(a, b, dims=NN):
    return lax.dot_general(a, b, dims, preferred_element_type=F32)


def params(limit):
    return pltpu.CompilerParams(vmem_limit_bytes=limit)


def norm_stats(v):
    mean = jnp.mean(v, axis=-1, keepdims=True)
    centred = v - mean
    spread = jnp.mean(centred * centred, axis=-1, keepdims=True)
    rstd = lax.rsqrt(spread + NORM_EPS)
    return centred * rstd, rstd


def norm_back(c, gain, u, rstd):
    cg = c * gain
    mean_cg = jnp.mean(cg, axis=-1, keepdims=True)
    mean_cgu = jnp.mean(cg * u, axis=-1, keepdims=True)
    return rstd * (cg - mean_cg - u * mean_cgu)


def head_window(h):
    low = h * HEAD
    first = low // 128
    last = (low + HEAD - 1) // 128
    return first, last + 1 - first


def head_mask(h):
    first, tiles = head_window(h)
    lane = lax.broadcasted_iota(jnp.int32, (1, tiles * 128), 1) + first * 128
    return (lane >= h * HEAD) & (lane < (h + 1) * HEAD)


def crop_target(position, height, breadth, top, left):
    row = (position >> 4) - top
    col = (position & (SIDE - 1)) - left
    inside = (row >= 0) & (row < height) & (col >= 0) & (col < breadth)
    return jnp.where(inside, row * breadth + col, -1)


def load_weights(core, mine_ref, other_ref, w_ref, copy_ref, sem, token_ref):
    copy = pltpu.make_async_copy(w_ref, copy_ref, sem)

    @pl.when(pl.program_id(0) == 0)
    def _():
        token_ref[...] = jnp.zeros_like(token_ref)

        def fill(low, high):
            for b in range(2):
                rows = slice(b * D, (b + 1) * D)
                w_ref[b] = low[rows, :]
                w_ref[2 + b] = high[rows, :]

        @pl.when(core == 0)
        def _():
            fill(mine_ref, other_ref)

        @pl.when(core != 0)
        def _():
            fill(other_ref, mine_ref)

        copy.start()

    @pl.when(pl.program_id(0) == pl.num_programs(0) - 1)
    def _():
        copy.wait()


def attention_forward_kernel(
    scal, crop, x_ref, mine_ref, other_ref,
    emb_ref, n1_ref, q_ref, k_ref, v_ref, p_ref, mixed_ref, after_ref, n2_ref, wcopy_ref, vec_ref, token_ref,
    w_ref, table_ref, sem,
):
    load_weights(scal[1], mine_ref, other_ref, w_ref, wcopy_ref, sem, token_ref)
    part = CELLS // (2 * OWNERS)

    @pl.when(pl.program_id(0) == 0)
    def _():
        for at, ref in ((scal[1], mine_ref), (1 - scal[1], other_ref)):
            for dp in range(OWNERS):
                row = pl.ds(pl.multiple_of((2 * dp + at) * part, part), part)
                table_ref[row, :] = ref[2 * D + dp * part : 2 * D + (dp + 1) * part, :]
        vec_ref[...] = jnp.zeros_like(vec_ref)
        wide, thin = D // OWNERS, D // (4 * OWNERS)
        first = 2 * D + CELLS // 2

        def unpack(ref, core):
            for dp in range(OWNERS):
                rows = slice(first + dp * part, first + dp * part + 6)
                if core == 0:
                    vec_ref[0:6, dp * wide : (dp + 1) * wide] = ref[rows, 0:wide].astype(F32)
                for x in range(2):
                    lane = x * (D // 2) + 128
                    at = (2 * x + core) * (D // 4) + dp * thin
                    vec_ref[8:14, at : at + thin] = ref[rows, lane : lane + thin].astype(F32)

        @pl.when(scal[1] == 0)
        def _():
            unpack(mine_ref, 0)
            unpack(other_ref, 1)

        @pl.when(scal[1] != 0)
        def _():
            unpack(other_ref, 0)
            unpack(mine_ref, 1)

    grid = scal[0] + pl.program_id(0)
    height, breadth, top, left = crop[grid, 0], crop[grid, 1], crop[grid, 2], crop[grid, 3]
    target = crop_target(
        lax.broadcasted_iota(jnp.int32, (1, CELLS), 1), height, breadth, top, left
    )
    cell = lax.broadcasted_iota(jnp.int32, (CELLS, CELLS), 0)
    onehot = jnp.where(cell == target, 1.0, 0.0).astype(BF)
    emb = x_ref[0].astype(F32) + dot(onehot, table_ref[...])
    emb_ref[...] = emb
    u, _ = norm_stats(emb)
    n1 = (u * vec_ref[0:1, :] + vec_ref[1:2, :]).astype(BF)
    n1_ref[...] = n1
    q_ref[...] = (dot(n1, w_ref[0]) + vec_ref[8:9, :]).astype(BF)
    k_ref[...] = dot(n1, w_ref[1]).astype(BF)
    v_ref[...] = (dot(n1, w_ref[2]) + vec_ref[9:10, :]).astype(BF)
    valid = lax.broadcasted_iota(jnp.int32, (1, CELLS), 1) < height * breadth
    tiles_out = [None] * (D // 128)
    for h in range(HEADS):
        first, tiles = head_window(h)
        lanes = slice(first * 128, (first + tiles) * 128)
        mask = head_mask(h)
        qh = jnp.where(mask, q_ref[:, lanes], 0).astype(BF)
        s = jnp.where(valid, dot(qh, k_ref[:, lanes], NT), MASK_FILL)
        top_score = jnp.max(s, axis=-1, keepdims=True)
        e = jnp.exp2((s - top_score) * (SCALE * LOG2E))
        p_ref[0, h] = (e * (1.0 / jnp.sum(e, axis=-1, keepdims=True))).astype(BF)
    for h in range(HEADS):
        first, tiles = head_window(h)
        lanes = slice(first * 128, (first + tiles) * 128)
        mask = head_mask(h)
        vh = jnp.where(mask, v_ref[:, lanes], 0).astype(BF)
        o = dot(p_ref[0, h], vh)
        for t in range(tiles):
            part = o[:, t * 128 : (t + 1) * 128]
            at = first + t
            tiles_out[at] = part if tiles_out[at] is None else tiles_out[at] + part
    for t in range(D // 128):
        mixed_ref[:, t * 128 : (t + 1) * 128] = tiles_out[t].astype(BF)
    attention = dot(mixed_ref[...], w_ref[3], NT)
    after = emb_ref[...] + attention + vec_ref[2:3, :]
    after_ref[...] = after
    u2, _ = norm_stats(after)
    n2_ref[...] = (u2 * vec_ref[3:4, :] + vec_ref[4:5, :]).astype(BF)


def up_kernel(
    scal, n2_ref, low_ref, high_ref, vec_ref, g_ref,
    hidden_ref, gp_ref, mine_ref, other_ref, wcopy_ref, token_ref, gt_ref, w_ref, sem,
):
    j = pl.program_id(0)
    load_weights(scal[1], low_ref, high_ref, w_ref, wcopy_ref, sem, token_ref)
    grids = g_ref.shape[0]

    @pl.when(j == 0)
    def _():
        for n in range(grids):
            gt_ref[:, n * CELLS : (n + 1) * CELLS] = g_ref[n].T

    bias = vec_ref[pl.ds(10 + j, 1), :]
    for n in range(grids):
        rows = slice(n * CELLS, (n + 1) * CELLS)
        pre = dot(n2_ref[rows, :], w_ref[j]) + bias
        phi = 0.5 + 0.5 * lax.erf(pre * (0.5**0.5))
        density = jnp.exp2(pre * pre * (-0.5 * LOG2E)) * INV_SQRT_2PI
        hidden_ref[0, rows, :] = (pre * phi).astype(BF)
        gp_ref[0, rows, :] = (phi + pre * density).astype(BF)
    grad = dot(gt_ref[...], hidden_ref[0]).astype(BF)
    keep(scal[1], 0, grad, mine_ref, other_ref)


def keep(core, at, grad, mine_ref, other_ref):
    parts = grad.reshape(OWNERS, 2, HALF, D)
    rows = slice(at * HALF, (at + 1) * HALF)

    @pl.when(core == 0)
    def _():
        mine_ref[:, rows, :] = parts[:, 0]
        other_ref[:, rows, :] = parts[:, 1]

    @pl.when(core != 0)
    def _():
        mine_ref[:, rows, :] = parts[:, 1]
        other_ref[:, rows, :] = parts[:, 0]


def down_kernel(
    scal, hidden_ref, low_ref, high_ref, after_ref, vec_ref, out_ref, wcopy_ref, token_ref, down_ref, sem
):
    load_weights(scal[1], low_ref, high_ref, down_ref, wcopy_ref, sem, token_ref)
    total = dot(hidden_ref[0], down_ref[0], NT)
    for j in range(1, 4):
        total = total + dot(hidden_ref[j], down_ref[j], NT)
    out_ref[0] = (after_ref[...] + total + vec_ref[5:6, :]).astype(BF)


def mlp_kernel(
    scal, gp_ref, down_ref, up_ref, n2_ref, g_ref, after_any, vec_ref, mixed_any,
    ga_ref, galow_ref, mine_ref, other_ref, gb_ref, gn_ref, token_ref,
    dn2_acc, n2t_ref, gpre_ref, after_ref, mixed_ref, sem,
):
    j = pl.program_id(0)
    grids = g_ref.shape[0]
    core = scal[1]
    late = (
        pltpu.make_async_copy(after_any, after_ref, sem.at[0]),
        pltpu.make_async_copy(mixed_any, mixed_ref, sem.at[1]),
    )

    @pl.when(j == 0)
    def _():
        for copy in late:
            copy.start()
        for n in range(grids):
            rows = slice(n * CELLS, (n + 1) * CELLS)
            n2t_ref[:, rows] = n2_ref[rows, :].T
        dn2_acc[...] = jnp.zeros_like(dn2_acc)
        gb_ref[...] = jnp.zeros_like(gb_ref)
        gn_ref[...] = jnp.zeros_like(gn_ref)
        token_ref[...] = jnp.zeros_like(token_ref)

    @pl.when(j < 4)
    def _():
        colsum = jnp.zeros((1, D), F32)
        for n in range(grids):
            rows = slice(n * CELLS, (n + 1) * CELLS)
            gh = dot(g_ref[n], down_ref[0])
            gpre = (gh * gp_ref[0, rows, :].astype(F32)).astype(BF)
            gpre_ref[rows, :] = gpre
            colsum = colsum + jnp.sum(gpre.astype(F32), axis=0, keepdims=True)
        for n in range(grids):
            rows = slice(n * CELLS, (n + 1) * CELLS)
            dn2_acc[rows, :] += dot(gpre_ref[rows, :], up_ref[0], NT)
        gb_ref[pl.ds(j, 1), :] = colsum
        keep(core, 0, dot(n2t_ref[...], gpre_ref[...]).astype(BF), mine_ref, other_ref)

    @pl.when(j == 4)
    def _():
        for copy in late:
            copy.wait()
        sums = [jnp.zeros((1, D), F32)] * 4
        for n in range(grids):
            rows = slice(n * CELLS, (n + 1) * CELLS)
            u, rstd = norm_stats(after_ref[rows, :])
            c = dn2_acc[rows, :]
            g = g_ref[n].astype(F32)
            ga = g + norm_back(c, vec_ref[3:4, :], u, rstd)
            ga_ref[rows, :] = ga
            galow = ga.astype(BF)
            galow_ref[rows, :] = galow
            n2t_ref[:, rows] = galow.T
            parts = (ga, c * u, c, g)
            sums = [s + jnp.sum(v, axis=0, keepdims=True) for s, v in zip(sums, parts)]
        for i in range(4):
            gn_ref[2 + i : 3 + i, :] = sums[i]
        keep(core, 0, dot(n2t_ref[...], mixed_ref[...]).astype(BF), mine_ref, other_ref)


def attention_backward_kernel(
    scal, crop, ga_ref, galow_ref, mixed_ref, p_ref, q_ref, k_ref, v_ref, emb_ref, n1_ref,
    w_ref, vec_ref, gn_ref, gb_ref,
    ig_ref, table_out, gs_out, mine_ref, other_ref, token_ref,
    dm_ref, ds_ref, dq_all, dk_all, dv_all, n1t_ref, table_ref, gs_ref,
):
    i = pl.program_id(0)
    grids = pl.num_programs(0) - 1
    core = scal[1]

    @pl.when(i == 0)
    def _():
        table_ref[...] = jnp.zeros_like(table_ref)
        gs_ref[...] = jnp.zeros_like(gs_ref)
        token_ref[...] = jnp.zeros_like(token_ref)

    @pl.when(i < grids)
    def _():
        grid = scal[0] + i
        height, breadth, top, left = crop[grid, 0], crop[grid, 1], crop[grid, 2], crop[grid, 3]
        here = pl.ds(pl.multiple_of(i * CELLS, CELLS), CELLS)
        n1t_ref[:, here] = n1_ref[...].T
        dm_ref[...] = dot(galow_ref[...], w_ref[3]).astype(BF)
        outs = [[None] * (D // 128) for _ in range(3)]
        for h in range(HEADS):
            first, tiles = head_window(h)
            lanes = slice(first * 128, (first + tiles) * 128)
            mask = head_mask(h)
            dmh = jnp.where(mask, dm_ref[:, lanes], 0).astype(BF)
            dp = dot(dmh, v_ref[:, lanes], NT)
            delta = jnp.sum(
                dmh.astype(F32) * mixed_ref[:, lanes].astype(F32), axis=-1, keepdims=True
            )
            ds_ref[h] = (p_ref[0, h].astype(F32) * (dp - delta)).astype(BF)
        for h in range(HEADS):
            first, tiles = head_window(h)
            lanes = slice(first * 128, (first + tiles) * 128)
            mask = head_mask(h)
            qh = jnp.where(mask, q_ref[:, lanes], 0).astype(BF)
            kh = jnp.where(mask, k_ref[:, lanes], 0).astype(BF)
            dmh = jnp.where(mask, dm_ref[:, lanes], 0).astype(BF)
            ds = ds_ref[h]
            got = (dot(ds, kh), dot(ds, qh, TN), dot(p_ref[0, h], dmh, TN))
            for o in range(3):
                for t in range(tiles):
                    part = got[o][:, t * 128 : (t + 1) * 128]
                    at = first + t
                    outs[o][at] = part if outs[o][at] is None else outs[o][at] + part
        for t in range(D // 128):
            lanes = slice(t * 128, (t + 1) * 128)
            dq_all[here, lanes] = (outs[0][t] * SCALE).astype(BF)
            dk_all[here, lanes] = (outs[1][t] * SCALE).astype(BF)
            dv_all[here, lanes] = outs[2][t].astype(BF)
        dq, dk, dv = dq_all[here, :], dk_all[here, :], dv_all[here, :]
        c = dot(dq, w_ref[0], NT) + dot(dk, w_ref[1], NT) + dot(dv, w_ref[2], NT)
        u, rstd = norm_stats(emb_ref[...])
        ge = ga_ref[...] + norm_back(c, vec_ref[0:1, :], u, rstd)
        high = ge.astype(BF)
        ig_ref[0] = high
        low = (ge - high.astype(F32)).astype(BF)
        target = crop_target(
            lax.broadcasted_iota(jnp.int32, (CELLS, 1), 0), height, breadth, top, left
        )
        cell = lax.broadcasted_iota(jnp.int32, (CELLS, CELLS), 1)
        onehot = jnp.where(cell == target, 1.0, 0.0).astype(BF)
        table_ref[...] += dot(onehot, high) + dot(onehot, low)
        for row, v in enumerate((dq.astype(F32), dv.astype(F32), c * u, c)):
            gs_ref[row : row + 1, :] += jnp.sum(v, axis=0, keepdims=True)

    @pl.when(i == grids)
    def _():
        for b, ref in enumerate((dq_all, dk_all, dv_all)):
            keep(core, b, dot(n1t_ref[...], ref[...]).astype(BF), mine_ref, other_ref)
        table_out[...] = table_ref[...]
        gs_out[...] = gs_ref[...]
        start = 3 * HALF
        table = table_ref[...].astype(BF).reshape(OWNERS, 2, 16, D)
        norm = jnp.concatenate([gs_ref[2:4, :], gn_ref[2:6, :]], axis=0).astype(BF)
        split = jnp.concatenate([gs_ref[0:2, :], gb_ref[0:4, :]], axis=0).astype(BF)
        wide, thin = D // OWNERS, D // (4 * OWNERS)
        side = D // 2

        def small(ref, half):
            ref[:, start : start + 16, :] = table[:, half]
            ref[:, start + 16 : start + 32, :] = jnp.zeros((OWNERS, 16, D), BF)
            for dp in range(OWNERS):
                for x in range(2):
                    lane = x * side
                    ref[dp, start + 16 : start + 22, lane : lane + wide] = norm[
                        :, dp * wide : (dp + 1) * wide
                    ]
                    at = (2 * x + half) * (D // 4) + dp * thin
                    ref[dp, start + 24 : start + 30, lane : lane + thin] = split[:, at : at + thin]

        @pl.when(core == 0)
        def _():
            small(mine_ref, 0)
            small(other_ref, 1)

        @pl.when(core != 0)
        def _():
            small(mine_ref, 1)
            small(other_ref, 0)


def sds(shape, dtype):
    return jax.ShapeDtypeStruct(shape, dtype)


TOKEN = sds((8, 128), F32)


def in_hbm(shape):
    return pltpu.HBM(shape.shape, shape.dtype)


def behind(value, token):
    return lax.optimization_barrier((value, token))


ANY = pl.BlockSpec(memory_space=pl.ANY)


def half_shape(blocks, extra=0):
    return sds((OWNERS, blocks * HALF + extra, D), BF)


def whole_block(shape, buffers=None):
    zeros = (0,) * len(shape)
    mode = None if buffers is None else pl.Buffered(buffers)
    return pl.BlockSpec(shape, lambda i, *_: zeros, pipeline_mode=mode)


def attention_forward(scal, crop, x, mine, other, grids, deps=()):
    tokens = grids * CELLS
    rows = pl.BlockSpec((CELLS, D), lambda i, *_: (i, 0))
    spec = pltpu.PrefetchScalarGridSpec(
        num_scalar_prefetch=2,
        grid=(grids,),
        in_specs=[
            pl.BlockSpec((1, CELLS, D), lambda i, s, c: (s[0] + i, 0, 0)),
            whole_block(mine.shape, 1),
            whole_block(mine.shape, 1),
        ] + [ANY] * len(deps),
        out_specs=[
            rows, rows, rows, rows, rows,
            pl.BlockSpec((1, HEADS, CELLS, CELLS), lambda i, *_: (i, 0, 0, 0)),
            rows, rows, rows,
            pl.BlockSpec(memory_space=pl.ANY),
            whole_block((16, D)),
            whole_block((8, 128)),
        ],
        scratch_shapes=[
            pltpu.VMEM((4, D, D), BF), pltpu.VMEM((CELLS, D), BF), pltpu.SemaphoreType.DMA,
        ],
    )
    low, full = pltpu.HBM((tokens, D), BF), pltpu.HBM((tokens, D), F32)
    return pl.pallas_call(
        ignoring(attention_forward_kernel, 5, len(deps)),
        grid_spec=spec,
        out_shape=[
            full, low, low, low, low, pltpu.HBM((grids, HEADS, CELLS, CELLS), BF), low, full,
            sds((tokens, D), BF), pltpu.HBM((4, D, D), BF), sds((16, D), F32), TOKEN,
        ],
        compiler_params=params(40 * MIB),
        cost_estimate=NO_COST,
        name="attention_forward",
    )(scal, crop, x, mine, other, *deps)


def up_forward(scal, n2, mine, other, vec, cotangent, grids, deps=()):
    tokens = grids * CELLS
    block = pl.BlockSpec((1, tokens, D), lambda j, *_: (j, 0, 0))
    half = pl.BlockSpec((OWNERS, HALF, D), lambda j, *_: (0, j, 0))
    spec = pltpu.PrefetchScalarGridSpec(
        num_scalar_prefetch=1,
        grid=(4,),
        in_specs=[
            whole_block((tokens, D), 1),
            whole_block((2 * D, D), 1),
            whole_block((2 * D, D), 1),
            whole_block((16, D)),
            pl.BlockSpec((grids, CELLS, D), lambda j, s: (s[2], 0, 0), pipeline_mode=pl.Buffered(1)),
        ] + [ANY] * len(deps),
        out_specs=[block, block, half, half, pl.BlockSpec(memory_space=pl.ANY), whole_block((8, 128))],
        scratch_shapes=[
            pltpu.VMEM((D, tokens), BF), pltpu.VMEM((4, D, D), BF), pltpu.SemaphoreType.DMA,
        ],
    )
    return pl.pallas_call(
        ignoring(up_kernel, 6, len(deps)),
        grid_spec=spec,
        out_shape=[
            sds((4, tokens, D), BF), pltpu.HBM((4, tokens, D), BF), half_shape(4), in_hbm(half_shape(4)),
            pltpu.HBM((4, D, D), BF), TOKEN,
        ],
        compiler_params=params(40 * MIB * tokens // 768),
        cost_estimate=NO_COST,
        name="up_forward",
    )(scal, n2, mine, other, vec, cotangent, *deps)


def down_forward(scal, hidden, mine, other, after, vec, grids, deps=()):
    tokens = grids * CELLS
    spec = pltpu.PrefetchScalarGridSpec(
        num_scalar_prefetch=1,
        grid=(grids,),
        in_specs=[
            pl.BlockSpec((4, CELLS, D), lambda i, *_: (0, i, 0)),
            whole_block((2 * D, D), 1),
            whole_block((2 * D, D), 1),
            pl.BlockSpec((CELLS, D), lambda i, *_: (i, 0)),
            whole_block((16, D)),
        ] + [ANY] * len(deps),
        out_specs=[
            pl.BlockSpec((1, CELLS, D), lambda i, *_: (i, 0, 0)),
            pl.BlockSpec(memory_space=pl.ANY),
            whole_block((8, 128)),
        ],
        scratch_shapes=[pltpu.VMEM((4, D, D), BF), pltpu.SemaphoreType.DMA],
    )
    return pl.pallas_call(
        ignoring(down_kernel, 6, len(deps)),
        grid_spec=spec,
        out_shape=[pltpu.HBM((grids, CELLS, D), BF), pltpu.HBM((4, D, D), BF), TOKEN],
        compiler_params=params(24 * MIB),
        cost_estimate=NO_COST,
        name="down_forward",
    )(scal, hidden, mine, other, after, vec, *deps)


def mlp_backward(scal, gp, down, up, n2, cotangent, after, vec, mixed, grids, deps=()):
    tokens = grids * CELLS
    last = lambda j: jnp.minimum(j, 3)
    block = pl.BlockSpec((1, tokens, D), lambda j, *_: (last(j), 0, 0))
    weight = pl.BlockSpec((1, D, D), lambda j, *_: (last(j), 0, 0))
    half = pl.BlockSpec((OWNERS, HALF, D), lambda j, *_: (0, j, 0))
    rows = whole_block((tokens, D))
    any_spec = pl.BlockSpec(memory_space=pl.ANY)
    spec = pltpu.PrefetchScalarGridSpec(
        num_scalar_prefetch=1,
        grid=(5,),
        in_specs=[
            block, weight, weight, whole_block((tokens, D), 1),
            pl.BlockSpec((grids, CELLS, D), lambda j, s: (s[2], 0, 0), pipeline_mode=pl.Buffered(1)),
            any_spec, whole_block((16, D)), any_spec,
        ] + [ANY] * len(deps),
        out_specs=[rows, rows, half, half, whole_block((8, D)), whole_block((8, D)), whole_block((8, 128))],
        scratch_shapes=[
            pltpu.VMEM((tokens, D), F32), pltpu.VMEM((D, tokens), BF), pltpu.VMEM((tokens, D), BF),
            pltpu.VMEM((tokens, D), F32), pltpu.VMEM((tokens, D), BF),
            pltpu.SemaphoreType.DMA((2,)),
        ],
    )
    return pl.pallas_call(
        ignoring(mlp_kernel, 9, len(deps)),
        grid_spec=spec,
        out_shape=[
            sds((tokens, D), F32), sds((tokens, D), BF),
            half_shape(5), in_hbm(half_shape(5)), sds((8, D), F32), sds((8, D), F32), TOKEN,
        ],
        compiler_params=params(40 * MIB * tokens // 768),
        cost_estimate=NO_COST,
        name="mlp_backward",
    )(scal, gp, down, up, n2, cotangent, after, vec, mixed, *deps)


def attention_backward(scal, crop, ga, galow, mixed, p, q, k, v, emb, n1, w, vec, gn, gb, grids, deps=()):
    tokens = grids * CELLS
    last = lambda i: jnp.minimum(i, grids - 1)
    rows = pl.BlockSpec((CELLS, D), lambda i, *_: (last(i), 0))
    half = half_shape(3, SMALL)
    few = whole_block((8, D))
    spec = pltpu.PrefetchScalarGridSpec(
        num_scalar_prefetch=2,
        grid=(grids + 1,),
        in_specs=[
            rows, rows, rows,
            pl.BlockSpec((1, HEADS, CELLS, CELLS), lambda i, *_: (last(i), 0, 0, 0)),
            rows, rows, rows, rows, rows,
            whole_block((4, D, D), 1),
            whole_block((16, D)), few, few,
        ] + [ANY] * len(deps),
        out_specs=[
            pl.BlockSpec((1, CELLS, D), lambda i, *_: (last(i), 0, 0)),
            whole_block((CELLS, D)),
            few,
            whole_block(half.shape, 1), whole_block(half.shape, 1),
            whole_block((8, 128)),
        ],
        scratch_shapes=[pltpu.VMEM((CELLS, D), BF), pltpu.VMEM((HEADS, CELLS, CELLS), BF)]
        + [pltpu.VMEM((tokens, D), BF)] * 3
        + [pltpu.VMEM((D, tokens), BF), pltpu.VMEM((CELLS, D), F32), pltpu.VMEM((8, D), F32)],
    )
    return pl.pallas_call(
        ignoring(attention_backward_kernel, 15, len(deps)),
        grid_spec=spec,
        out_shape=[
            pltpu.HBM((grids, CELLS, D), BF), sds((CELLS, D), F32), sds((8, D), F32), half, in_hbm(half), TOKEN,
        ],
        compiler_params=params(40 * MIB),
        cost_estimate=NO_COST,
        name="attention_backward",
    )(scal, crop, ga, galow, mixed, p, q, k, v, emb, n1, w, vec, gn, gb, *deps)


class Place:
    def __init__(self, dp_size, mp_size):
        self.z_size = dp_size // 2
        dp, mp = lax.axis_index("dp"), lax.axis_index("mp")
        self.dp, self.mp = dp, mp
        self.z, self.y = dp // 2, dp % 2
        self.x, self.c = mp // 2, mp % 2
        self.core_pairs = [(i, i ^ 1) for i in range(mp_size)]
        self.x_pairs = [(i, i ^ 2) for i in range(mp_size)]
        self.y_pairs = [(i, i ^ 1) for i in range(dp_size)]
        self.z_shift = [
            [(i, ((i // 2 + s) % self.z_size) * 2 + i % 2) for i in range(dp_size)]
            for s in range(self.z_size)
        ]

        self.corner_pairs = [
            (d * mp_size + m, (d ^ 1) * mp_size + (m ^ 2))
            for d in range(dp_size)
            for m in range(mp_size)
        ]

    def core(self, v):
        return lax.ppermute(v, "mp", self.core_pairs)

    def over_corner(self, v):
        return lax.ppermute(v, ("dp", "mp"), self.corner_pairs)

    def over_x(self, v):
        return lax.ppermute(v, "mp", self.x_pairs)

    def over_y(self, v):
        return lax.ppermute(v, "dp", self.y_pairs)

    def over_z(self, v, shift):
        return lax.ppermute(v, "dp", self.z_shift[shift])


def ignoring(kernel, at, count):
    return lambda *refs: kernel(*refs[:at], *refs[at + count :])


def assemble_kernel(rows, extra, depth, views, where, *refs):
    count = 1 + max(at for at, _ in views)
    out, token = refs[count:]
    token[...] = jnp.zeros_like(token)
    z, y, x = where[0], where[1], where[2]
    unit = rows + extra
    held = [(refs[at], row) for at, row in views]
    for s in range(depth):
        zs = lax.rem(z - s + depth, depth)
        for xr in range(2):
            for yr in range(2):
                xs = x if xr == 0 else 1 - x
                ys = y if yr == 0 else 1 - y
                dp = zs * 2 + ys
                lane = pl.ds(pl.multiple_of(xs * (D // 2), D // 2), D // 2)
                for b in range(2):
                    if xr and yr:
                        ref, first = held[3 + b]
                        first += s * unit
                    else:
                        ref, first = held[xr + 2 * yr]
                        first += (b * depth + s) * unit
                    row = pl.ds(pl.multiple_of(b * D + dp * rows, rows), rows)
                    out[row, lane] = ref[first : first + rows, :]
                    if extra:
                        at = 2 * D + b * depth * 2 * extra + dp * extra
                        row = pl.ds(pl.multiple_of(at, extra), extra)
                        out[row, lane] = ref[first + rows : first + unit, :]


def assemble(where, views, pieces, extra, dp_size, deps=()):
    kernel = functools.partial(assemble_kernel, D // dp_size, extra, dp_size // 2, views)
    shape = sds((2 * D + 2 * dp_size * extra, D), BF)
    return call(kernel, "assemble", where, pieces, [shape], deps)


def gather_z(place, u):
    return [u] + [place.over_z(u, s) for s in range(1, place.z_size)]


def call(kernel, name, where, ins, shapes, deps=(), limit=16):
    vmem = pl.BlockSpec(memory_space=pltpu.VMEM)
    return pl.pallas_call(
        ignoring(kernel, 1 + len(ins), len(deps)),
        in_specs=[pl.BlockSpec(memory_space=pltpu.SMEM)] + [vmem] * len(ins) + [ANY] * len(deps),
        out_specs=[vmem] * (len(shapes) + 1),
        out_shape=[*shapes, TOKEN],
        compiler_params=params(limit * MIB),
        cost_estimate=NO_COST,
        name=name,
    )(where, *ins, *deps)


def shards_kernel(where, front, back, mine, sent, token):
    token[...] = jnp.zeros_like(token)
    chunks = ((0, 1, 2, 7), (3, 4, 5, 6), (8, 9, 10, 11))

    def fill(low, high):
        for k, blocks in enumerate(chunks):
            for j, at in enumerate(blocks):
                value = front[at] if at < 7 else back[at - 7].T
                (low if j < 2 else high)[k, j % 2] = value.astype(BF)

    @pl.when(where[3] == 0)
    def _():
        fill(mine, sent)

    @pl.when(where[3] != 0)
    def _():
        fill(sent, mine)


def pack_kernel(count, has_next, unit_at, where, *refs):
    parts, refs = refs[:count], refs[count:]
    half, lows = 0, None
    if has_next:
        by_x, by_y, refs = refs[0], refs[1], refs[2:]
        half = has_next
    token = refs[-1]
    token[...] = jnp.zeros_like(token)
    outs = refs[:-1]
    if unit_at:
        units, outs = outs[0], outs[1:]
        outs[-1][...] = units[unit_at]
        outs = outs[:-1]
    if half:
        first_x, first_y = half[0], half[1]
        size = half[2]
        outs[-2][:size, :] = by_x[first_x : first_x + size, :]
        outs[-1][:size, :] = by_y[first_y : first_y + size, :]
    if count:
        unit = parts[0].shape[1]
        for b in range(2):
            for s in range(count):
                value = parts[s][b]
                at = (b * count + s) * unit
                outs[0][at : at + unit, :] = value
                if half:
                    outs[-2][size + at : size + at + unit, :] = value
                    outs[-1][size + at : size + at + unit, :] = value


def pack(where, parts, by_x, by_y, half, units=None, unit_at=0, deps=()):
    count = len(parts)
    shapes = []
    rows = 2 * count * parts[0].shape[1] if count else 0
    if count:
        shapes.append(sds((rows, D // 2), BF))
    ins = list(parts)
    if half:
        ins += [by_x, by_y]
        shapes += [sds((half[2] + rows, D // 2), BF)] * 2
    if unit_at:
        ins.append(units)
        shapes.append(sds(units.shape[1:], BF))
    kernel = functools.partial(pack_kernel, count, half, unit_at)
    return call(kernel, "pack", where, ins, shapes, deps)


def add(a, b):
    return a.astype(F32) + b.astype(F32)


def dp_of(z, y):
    return z * 2 + y


def split_y(y, value_at, depth, send, keep):
    for z in range(depth):
        send[z] = value_at(dp_of(z, 1 - y)).astype(BF)
        keep[z] = value_at(dp_of(z, y)).astype(BF)


def split_x(x, value, send, keep):
    side = D // 2
    left, right = value[:, :side].astype(BF), value[:, side:].astype(BF)

    @pl.when(x == 0)
    def _():
        send[...] = right
        keep[...] = left

    @pl.when(x != 0)
    def _():
        send[...] = left
        keep[...] = right


def first_y_kernel(where, mine, got, send, keep, token):
    token[...] = jnp.zeros_like(token)
    split_y(where[1], lambda dp: add(mine[dp], got[dp]), OWNERS // 2, send, keep)


def first_y(where, mine, got, deps=()):
    rows = mine.shape[1]
    shape = sds((OWNERS // 2, rows, D), BF)
    return call(first_y_kernel, "first_y", where, [mine, got], [shape, shape], deps)


def first_both_kernel(cut, where, mine, got, send_y, keep_y, send_x, keep_x, token):
    token[...] = jnp.zeros_like(token)
    depth = OWNERS // 2
    split_y(where[1], lambda dp: add(mine[dp, :cut], got[dp, :cut]), depth, send_y, keep_y)
    for dp in range(OWNERS):
        split_x(where[2], add(mine[dp, cut:], got[dp, cut:]), send_x.at[dp], keep_x.at[dp])


def first_both(where, mine, got, deps=()):
    rows = mine.shape[1]
    cut = (2 * rows // 3) // 16 * 16
    over_y = sds((OWNERS // 2, cut, D), BF)
    over_x = sds((OWNERS, rows - cut, D // 2), BF)
    kernel = functools.partial(first_both_kernel, cut)
    return call(kernel, "first_both", where, [mine, got], [over_y, over_y, over_x, over_x], deps)


def first_x_kernel(where, mine, got, send, keep, token):
    token[...] = jnp.zeros_like(token)
    for dp in range(OWNERS):
        split_x(where[2], add(mine[dp], got[dp]), send.at[dp], keep.at[dp])


def first_x(where, mine, got, deps=()):
    shape = sds((OWNERS, mine.shape[1], D // 2), BF)
    return call(first_x_kernel, "first_x", where, [mine, got], [shape, shape], deps)


def second_y_kernel(where, mine, got, send, keep, token):
    token[...] = jnp.zeros_like(token)
    split_y(where[1], lambda dp: add(mine[dp], got[dp]), OWNERS // 2, send, keep)


def second_y(where, mine, got, deps=()):
    shape = sds((OWNERS // 2,) + mine.shape[1:], BF)
    return call(second_y_kernel, "second_y", where, [mine, got], [shape, shape], deps)


def second_both_kernel(where, keep_y, got_y, keep_x, got_x, send_a, left_a, send_b, left_b, token):
    token[...] = jnp.zeros_like(token)
    depth = OWNERS // 2
    for z in range(depth):
        split_x(where[2], add(keep_y[z], got_y[z]), send_a.at[z], left_a.at[z])
    split_y(where[1], lambda dp: add(keep_x[dp], got_x[dp]), depth, send_b, left_b)


def second_both(where, keep_y, got_y, keep_x, got_x, deps=()):
    over_x = sds((OWNERS // 2, keep_y.shape[1], D // 2), BF)
    over_y = sds((OWNERS // 2, keep_x.shape[1], D // 2), BF)
    ins = [keep_y, got_y, keep_x, got_x]
    return call(second_both_kernel, "second_both", where, ins, [over_x, over_x, over_y, over_y], deps)


def split_z_kernel(pairs, where, *refs):
    ins, outs = refs[: 2 * pairs], refs[2 * pairs : -1]
    refs[-1][...] = jnp.zeros_like(refs[-1])
    depth = ins[0].shape[0]
    for s in range(depth):
        z = lax.rem(where[0] + s, depth)
        row = 0
        for i in range(pairs):
            value = add(ins[2 * i][z], ins[2 * i + 1][z]).astype(BF)
            outs[s][row : row + value.shape[0], :] = value
            row += value.shape[0]


def split_z(where, *ins, deps=()):
    depth, width = ins[0].shape[0], ins[0].shape[2]
    rows = sum(v.shape[1] for v in ins[::2])
    kernel = functools.partial(split_z_kernel, len(ins) // 2)
    return call(kernel, "split_z", where, list(ins), [sds((rows, width), BF)] * depth, deps)


def z_to_x_kernel(where, keep, *refs):
    got, (send, left, token) = refs[:-3], refs[-3:]
    token[...] = jnp.zeros_like(token)
    total = keep[...].astype(F32)
    for ref in got:
        total = total + ref[...].astype(F32)
    split_x(where[2], total, send, left)


def z_to_x(where, keep, got, deps=()):
    shape = sds((keep.shape[0], D // 2), BF)
    return call(z_to_x_kernel, "z_to_x", where, [keep, *got], [shape, shape], deps)


def pair_kernel(where, own, by_x, out, token):
    token[...] = jnp.zeros_like(token)
    out[0] = own[...]
    out[1] = by_x[...]


def collect_kernel(where, here, there, out, token):
    token[...] = jnp.zeros_like(token)
    x, c = where[2], where[3]
    grids = here.shape[1]
    for piece, core in ((here, c), (there, 1 - c)):
        for half in range(2):
            mp = 2 * (x if half == 0 else 1 - x) + core
            for n in range(grids):
                out[mp * grids + n] = piece[half, n]


def pair_grids(where, own, by_x, deps=()):
    return call(pair_kernel, "pair", where, [own, by_x], [sds((2,) + own.shape, own.dtype)], deps)


def finish_grids(where, here, there, deps=()):
    shape = sds((here.shape[0] * 2 * here.shape[1],) + here.shape[2:], here.dtype)
    return call(collect_kernel, "collect", where, [here, there], [shape], deps)


def plane_kernel(where, own, by_x, by_y, by_corner, out, token):
    token[...] = jnp.zeros_like(token)
    out[0:16, :] = own[0:16, :]
    out[16:32, :] = by_x[0:16, :]
    here = own[16:24, :] + by_x[16:24, :]
    out[32:40, :] = here + (by_y[...] + by_corner[...])


def sum_plane(place, where, packed, square):
    ins = [packed, place.over_x(packed), place.over_y(square), place.over_corner(square)]
    here, _ = call(plane_kernel, "plane", where, ins, [sds((40, D // 2), F32)])
    there = place.core(here)
    value = here[32:40, :128] + there[32:40, :128]
    return here, there, [value] + [place.over_z(value, s) for s in range(1, place.z_size)]


ROWS1, ROWS2, ROWS3 = 4 * HALF, 5 * HALF, 3 * HALF
ROWS = ROWS1 + ROWS2 + ROWS3


def sums_kernel(where, keep, *refs):
    got, (total, token) = refs[:-2], refs[-2:]
    token[...] = jnp.zeros_like(token)
    value = keep[...].astype(F32)
    for ref in got:
        value = value + ref[...].astype(F32)
    total[...] = value


def sums(where, keep, got, deps=()):
    return call(sums_kernel, "sums", where, [keep, *got], [sds(keep.shape, F32)], deps)


def totals_kernel(where, *refs):
    keep1, got1, total2, keep3, *got3 = refs[:-6]
    kept_ref, sent_ref, tail_ref, packed_ref, square_ref, token = refs[-6:]
    token[...] = jnp.zeros_like(token)
    x, c = where[2], where[3]
    whole3 = keep3[...].astype(F32)
    for ref in got3:
        whole3 = whole3 + ref[...].astype(F32)
    parts = (add(keep1[...], got1[...]), total2[...], whole3[:ROWS3])
    wide = D // 4
    row = 0
    square = jnp.zeros((1, D // 2), F32)
    for value in parts:
        rows = slice(row, row + value.shape[0])
        left, right = value[:, :wide], value[:, wide:]

        @pl.when(c == 0)
        def _():
            kept_ref[rows, :] = left
            sent_ref[rows, :] = right

        @pl.when(c != 0)
        def _():
            kept_ref[rows, :] = right
            sent_ref[rows, :] = left

        square = square + jnp.sum(value * value, axis=0, keepdims=True)
        row += value.shape[0]
    tail = whole3[ROWS3:]
    tail_ref[...] = tail
    lane = lax.broadcasted_iota(jnp.int32, (16, D // 2), 1)
    line = lax.broadcasted_iota(jnp.int32, (16, D // 2), 0)
    owner = jnp.where((x == 0) & (c == 0), 1.0, 0.0)
    codes = tail[16:32]
    small = jnp.where(line < 8, jnp.where(lane < D // OWNERS, codes * owner, 0.0), 0.0)
    small = jnp.where((line >= 8) & (lane < D // (4 * OWNERS)), codes, small)
    square = square + jnp.sum(tail[:16] * tail[:16] + small * small, axis=0, keepdims=True)
    square_ref[...] = jnp.full((8, D // 2), jnp.sum(square), F32)
    packed_ref[0:16, :] = tail[:16]
    packed_ref[16:24, :] = square_ref[...]


def totals(where, keep1, got1, total2, keep3, got3, deps=()):
    ins = [keep1, got1, total2, keep3, *got3]
    half = sds((ROWS, D // 4), F32)
    shapes = [half, half] + [sds((rows, D // 2), F32) for rows in (SMALL, 24, 8)]
    return call(totals_kernel, "totals", where, ins, shapes, deps)


def update_kernel(where, *refs):
    kept, got, tail, plane, other_plane = refs[:5]
    squares = refs[5:9]
    state, outs = refs[9:24], refs[24:]
    x, c = where[2], where[3]
    square = (squares[0][0:1, 0:1] + squares[2][0:1, 0:1]) + (
        squares[1][0:1, 0:1] + squares[3][0:1, 0:1]
    )
    norm = jnp.sqrt(square)
    factor = jnp.minimum(1.0, CLIP_LIMIT / (norm + 1e-06))
    outs[0][...] = norm

    def step(at, index, gradient, rate, decay):
        weight, first, second = (state[at + 5 * i][index] for i in range(3))
        new = adam_step(weight, gradient, first, second, rate, decay)
        for i in range(3):
            outs[1 + at + 5 * i][index] = new[i]

    def block(row):
        rows = slice(row, row + HALF)
        own, other = kept[rows, :], got[rows, :]
        top = jnp.where(c == 0, own, other)
        bottom = jnp.where(c == 0, other, own)
        return jnp.concatenate([top, bottom], axis=0) * factor

    front = [ROWS1 + ROWS2 + HALF * b for b in range(3)] + [ROWS1 + HALF * b for b in range(4)]
    for b, row in enumerate(front):
        step(0, b, block(row), RATE_MATRIX, DECAY_RATE)
    back = [ROWS1 + 4 * HALF] + [HALF * b for b in range(4)]
    for b, row in enumerate(back):
        step(1, b, block(row).T, RATE_MATRIX, DECAY_RATE)
    norm_grad = tail[16:22, : D // OWNERS] * factor
    outs[16][...] = norm_grad
    step(3, Ellipsis, norm_grad, RATE_VECTOR, 0.0)
    step(2, Ellipsis, tail[24:30, : D // (4 * OWNERS)] * factor, RATE_VECTOR, 0.0)
    own, by_x = plane[0:16, :], plane[16:32, :]
    by_core, by_both = other_plane[0:16, :], other_plane[16:32, :]
    here = jnp.concatenate(
        [jnp.where(c == 0, own, by_core), jnp.where(c == 0, by_core, own)], axis=0
    )
    there = jnp.concatenate(
        [jnp.where(c == 0, by_x, by_both), jnp.where(c == 0, by_both, by_x)], axis=0
    )
    side = D // 2
    for half in range(2):
        gradient = jnp.where(x == half, here, there) * factor
        lanes = (slice(None), slice(half * side, (half + 1) * side))
        step(4, lanes, gradient, RATE_TABLE, DECAY_RATE)


def update(where, kept, got, tail, here, there, squares, state, deps):
    vmem = pl.BlockSpec(memory_space=pltpu.VMEM)
    ins = [kept, got, tail, here, there, *squares, *state]
    shapes = [sds((1, 1), F32)] + [sds(v.shape, F32) for v in state] + [sds(state[3].shape, F32)]
    return pl.pallas_call(
        ignoring(update_kernel, 1 + len(ins), len(deps)),
        in_specs=[pl.BlockSpec(memory_space=pltpu.SMEM)] + [vmem] * len(ins) + [ANY] * len(deps),
        out_specs=[vmem] * len(shapes),
        out_shape=shapes,
        compiler_params=params(24 * MIB),
        cost_estimate=NO_COST,
        name="update",
    )(where, *ins, *deps)


def adam_step(weight, gradient, first, second, rate, decay):
    first_new = BETA_FIRST * first + (1.0 - BETA_FIRST) * gradient
    second_new = BETA_SECOND * second + (1.0 - BETA_SECOND) * gradient * gradient
    first_hat = first_new / (1.0 - BETA_FIRST**STEP)
    second_hat = second_new / (1.0 - BETA_SECOND**STEP)
    weight_new = weight - rate * (first_hat / (jnp.sqrt(second_hat) + ADAM_EPS) + decay * weight)
    return (weight_new, first_new, second_new)


def body(
    dp_size, mp_size,
    block_input, cotangent, crop_boxes, front_weights, back_weights, split_biases, norm_params,
    pos_table, front_first, back_weight_first_moment, split_first, norm_first, table_first,
    front_second, back_second, split_second, norm_second, table_second,
):
    place = Place(dp_size, mp_size)
    block_input = pltpu.with_memory_space_constraint(block_input, pltpu.HBM)
    direct = dp_size == 8 and mp_size == 4
    x, y, z, c = place.x, place.y, place.z, place.c
    grids = block_input.shape[0] // mp_size
    scal = jnp.stack([place.mp * grids, c, place.mp, place.dp]).astype(jnp.int32)
    where = jnp.stack([z, y, x, c]).astype(jnp.int32)
    turned = jnp.swapaxes(back_weights, 1, 2).astype(BF)
    low_front = front_weights.astype(BF)
    rows, lanes = low_front.shape[1], low_front.shape[2]

    if direct:
        shape = sds((3, 2, front_weights.shape[1], front_weights.shape[2]), BF)
        held = [pltpu.with_memory_space_constraint(v, pltpu.HBM) for v in (front_weights, back_weights)]
        mine, sent, _ = call(shards_kernel, "shards", where, held, [shape, shape])
        got = place.core(sent)
        units = jnp.where(
            c == 0, jnp.concatenate([mine, got], -1), jnp.concatenate([got, mine], -1)
        )
        extra = pos_table.shape[0] // 2
        half = jnp.where(c == 0, pos_table[:extra], pos_table[extra:]).astype(BF)
        half = jnp.where(x == 0, half[:, : D // 2], half[:, D // 2 :])
        packed = jnp.zeros((extra, D // 2), BF)
        packed = lax.dynamic_update_slice(packed, norm_params.astype(BF), (0, 0))
        packed = lax.dynamic_update_slice(packed, split_biases.astype(BF), (0, 128))
        first_unit = jnp.concatenate([units[0], jnp.stack([half, packed])], axis=1)
        own1, unit2, _ = pack(where, gather_z(place, first_unit), None, None, None, units, 1)
        x1, y1 = place.over_x(own1), place.over_y(own1)
        size1, size2 = own1.shape[0] // 2, units.shape[1] * units.shape[2] * place.z_size // 2
        own2, sent_y, sent_x, unit3, _ = pack(
            where, gather_z(place, unit2), x1, y1, (0, size1, size1), units, 2
        )
        y2, x2 = place.over_y(sent_y), place.over_x(sent_x)
        parts3 = gather_z(place, unit3)
        attn_mine, token = assemble(
            where, ((0, 0), (1, 0), (2, 0), (4, 0), (3, 0)), (own1, x1, y1, x2, y2), extra, dp_size,
            tuple(parts3[1:]),
        )
        attn_other = place.core(attn_mine)
        own3, sent_y, sent_x, token3 = pack(
            where, parts3, x2, y2, (size1, size1 + size2, size2), deps=(token,)
        )
        y3, x3 = place.over_y(sent_y), place.over_x(sent_x)
        first_deps = (token3,)
    else:

        def halves(v):
            v = lax.all_gather(v, "dp", axis=1, tiled=True)
            v = lax.all_gather(v, "mp", axis=2, tiled=True).reshape(2, 2 * D, D)
            return jnp.where(c == 0, v[0], v[1]), jnp.where(c == 0, v[1], v[0])

        attn_mine, attn_other = halves(jnp.concatenate([low_front[:3], turned[:1]]))
        up_pair, down_pair = halves(low_front[3:]), halves(turned[1:])
        table = lax.all_gather(pos_table.astype(BF), "dp", axis=0, tiled=True)
        table = table.reshape(OWNERS, 2, CELLS // (2 * OWNERS), D)
        table = jnp.swapaxes(table, 0, 1).reshape(2, CELLS // 2, D)
        norms = lax.all_gather(norm_params.astype(BF), "dp", axis=1, tiled=True)
        splits = lax.all_gather(split_biases.astype(BF), ("mp", "dp"), axis=1, tiled=True)
        norms = jnp.swapaxes(norms.reshape(6, OWNERS, D // OWNERS), 0, 1)
        splits = jnp.transpose(splits.reshape(6, 2, 2, OWNERS, -1), (2, 3, 0, 1, 4))
        codes = jnp.zeros((2, OWNERS, CELLS // (2 * OWNERS), D), BF)
        codes = codes.at[:, :, 0:6, : norms.shape[2]].set(norms)
        for side in range(2):
            lane = side * (D // 2) + 128
            codes = codes.at[:, :, 0:6, lane : lane + splits.shape[4]].set(splits[:, :, :, side])
        table = jnp.concatenate([table, codes.reshape(2, -1, D)], axis=1)
        attn_mine = jnp.concatenate([attn_mine, jnp.where(c == 0, table[0], table[1])])
        attn_other = jnp.concatenate([attn_other, jnp.where(c == 0, table[1], table[0])])
        first_deps = ()

    emb, normed1, q, k, v, p, mixed, after, normed2, w_attn, vec, token = attention_forward(
        scal, crop_boxes, block_input, attn_mine, attn_other, grids, first_deps
    )
    deps = ()
    if direct:
        half, token = assemble(
            where, ((0, 0), (1, size1), (2, size1), (4, 0), (3, 0)), (own2, x2, y2, x3, y3), 0, dp_size,
            (token,),
        )
        up_pair = half, place.core(half)
        sent_y, sent_x, token4 = pack(where, [], x3, y3, (size2, 2 * size2, size2), deps=(token,))
        y4, x4 = place.over_y(sent_y), place.over_x(sent_x)
        deps = (token4,)
    hidden, gp, down_mine, down_other, w_up, token = up_forward(
        scal, normed2, *up_pair, vec, cotangent, grids, deps
    )
    if direct:
        half, token = assemble(
            where, ((0, 0), (1, size2), (2, size2), (4, 0), (3, 0)), (own3, x3, y3, x4, y4), 0, dp_size,
            (token,),
        )
        down_pair = half, place.core(half)
        down_other, token = behind(down_other, token)
        sent, keep1, token = first_y(where, down_mine, place.core(down_other))
        got1 = place.over_y(sent)
        deps = (token,)
    out, w_down, token = down_forward(scal, hidden, *down_pair, after, vec, grids, deps)
    if direct:
        out_x = place.over_x(out)
        deps = (token,)
    ga, galow, up_mine, up_other, gb, gn, token = mlp_backward(
        scal, gp, w_down, w_up, normed2, cotangent, after, vec, mixed, grids, deps
    )
    if direct:
        out_pair, token = pair_grids(where, out, out_x, (token,))
        keep1, *sent, token1 = split_z(where, keep1, got1, deps=(token,))
        got1 = [place.over_z(sent[s - 1], s) for s in range(1, place.z_size)]
        up_other, token1 = behind(up_other, token1)
        sent_x, keep2, token2 = first_x(where, up_mine, place.core(up_other), (token1,))
        got2 = place.over_x(sent_x)
        out_far = place.core(out_pair)
        deps = (token1, token2)
    ig, dtable, gs, mine3, other3, token = attention_backward(
        scal, crop_boxes, ga, galow, mixed, p, q, k, v, emb, normed1, w_attn, vec, gn, gb, grids, deps
    )
    cells_here, norm_here = pos_table.shape[0], norm_params.shape[1]
    split_here = split_biases.shape[1]
    if direct:
        sent1, keep1, token1 = z_to_x(where, keep1, got1, (token,))
        got1 = place.over_x(sent1)
        sent_y, keep2, token2 = second_y(where, keep2, got2, (token1,))
        got2 = place.over_y(sent_y)
        ig_x = place.over_x(ig)
        other3, token2 = behind(other3, token2)
        sent_y, keep3a, sent_x, keep3b, token3 = first_both(
            where, mine3, place.core(other3), (token1, token2)
        )
        got3a, got3b = place.over_y(sent_y), place.over_x(sent_x)
        block_output, token3 = finish_grids(where, out_pair, out_far, (token3,))
        keep2, *sent, token = split_z(where, keep2, got2, deps=(token3,))
        got2 = [place.over_z(sent[s - 1], s) for s in range(1, place.z_size)]
        total2, token = sums(where, keep2, got2, (token,))
        sent_x, keep3a, sent_y, keep3b, token = second_both(
            where, keep3a, got3a, keep3b, got3b, (token,)
        )
        got3a, got3b = place.over_x(sent_x), place.over_y(sent_y)
        ig_pair, token = pair_grids(where, ig, ig_x, (token,))
        keep3, *sent, token = split_z(where, keep3a, got3a, keep3b, got3b, deps=(token,))
        got3 = [place.over_z(sent[s - 1], s) for s in range(1, place.z_size)]
        input_grad, token = finish_grids(where, ig_pair, place.core(ig_pair), (token,))
        kept, sent, tail, packed, square, _ = totals(
            where, keep1, got1, total2, keep3, got3, (token,)
        )
        got = place.core(sent)
        here, there, squares = sum_plane(place, where, packed, square)
        state = (
            front_weights, back_weights, split_biases, norm_params, pos_table,
            front_first, back_weight_first_moment, split_first, norm_first, table_first,
            front_second, back_second, split_second, norm_second, table_second,
        )
        state = [pltpu.with_memory_space_constraint(v, pltpu.HBM) for v in state]
        new = update(where, kept, got, tail, here, there, squares, state, ())
        return (block_output, input_grad, new[0][0, 0], *new[1:])
    else:

        def share(mine, other, blocks):
            low, high = jnp.where(c == 0, mine, other), jnp.where(c == 0, other, mine)
            full = jnp.stack([low, high], 1)[:, :, : blocks * HALF].astype(F32)
            full = full.reshape(OWNERS, 2, blocks, HALF, D)
            full = jnp.transpose(full, (2, 0, 1, 3, 4)).reshape(blocks, D, D)
            full = lax.psum_scatter(full, "dp", scatter_dimension=1, tiled=True)
            return lax.psum_scatter(full, "mp", scatter_dimension=2, tiled=True)

        down_share = share(down_mine, down_other, 4)
        up_share = share(up_mine, up_other, 5)
        out_share, up_share = up_share[4:], up_share[:4]
        qkv_share = share(mine3, other3, 3)
        block_output = lax.all_gather(out, "mp", axis=0, tiled=True)
        input_grad = lax.all_gather(ig, "mp", axis=0, tiled=True)
        norm_grad = jnp.concatenate([gs[2:4], gn[2:6]])
        split_grad = jnp.concatenate([gs[0:2], gb[0:4]])
        dtable = lax.psum(dtable, ("dp", "mp"))
        norm_grad = lax.psum(norm_grad, ("dp", "mp"))
        split_grad = lax.psum(split_grad, ("dp", "mp"))
        table_share = lax.dynamic_slice(dtable, (place.dp * cells_here, 0), (cells_here, D))
        norm_share = lax.dynamic_slice(norm_grad, (0, place.dp * norm_here), (6, norm_here))
        split_share = lax.dynamic_slice(
            split_grad, (0, (place.mp * dp_size + place.dp) * split_here), (6, split_here)
        )
        table_square = jnp.sum(table_share * table_share) / mp_size
    front_share = jnp.concatenate([qkv_share, up_share])
    back_share = jnp.concatenate([out_share, down_share])
    owner = (place.mp == 0).astype(F32)
    square = (
        jnp.sum(qkv_share * qkv_share)
        + jnp.sum(out_share * out_share)
        + jnp.sum(up_share * up_share)
        + jnp.sum(down_share * down_share)
        + jnp.sum(split_share * split_share)
        + owner * jnp.sum(norm_share * norm_share)
        + table_square
    )
    clip_norm = jnp.sqrt(lax.psum(square, ("dp", "mp")))
    factor = jnp.minimum(1.0, CLIP_LIMIT / (clip_norm + 1e-06))
    norm_clipped = norm_share * factor
    new_front, front_first_new, front_second_new = adam_step(
        front_weights, front_share * factor, front_first, front_second, RATE_MATRIX, DECAY_RATE
    )
    new_back, back_first_new, back_second_new = adam_step(
        back_weights,
        jnp.swapaxes(back_share, 1, 2) * factor,
        back_weight_first_moment,
        back_second,
        RATE_MATRIX,
        DECAY_RATE,
    )
    new_split, split_first_new, split_second_new = adam_step(
        split_biases, split_share * factor, split_first, split_second, RATE_VECTOR, 0.0
    )
    new_norm, norm_first_new, norm_second_new = adam_step(
        norm_params, norm_clipped, norm_first, norm_second, RATE_VECTOR, 0.0
    )
    new_table, table_first_new, table_second_new = adam_step(
        pos_table, table_share * factor, table_first, table_second, RATE_TABLE, DECAY_RATE
    )
    return (
        block_output, input_grad, clip_norm,
        new_front, new_back, new_split, new_norm, new_table,
        front_first_new, back_first_new, split_first_new, norm_first_new, table_first_new,
        front_second_new, back_second_new, split_second_new, norm_second_new, table_second_new,
        norm_clipped,
    )


def solution(mesh):
    front, back = P(None, "dp", "mp"), P(None, "mp", "dp")
    split, norm, table = P(None, ("mp", "dp")), P(None, "dp"), P("dp", None)
    state = (front, back, split, norm, table)
    rows = P("dp", None, None)
    return jax.shard_map(
        functools.partial(body, mesh.shape["dp"], mesh.shape["mp"]),
        mesh=mesh,
        in_specs=(rows, rows, P("dp", None)) + state * 3,
        out_specs=(rows, rows, P()) + state * 3 + (norm,),
        check_vma=False,
    )
```
